256 devices in a mesh: group: 32 (over z, y_lo, core), tp: 8 (over x, y_hi).
Axes of the slice: x: 4, y: 4 (y_hi: 2, y_lo: 2; y = y_hi * 2 + y_lo), z: 8, core: 2. Of those that a mesh axis runs over, the one named last changes fastest.
Arguments:
- prefill_queries: bfloat16 [32768, 8192], P(('group', 'tp')), may hold values from -160 to 160
- span_keys: bfloat16 [32768, 1024], P(('group', 'tp')), may hold values from -6 to 6
- span_values: bfloat16 [32768, 1024], P(('group', 'tp')), may hold values from -6 to 6
- prefix_keys: bfloat16 [32768, 1024], P(('group', 'tp')), may hold values from -6 to 6
- prefix_values: bfloat16 [32768, 1024], P(('group', 'tp')), may hold values from -6 to 6
- span_offsets: int32 [32], P('group'), may hold values from 0 to 1024, as said below
- prompt_lengths: int32 [32], P('group'), may hold values from 1 to 3072, as said below
- decode_queries: bfloat16 [1024, 2, 8192], P('group', None, 'tp'), may hold values from -160 to 160
- decode_new_keys: bfloat16 [1024, 2, 1024], P('group', None, 'tp'), may hold values from -6 to 6
- decode_new_values: bfloat16 [1024, 2, 1024], P('group', None, 'tp'), may hold values from -6 to 6
- cache_keys: bfloat16 [1024, 128, 1024], P('group', None, 'tp'), may hold values from -6 to 6
- cache_values: bfloat16 [1024, 128, 1024], P('group', None, 'tp'), may hold values from -6 to 6
- context_lengths: int32 [1024], P('group'), may hold values from 1 to 128
- placement: int32 [1024], replicated, may hold values from 0 to 31, as said below
- finished_lengths: int32 [1024], replicated, may hold values from 1 to 256, 131072 in all
- finished_keys: bfloat16 [1024, 256, 1024], P('group', 'tp'), may hold values from -6 to 6
- finished_values: bfloat16 [1024, 256, 1024], P('group', 'tp'), may hold values from -6 to 6
- arrival_queries: bfloat16 [2048, 2, 8192], P('group', None, 'tp'), may hold values from -160 to 160
- arrival_new_keys: bfloat16 [2048, 2, 1024], P('group', None, 'tp'), may hold values from -6 to 6
- arrival_new_values: bfloat16 [2048, 2, 1024], P('group', None, 'tp'), may hold values from -6 to 6
Outputs:
- prefill_out: bfloat16 [32768, 8192], P(('group', 'tp'))
- decode_out: bfloat16 [1024, 2, 8192], P('group', None, 'tp')
- arrival_out: bfloat16 [2048, 2, 8192], P('group', None, 'tp')
The draws below stay inside these ranges and needn't reach their ends.
Inputs may be any that keep to these rules, and one draw needn't show every extreme that they name: `span_offsets`: multiples of 1024. `prompt_lengths`: each exceeds its group's span offset by 1 to 2048. `placement`: no group sends more than 2 of its finished prompts to one group; arrival slots without a prompt are ignored.
All inputs are finite; a program needn't handle non-finite values.
Results may differ from the reference program's by a relative error of at most 0.018.
Values may be sent and summed in bfloat16 or wider, within the bound.
A program may use at most 128 MiB of HBM per device.

```python
import math
import jax
import jax.numpy as jnp
import numpy as np
from jax import lax

Q_HEADS = 64
KV_HEADS = 8
HEAD_DIM = 128
PREFIX_SPANS = 1
DEC_ROWS = 32
CACHE_LEN = 128
FINISHED = 32
HANDOFF_LEN = 256
CAPACITY = 2
GROUPS = 32
SPAN = 1024
PREFIX = 1024
ARRIVALS = 64


def paired_draw(key, lead, bias):
    key_keys, key_noise = jax.random.split(key, 2)
    group_size = Q_HEADS // KV_HEADS
    keys = jnp.clip(jax.random.normal(key_keys, lead + (KV_HEADS, HEAD_DIM), jnp.float32), -5.0, 5.0)
    noise = jnp.clip(jax.random.normal(key_noise, lead + (KV_HEADS, group_size, HEAD_DIM), jnp.float32), -5.0, 5.0)
    queries = noise + bias * keys[..., None, :]
    return (queries.reshape(lead + (Q_HEADS * HEAD_DIM,)), keys.reshape(lead + (KV_HEADS * HEAD_DIM,)))


def offsets_and_lengths(key):
    key_steps, key_extra, key_chosen = jax.random.split(key, 3)
    group_ids = jnp.arange(GROUPS, dtype=jnp.int32)
    span_steps = jax.random.randint(key_steps, (GROUPS,), 0, PREFIX_SPANS + 1)
    extra = jax.random.randint(key_extra, (GROUPS,), 1, 2 * SPAN + 1)
    chosen = jax.random.randint(key_chosen, (), 0, GROUPS)
    span_steps = jnp.where(group_ids == chosen, PREFIX_SPANS, span_steps)
    extra = jnp.where(group_ids == chosen, 2 * SPAN, extra)
    span_steps = jnp.where(group_ids == (chosen + 1) % GROUPS, 0, span_steps)
    offsets = span_steps * SPAN
    return (offsets.astype(jnp.int32), (offsets + extra).astype(jnp.int32))


def draw_prefill_queries(key, part):
    queries, keys = paired_draw(jax.random.fold_in(key, 101), (GROUPS * SPAN,), 0.0)
    return queries.astype(jnp.bfloat16)


def draw_span_keys(key, part):
    queries, keys = paired_draw(jax.random.fold_in(key, 101), (GROUPS * SPAN,), 0.0)
    return keys.astype(jnp.bfloat16)


def draw_decode_queries(key, part):
    queries, keys = paired_draw(jax.random.fold_in(key, 202), (GROUPS * DEC_ROWS, 2), 0.3)
    return queries.astype(jnp.bfloat16)


def draw_decode_new_keys(key, part):
    queries, keys = paired_draw(jax.random.fold_in(key, 202), (GROUPS * DEC_ROWS, 2), 0.3)
    return keys.astype(jnp.bfloat16)


def draw_arrival_queries(key, part):
    queries, keys = paired_draw(jax.random.fold_in(key, 303), (GROUPS * ARRIVALS, 2), 0.3)
    return queries.astype(jnp.bfloat16)


def draw_arrival_new_keys(key, part):
    queries, keys = paired_draw(jax.random.fold_in(key, 303), (GROUPS * ARRIVALS, 2), 0.3)
    return keys.astype(jnp.bfloat16)


def draw_span_offsets(key, part):
    offsets, lengths = offsets_and_lengths(jax.random.fold_in(key, 404))
    return offsets


def draw_prompt_lengths(key, part):
    offsets, lengths = offsets_and_lengths(jax.random.fold_in(key, 404))
    return lengths


def draw_context_lengths(key, part):
    key = jax.random.fold_in(key, 7)
    key_limit, key_chosen, key_rows, key_pick = jax.random.split(key, 4)
    group_ids = jnp.arange(GROUPS, dtype=jnp.int32)
    row_ids = jnp.arange(DEC_ROWS, dtype=jnp.int32)
    limit = jax.random.randint(key_limit, (GROUPS, 1), max(CACHE_LEN // 8, 1), CACHE_LEN + 1)
    chosen = jax.random.randint(key_chosen, (), 0, GROUPS)
    limit = jnp.where(group_ids[:, None] == chosen, CACHE_LEN, limit)
    lengths = jax.random.randint(key_rows, (GROUPS, DEC_ROWS), 1, limit + 1)
    picked_row = jax.random.randint(key_pick, (), 0, DEC_ROWS)
    lengths = jnp.where((group_ids[:, None] == chosen) & (row_ids[None, :] == picked_row), CACHE_LEN, lengths)
    return lengths.reshape(GROUPS * DEC_ROWS).astype(jnp.int32)


def draw_placement(key, part):
    key = jax.random.fold_in(key, 9)
    key_target, key_rows = jax.random.split(key, 2)
    target = jax.random.randint(key_target, (), 0, GROUPS)
    candidates = jnp.arange((GROUPS - 1) * CAPACITY, dtype=jnp.int32) // CAPACITY
    candidates = candidates + (candidates >= target).astype(jnp.int32)

    def route_one(subkey):
        first_key, second_key = jax.random.split(subkey)
        chosen_dests = jax.random.permutation(first_key, candidates)[:FINISHED - CAPACITY]
        route_row = jnp.concatenate([jnp.full((CAPACITY,), target, jnp.int32), chosen_dests])
        return jax.random.permutation(second_key, route_row)
    routes = jax.vmap(route_one)(jax.random.split(key_rows, GROUPS))
    return routes.reshape(GROUPS * FINISHED).astype(jnp.int32)


def level_of(stream_key, dims, cuts, smallest, largest):
    factor_of = 1.0
    for dim, blocks in cuts:
        draws = jax.random.uniform(jax.random.fold_in(jax.random.fold_in(stream_key, 6), dim), (blocks,), jnp.float32, smallest / len(cuts), largest / len(cuts))
        factor_of = factor_of * jnp.repeat(jnp.exp(draws), dims[dim] // blocks).reshape((-1,) + (1,) * (len(dims) - 1 - dim))
    return factor_of


def length_profile(count, total, most, slope):
    portions = [(1 << 20) // math.isqrt(rank ** slope) + 1 for rank in range(2, count + 1)]
    surplus, given = total - most - (count - 1), [1] * (count - 1)
    while surplus > 0:
        movable = [i for i in range(count - 1) if given[i] < most]
        whole, remaining = sum([portions[i] for i in movable]), surplus
        for i in movable:
            addition = min(most - given[i], max(1, remaining * portions[i] // whole), surplus)
            given[i] = given[i] + addition
            surplus = surplus - addition
    return np.array([most] + given)


def uneven(rng, count, total, bound, skew):
    if count == 2:
        one = jax.random.randint(rng, (), max(1, total - bound), min(bound, total - 1) + 1)
        return jnp.stack([one, total - one])
    sizes = jnp.asarray(length_profile(count, total, bound, skew), jnp.int32)
    pairs = (count - 1) // 2
    source_of, sink = sizes[1:1 + 2 * pairs:2], sizes[2:2 + 2 * pairs:2]
    room = jnp.minimum(source_of - 1, bound - sink)
    shifted = jax.random.randint(jax.random.fold_in(rng, 1), (pairs,), 0, 1 << 20) % (room + 1)
    sizes = sizes.at[1:1 + 2 * pairs:2].set(source_of - shifted).at[2:2 + 2 * pairs:2].set(sink + shifted)
    return sizes[jax.random.permutation(jax.random.fold_in(rng, 2), count)]


def bell_draw(key, extent, deviation, most, pieces=(), held_as=jnp.bfloat16):
    factor_of = level_of(key, extent, pieces, -0.22, 0.18) if pieces else 1.0
    result = jax.random.normal(key, extent, jnp.float32) * deviation * factor_of
    return jnp.minimum(jnp.maximum(result, -most), most).astype(held_as)


def setup_inputs(seed: int = 0) -> dict:
    streams_of = jax.random.split(jax.random.key(seed), 21)
    return {
        "prefill_queries": draw_prefill_queries(jax.random.fold_in(streams_of[20], 71), 0),
        "span_keys": draw_span_keys(jax.random.fold_in(streams_of[20], 71), 0),
        "span_values": bell_draw(streams_of[2], (GROUPS * SPAN, KV_HEADS * HEAD_DIM), 1.0, 6.0, ((0, 256),)),
        "prefix_keys": bell_draw(streams_of[3], (GROUPS * PREFIX, KV_HEADS * HEAD_DIM), 1.0, 6.0, ((0, 256),)),
        "prefix_values": bell_draw(streams_of[4], (GROUPS * PREFIX, KV_HEADS * HEAD_DIM), 1.0, 6.0, ((0, 256),)),
        "span_offsets": draw_span_offsets(jax.random.fold_in(streams_of[20], 71), 0),
        "prompt_lengths": draw_prompt_lengths(jax.random.fold_in(streams_of[20], 71), 0),
        "decode_queries": draw_decode_queries(jax.random.fold_in(streams_of[20], 71), 0),
        "decode_new_keys": draw_decode_new_keys(jax.random.fold_in(streams_of[20], 71), 0),
        "decode_new_values": bell_draw(streams_of[9], (GROUPS * DEC_ROWS, 2, KV_HEADS * HEAD_DIM), 1.0, 6.0, ((0, 32), (2, 8))),
        "cache_keys": bell_draw(streams_of[10], (GROUPS * DEC_ROWS, CACHE_LEN, KV_HEADS * HEAD_DIM), 1.0, 6.0, ((0, 32), (2, 8))),
        "cache_values": bell_draw(streams_of[11], (GROUPS * DEC_ROWS, CACHE_LEN, KV_HEADS * HEAD_DIM), 1.0, 6.0, ((0, 32), (2, 8))),
        "context_lengths": draw_context_lengths(jax.random.fold_in(streams_of[20], 71), 0),
        "placement": draw_placement(jax.random.fold_in(streams_of[20], 71), 0),
        "finished_lengths": uneven(streams_of[14], GROUPS * FINISHED, GROUPS * FINISHED * HANDOFF_LEN // 2, HANDOFF_LEN, 2).astype(jnp.int32),
        "finished_keys": bell_draw(streams_of[15], (GROUPS * FINISHED, HANDOFF_LEN, KV_HEADS * HEAD_DIM), 1.0, 6.0, ((0, 32), (1, 8))),
        "finished_values": bell_draw(streams_of[16], (GROUPS * FINISHED, HANDOFF_LEN, KV_HEADS * HEAD_DIM), 1.0, 6.0, ((0, 32), (1, 8))),
        "arrival_queries": draw_arrival_queries(jax.random.fold_in(streams_of[20], 71), 0),
        "arrival_new_keys": draw_arrival_new_keys(jax.random.fold_in(streams_of[20], 71), 0),
        "arrival_new_values": bell_draw(streams_of[19], (GROUPS * ARRIVALS, 2, KV_HEADS * HEAD_DIM), 1.0, 6.0, ((0, 32), (2, 8))),
    }


MASK_SCORE = -1e+30

def rounded(weights):
    return lax.optimization_barrier(weights.astype(jnp.bfloat16)).astype(jnp.float32)

def rows_of(array, first_row, amount):
    return lax.dynamic_slice_in_dim(array, first_row.astype(jnp.int32), amount, 0)

def decode_attend(queries, new_keys, new_values, cache_keys, cache_values, visible, filled):
    row_count, step_count, width = queries.shape
    kv_count = new_keys.shape[2] // HEAD_DIM
    group_size = width // HEAD_DIM // kv_count
    cache_count = cache_keys.shape[1]
    scale = 1.0 / math.sqrt(HEAD_DIM)
    query_heads = queries.reshape(row_count, step_count, kv_count, group_size, HEAD_DIM).astype(jnp.float32)
    key_cache = cache_keys.reshape(row_count, cache_count, kv_count, HEAD_DIM).astype(jnp.float32)
    value_cache = cache_values.reshape(row_count, cache_count, kv_count, HEAD_DIM).astype(jnp.float32)
    key_new = new_keys.reshape(row_count, step_count, kv_count, HEAD_DIM).astype(jnp.float32)
    value_new = new_values.reshape(row_count, step_count, kv_count, HEAD_DIM).astype(jnp.float32)
    cache_scores = jnp.einsum('bskgd,blkd->bskgl', query_heads, key_cache) * scale
    new_scores = jnp.einsum('bskgd,btkd->bskgt', query_heads, key_new) * scale
    cache_scores = jnp.where(visible[:, None, None, None, :], cache_scores, MASK_SCORE)
    step_ids = jnp.arange(step_count, dtype=jnp.int32)
    causal = step_ids[None, :] <= step_ids[:, None]
    new_scores = jnp.where(causal[None, :, None, None, :], new_scores, MASK_SCORE)
    row_max = jnp.maximum(lax.optimization_barrier(jnp.max(cache_scores, axis=-1)), lax.optimization_barrier(jnp.max(new_scores, axis=-1)))
    cache_weights = jnp.exp(cache_scores - row_max[..., None])
    new_weights = jnp.exp(new_scores - row_max[..., None])
    totals = lax.optimization_barrier(jnp.sum(cache_weights, axis=-1)) + lax.optimization_barrier(jnp.sum(new_weights, axis=-1))
    mixed = jnp.einsum('bskgl,blkd->bskgd', rounded(cache_weights), value_cache)
    mixed = mixed + jnp.einsum('bskgt,btkd->bskgd', rounded(new_weights), value_new)
    mixed = mixed / totals[..., None]
    mixed = jnp.where(filled[:, None, None, None, None], mixed, 0.0)
    return mixed.reshape(row_count, step_count, width).astype(jnp.bfloat16)

def reference(prefill_queries, span_keys, span_values, prefix_keys, prefix_values, span_offsets, prompt_lengths, decode_queries, decode_new_keys, decode_new_values, cache_keys, cache_values, context_lengths, placement, finished_lengths, finished_keys, finished_values, arrival_queries, arrival_new_keys, arrival_new_values):
    scale = 1.0 / math.sqrt(HEAD_DIM)
    group_size = Q_HEADS // KV_HEADS
    span_ids = jnp.arange(SPAN, dtype=jnp.int32)
    prefix_ids = jnp.arange(PREFIX, dtype=jnp.int32)
    causal = span_ids[None, :] <= span_ids[:, None]

    def prefill_group(group):
        queries = rows_of(prefill_queries, group * SPAN, SPAN)
        keys = jnp.concatenate([rows_of(prefix_keys, group * PREFIX, PREFIX), rows_of(span_keys, group * SPAN, SPAN)], axis=0)
        values = jnp.concatenate([rows_of(prefix_values, group * PREFIX, PREFIX), rows_of(span_values, group * SPAN, SPAN)], axis=0)
        offset = span_offsets[group]
        length = prompt_lengths[group]
        query_heads = queries.reshape(SPAN, KV_HEADS, group_size, HEAD_DIM).transpose(1, 2, 0, 3).astype(jnp.float32)
        key_heads = keys.reshape(PREFIX + SPAN, KV_HEADS, HEAD_DIM).transpose(1, 0, 2).astype(jnp.float32)
        value_heads = values.reshape(PREFIX + SPAN, KV_HEADS, HEAD_DIM).transpose(1, 0, 2).astype(jnp.float32)
        prefix_visible = jnp.broadcast_to((prefix_ids < offset)[None, :], (SPAN, PREFIX))
        visible = jnp.concatenate([prefix_visible, causal], axis=1)

        def per_head(operands):
            query_one, key_one, value_one = operands
            scores = jnp.einsum('gid,jd->gij', query_one, key_one) * scale
            scores = jnp.where(visible[None], scores, MASK_SCORE)
            row_max = lax.optimization_barrier(jnp.max(scores, axis=-1))
            weights = jnp.exp(scores - row_max[..., None])
            totals = lax.optimization_barrier(jnp.sum(weights, axis=-1))
            return jnp.einsum('gij,jd->gid', rounded(weights), value_one) / totals[..., None]
        mixed = lax.map(per_head, (query_heads, key_heads, value_heads))
        output = mixed.transpose(2, 0, 1, 3).reshape(SPAN, Q_HEADS * HEAD_DIM)
        filled = offset + span_ids < length
        return jnp.where(filled[:, None], output, 0.0).astype(jnp.bfloat16)
    group_ids = jnp.arange(GROUPS, dtype=jnp.int32)
    prefill_out = lax.map(prefill_group, group_ids).reshape(GROUPS * SPAN, Q_HEADS * HEAD_DIM)
    cache_ids = jnp.arange(CACHE_LEN, dtype=jnp.int32)

    def resident_group(group):
        first_row = group * DEC_ROWS
        visible = cache_ids[None, :] < rows_of(context_lengths, first_row, DEC_ROWS)[:, None]
        filled = jnp.ones((DEC_ROWS,), jnp.bool_)
        return decode_attend(rows_of(decode_queries, first_row, DEC_ROWS), rows_of(decode_new_keys, first_row, DEC_ROWS), rows_of(decode_new_values, first_row, DEC_ROWS), rows_of(cache_keys, first_row, DEC_ROWS), rows_of(cache_values, first_row, DEC_ROWS), visible, filled)
    decode_out = lax.map(resident_group, group_ids).reshape(GROUPS * DEC_ROWS, 2, Q_HEADS * HEAD_DIM)
    routes = placement.reshape(GROUPS, FINISHED)
    finished_ids = jnp.arange(FINISHED, dtype=jnp.int32)
    earlier = finished_ids[None, :] < finished_ids[:, None]
    arrival_rank = lax.optimization_barrier(jnp.sum(((routes[:, :, None] == routes[:, None, :]) & earlier[None]).astype(jnp.int32), axis=2))
    prompt_lens = finished_lengths.reshape(GROUPS, FINISHED)
    slot_ids = jnp.arange(CAPACITY, dtype=jnp.int32)
    handoff_ids = jnp.arange(HANDOFF_LEN, dtype=jnp.int32)

    def arrival_group(group):
        matched = (routes == group)[:, None, :] & (arrival_rank[:, None, :] == slot_ids[None, :, None])
        source_row = lax.optimization_barrier(jnp.sum(jnp.where(matched, finished_ids[None, None, :], 0), axis=-1))
        filled = jnp.any(matched, axis=-1).reshape(ARRIVALS)
        slot_len = lax.optimization_barrier(jnp.sum(jnp.where(matched, prompt_lens[:, None, :], 0), axis=-1)).reshape(ARRIVALS)
        gathered_rows = (group_ids[:, None] * FINISHED + source_row).reshape(ARRIVALS)
        visible = handoff_ids[None, :] < slot_len[:, None]
        first_row = group * ARRIVALS
        return decode_attend(rows_of(arrival_queries, first_row, ARRIVALS), rows_of(arrival_new_keys, first_row, ARRIVALS), rows_of(arrival_new_values, first_row, ARRIVALS), finished_keys[gathered_rows], finished_values[gathered_rows], visible, filled)
    arrival_out = lax.map(arrival_group, group_ids).reshape(GROUPS * ARRIVALS, 2, Q_HEADS * HEAD_DIM)
    return (prefill_out, decode_out, arrival_out)
```

```python
import functools
import math

import jax
import jax.numpy as jnp
from jax import lax
from jax.experimental import pallas as pl
from jax.experimental.pallas import tpu as pltpu
from jax.sharding import PartitionSpec as P

KV_HEADS = 8
GROUP_SIZE = 8
HEAD_DIM = 128
CAPACITY = 2
STEPS = 2
ROWS16 = GROUP_SIZE * STEPS
MESH = pl.DeviceIdType.MESH
NEG = -1e30
RATE = math.log2(math.e) / math.sqrt(HEAD_DIM)
X_CHIPS = 4


def dot_t(a, b):
    return lax.dot_general(a, b, (((1,), (1,)), ((), ())), preferred_element_type=jnp.float32)


def dot_n(a, b):
    return lax.dot_general(a, b, (((1,), (0,)), ((), ())), preferred_element_type=jnp.float32)


def spread(row, reps):
    n = row.shape[1]
    owner = lax.broadcasted_iota(jnp.int32, (n * reps, n), 0) // reps
    lane = lax.broadcasted_iota(jnp.int32, (n * reps, n), 1)
    return jnp.sum(jnp.where(owner == lane, row, 0.0), axis=1, keepdims=True)


def new_scores(q3, nk):
    shape = q3.shape[:2] + (1,)
    step = lax.broadcasted_iota(jnp.int32, shape, 1) % STEPS
    first = jnp.sum(q3 * nk[0], axis=2, keepdims=True)
    second = jnp.sum(q3 * nk[1], axis=2, keepdims=True)
    return first, jnp.where(step >= 1, second, NEG)


def body(
    n_groups,
    n_tp,
    pq,
    sk,
    sv,
    pk,
    pv,
    span_offset,
    prompt_length,
    dq,
    dnk,
    dnv,
    ck,
    cv,
    context,
    routes,
    lengths,
    fk,
    fv,
    msg,
    p_out,
    d_out,
    a_out,
    kv,
    q_s,
    ck_s,
    cv_s,
    fk_s,
    fv_s,
    rm,
    aq,
    po,
    ro,
    ps,
    rs,
    sel,
    bias,
    ret,
    ao,
    load_kv,
    load_big,
    x_send,
    x_recv,
    m_send,
    m_recv,
    q_send,
    q_recv,
    o_send,
    o_recv,
    s_send,
    s_recv,
    b_send,
    b_recv,
    own_sem,
):
    g = lax.axis_index("group")
    t = lax.axis_index("tp")
    x, yh = t // 2, t % 2
    right = ((x + 1) % X_CHIPS) * 2 + yh
    left = ((x + X_CHIPS - 1) % X_CHIPS) * 2 + yh
    partner = x * 2 + (1 - yh)
    right_x = (x + 1) % X_CHIPS
    left_x = (x + X_CHIPS - 1) % X_CHIPS
    far_x = (x + 2) % X_CHIPS
    n_prompts = routes.shape[1]
    a_rows = n_prompts * ROWS16
    quads = n_prompts // 4
    rows = pq.shape[0]

    arrays = (pk, sk, pv, sv)

    def kv_load(h, a):
        cols = pl.ds(pl.multiple_of(h * HEAD_DIM, HEAD_DIM), HEAD_DIM)
        return pltpu.make_async_copy(arrays[a].at[:, cols], kv.at[h, a, t], load_kv.at[h, a])

    def start_loads(h, c):
        for a in range(4):
            kv_load(h, a).start()
        return c

    lax.fori_loop(0, KV_HEADS, start_loads, 0)
    big = [
        pltpu.make_async_copy(src, dst, load_big.at[i])
        for i, (src, dst) in enumerate(
            ((ck, ck_s), (cv, cv_s), (pq, q_s), (fk, fk_s), (fv, fv_s))
        )
    ]
    for copy in big:
        copy.start()
    own_msg = pltpu.make_async_copy(msg.at[g], rm.at[g], own_sem)
    own_msg.start()

    barrier = pltpu.get_barrier_semaphore()

    def greet_group(k, c):
        pl.semaphore_signal(
            barrier, inc=1, device_id={"group": (g + k) % n_groups}, device_id_type=MESH
        )
        return c

    def greet_tp(k, c):
        pl.semaphore_signal(barrier, inc=1, device_id={"tp": (t + k) % n_tp}, device_id_type=MESH)
        return c

    lax.fori_loop(1, n_groups, greet_group, 0)
    lax.fori_loop(1, n_tp, greet_tp, 0)
    pl.semaphore_wait(barrier, n_groups - 1 + n_tp - 1)

    def to_tp(src, dst, kind, h, peer):
        return pltpu.make_async_remote_copy(
            src_ref=src,
            dst_ref=dst,
            send_sem=x_send.at[h, kind],
            recv_sem=x_recv.at[h, kind],
            device_id={"tp": peer},
            device_id_type=MESH,
        )

    def block_copy(h, block, kind, peer):
        ref = kv.at[h, :, block]
        return to_tp(ref, ref, kind, h, peer)

    def pair_copy(h, arr, xs, kind, peer):
        ref = kv.at[h, pl.ds(arr, 2), pl.ds(xs * 2, 2)]
        return to_tp(ref, ref, kind, h, peer)

    def stage1(h):
        for a in range(4):
            kv_load(h, a).wait()
        block_copy(h, t, 0, partner).start()
        block_copy(h, t, 1, right).start()
        block_copy(h, t, 2, left).start()

    def stage2(h):
        block_copy(h, partner, 0, partner).wait_recv()
        block_copy(h, partner, 3, right).start()
        block_copy(h, partner, 4, left).start()

    def stage3(h):
        block_copy(h, left_x * 2 + yh, 1, right).wait_recv()
        block_copy(h, left_x * 2 + (1 - yh), 3, right).wait_recv()
        pair_copy(h, 0, left_x, 5, right).start()
        block_copy(h, right_x * 2 + yh, 2, left).wait_recv()
        block_copy(h, right_x * 2 + (1 - yh), 4, left).wait_recv()
        pair_copy(h, 2, right_x, 6, left).start()

    def stage4(h):
        pair_copy(h, 0, far_x, 5, right).wait_recv()
        pair_copy(h, 2, far_x, 6, left).wait_recv()

    def msg_copy(k):
        peer = (g + k) % n_groups
        return pltpu.make_async_remote_copy(
            src_ref=msg.at[peer],
            dst_ref=rm.at[g],
            send_sem=m_send.at[k],
            recv_sem=m_recv.at[g],
            device_id={"group": peer},
            device_id_type=MESH,
        )

    def msg_wait(k):
        peer = (g + k) % n_groups
        pltpu.make_async_remote_copy(
            src_ref=rm.at[peer],
            dst_ref=rm.at[peer],
            send_sem=m_send.at[k],
            recv_sem=m_recv.at[peer],
            device_id={"group": peer},
            device_id_type=MESH,
        ).wait_recv()

    def send_msg(k, c):
        msg_copy(k).start()
        return c

    def wait_msg(k, c):
        msg_wait(k)
        return c

    lax.fori_loop(1, n_groups, send_msg, 0)

    def decode():
        big[0].wait()
        big[1].wait()
        b = dnk.shape[0]
        q = dq[...].reshape(b, ROWS16, HEAD_DIM)
        s = lax.dot_general(
            q, ck_s[...], (((2,), (2,)), ((0,), (0,))), preferred_element_type=jnp.float32
        )
        limit = spread(context[...].astype(jnp.float32), ROWS16).reshape(b, ROWS16, 1)
        slot = lax.broadcasted_iota(jnp.int32, s.shape, 2).astype(jnp.float32)
        s = jnp.where(slot < limit, s, NEG)
        nk = dnk[...].astype(jnp.float32)
        nv = dnv[...].astype(jnp.float32)
        n0, n1 = new_scores(q.astype(jnp.float32), (nk[:, 0:1], nk[:, 1:2]))
        m = jnp.maximum(jnp.max(s, axis=2, keepdims=True), jnp.maximum(n0, n1))
        w = jnp.exp2((s - m) * RATE)
        w0 = jnp.exp2((n0 - m) * RATE)
        w1 = jnp.exp2((n1 - m) * RATE)
        total = jnp.sum(w, axis=2, keepdims=True) + w0 + w1
        o = lax.dot_general(
            w.astype(jnp.bfloat16),
            cv_s[...],
            (((2,), (1,)), ((0,), (0,))),
            preferred_element_type=jnp.float32,
        )
        o = o + w0.astype(jnp.bfloat16).astype(jnp.float32) * nv[:, 0:1]
        o = o + w1.astype(jnp.bfloat16).astype(jnp.float32) * nv[:, 1:2]
        d_out[...] = (o / total).reshape(b * ROWS16, HEAD_DIM).astype(jnp.bfloat16)

    def aq_copy(k):
        peer = (t + k) % n_tp
        return pltpu.make_async_remote_copy(
            src_ref=aq.at[t],
            dst_ref=aq.at[t],
            send_sem=q_send.at[k],
            recv_sem=q_recv.at[t],
            device_id={"tp": peer},
            device_id_type=MESH,
        )

    def aq_wait(k):
        peer = (t + k) % n_tp
        pltpu.make_async_remote_copy(
            src_ref=aq.at[peer],
            dst_ref=aq.at[peer],
            send_sem=q_send.at[k],
            recv_sem=q_recv.at[peer],
            device_id={"tp": peer},
            device_id_type=MESH,
        ).wait_recv()

    def arrivals_choose():
        own_msg.wait()
        lax.fori_loop(1, n_groups, wait_msg, 0)
        own = routes[pl.ds(g, 1), :].astype(jnp.float32)
        dest = spread(own, ROWS16)
        owner = lax.broadcasted_iota(jnp.int32, (a_rows, n_prompts), 0) // ROWS16
        other = lax.broadcasted_iota(jnp.int32, (a_rows, n_prompts), 1)
        rank = jnp.sum(
            jnp.where((dest == own) & (other < owner), 1.0, 0.0), axis=1, keepdims=True
        )
        within = lax.broadcasted_iota(jnp.int32, (a_rows, 1), 0) % ROWS16
        target = (dest * CAPACITY + rank) * ROWS16 + within.astype(jnp.float32)
        slot_rows = n_groups * CAPACITY * ROWS16
        column = lax.broadcasted_iota(jnp.int32, (a_rows, slot_rows), 1).astype(jnp.float32)
        sel[...] = jnp.where(column == target, 1.0, 0.0).astype(jnp.bfloat16)
        got = rm[:, :, 0:ROWS16, :].reshape(slot_rows, HEAD_DIM)
        aq[t] = dot_n(sel[...], got).astype(jnp.bfloat16)

        def send(k, c):
            aq_copy(k).start()
            return c

        lax.fori_loop(1, n_tp, send, 0)
        local_len = fk_s.shape[0] // n_prompts
        own_len = lengths[pl.ds(g, 1), :].astype(jnp.float32)
        limit = spread(own_len, ROWS16) - (t * local_len).astype(jnp.float32)
        col = lax.broadcasted_iota(jnp.int32, (a_rows, HEAD_DIM), 1)
        quad_row = (lax.broadcasted_iota(jnp.int32, (a_rows, HEAD_DIM), 0) // ROWS16) % 4
        keep = (col // local_len == quad_row) & ((col % local_len).astype(jnp.float32) < limit)
        bias[...] = jnp.where(keep, 0.0, NEG)

    def po_copy(h, k):
        return pltpu.make_async_remote_copy(
            src_ref=po.at[h],
            dst_ref=ro.at[t],
            send_sem=o_send.at[k],
            recv_sem=o_recv.at[t],
            device_id={"tp": h},
            device_id_type=MESH,
        )

    def ps_copy(h, k):
        return pltpu.make_async_remote_copy(
            src_ref=ps.at[h],
            dst_ref=rs.at[t],
            send_sem=s_send.at[k],
            recv_sem=s_recv.at[t],
            device_id={"tp": h},
            device_id_type=MESH,
        )

    def po_wait(k):
        peer = (t + k) % n_tp
        for send_sem, recv_sem, ref in ((o_send, o_recv, ro), (s_send, s_recv, rs)):
            pltpu.make_async_remote_copy(
                src_ref=ref.at[peer],
                dst_ref=ref.at[peer],
                send_sem=send_sem.at[k],
                recv_sem=recv_sem.at[peer],
                device_id={"tp": peer},
                device_id_type=MESH,
            ).wait_recv()

    def partial_head(h, o_ref, s_ref, at):
        cols = pl.ds(pl.multiple_of(h * HEAD_DIM, HEAD_DIM), HEAD_DIM)
        lane = lax.broadcasted_iota(jnp.int32, (4 * ROWS16, HEAD_DIM), 1)
        stats = jnp.zeros((4 * ROWS16, HEAD_DIM), jnp.float32)
        for i in range(quads):
            rows_i = slice(i * 4 * ROWS16, (i + 1) * 4 * ROWS16)
            keys_i = slice(i * HEAD_DIM, (i + 1) * HEAD_DIM)
            s = dot_t(aq[h, rows_i, :], fk_s[keys_i, cols]) + bias[rows_i, :]
            m = jnp.max(s, axis=1, keepdims=True)
            w = jnp.exp2((s - m) * RATE)
            total = jnp.sum(w, axis=1, keepdims=True)
            o_ref[at, rows_i, :] = dot_n(w.astype(jnp.bfloat16), fv_s[keys_i, cols]).astype(
                jnp.bfloat16
            )
            stats = jnp.where(lane == i, m, stats)
            stats = jnp.where(lane == quads + i, total, stats)
        s_ref[at] = stats

    def arrivals_partial():
        def wait(k, c):
            aq_wait(k)
            return c

        lax.fori_loop(1, n_tp, wait, 0)
        big[3].wait()
        big[4].wait()

        def one(k, c):
            h = (t + k) % n_tp
            partial_head(h, po, ps, h)
            po_copy(h, k).start()
            ps_copy(h, k).start()
            return c

        lax.fori_loop(1, n_tp, one, 0)
        partial_head(t, ro, rs, t)

    def ret_copy(k):
        peer = (g + k) % n_groups
        return pltpu.make_async_remote_copy(
            src_ref=ret.at[peer],
            dst_ref=ao.at[g],
            send_sem=b_send.at[k],
            recv_sem=b_recv.at[g],
            device_id={"group": peer},
            device_id_type=MESH,
        )

    def ret_wait(k):
        peer = (g + k) % n_groups
        pltpu.make_async_remote_copy(
            src_ref=ao.at[peer],
            dst_ref=ao.at[peer],
            send_sem=b_send.at[k],
            recv_sem=b_recv.at[peer],
            device_id={"group": peer},
            device_id_type=MESH,
        ).wait_recv()

    def arrivals_join():
        def wait(k, c):
            po_wait(k)
            return c

        lax.fori_loop(1, n_tp, wait, 0)
        slot_rows = n_groups * CAPACITY * ROWS16
        extra = rm[:, :, ROWS16 : 2 * ROWS16, :].reshape(slot_rows, HEAD_DIM)
        new = dot_n(sel[...], extra).reshape(n_prompts, ROWS16, HEAD_DIM)
        q3 = aq[t].astype(jnp.float32).reshape(n_prompts, ROWS16, HEAD_DIM)
        n0, n1 = new_scores(q3, (new[:, 0:1], new[:, 1:2]))
        n0 = n0.reshape(a_rows, 1)
        n1 = n1.reshape(a_rows, 1)
        ms = [
            jnp.concatenate([rs[p][:, i : i + 1] for i in range(quads)], axis=0)
            for p in range(n_tp)
        ]
        m = jnp.maximum(n0, n1)
        for mp in ms:
            m = jnp.maximum(m, mp)
        w0 = jnp.exp2((n0 - m) * RATE)
        w1 = jnp.exp2((n1 - m) * RATE)
        total = w0 + w1
        o = jnp.zeros((a_rows, HEAD_DIM), jnp.float32)
        for p in range(n_tp):
            wp = jnp.exp2((ms[p] - m) * RATE)
            lp = jnp.concatenate(
                [rs[p][:, quads + i : quads + i + 1] for i in range(quads)], axis=0
            )
            total = total + wp * lp
            o = o + wp * ro[p].astype(jnp.float32)
        w0 = w0.astype(jnp.bfloat16).astype(jnp.float32).reshape(n_prompts, ROWS16, 1)
        w1 = w1.astype(jnp.bfloat16).astype(jnp.float32).reshape(n_prompts, ROWS16, 1)
        o = o + (w0 * new[:, 2:3] + w1 * new[:, 3:4]).reshape(a_rows, HEAD_DIM)
        res = (o / total).astype(jnp.bfloat16)
        back = lax.dot_general(
            sel[...], res, (((0,), (0,)), ((), ())), preferred_element_type=jnp.float32
        )
        ret[...] = back.astype(jnp.bfloat16).reshape(n_groups, CAPACITY, ROWS16, HEAD_DIM)

        def send(k, c):
            ret_copy(k).start()
            return c

        lax.fori_loop(1, n_groups, send, 0)

    def prefill_head(h):
        vis = span_offset[0] > 0
        filled = span_offset[0] + t * rows < prompt_length[0]
        part = 4
        n_rows = part * rows
        kp = kv[h, 0].reshape(n_tp * rows, HEAD_DIM)
        ks = kv[h, 1].reshape(n_tp * rows, HEAD_DIM)
        vp = kv[h, 2].reshape(n_tp * rows, HEAD_DIM)
        vs = kv[h, 3].reshape(n_tp * rows, HEAD_DIM)
        position = lax.broadcasted_iota(jnp.int32, (n_rows, 1), 0) % rows + t * rows
        key_ids = lax.broadcasted_iota(jnp.int32, (n_rows, n_tp * rows), 1)
        live = span_offset[0] + position < prompt_length[0]

        def half(j, c):
            def cols(i):
                start = h * (GROUP_SIZE * HEAD_DIM) + (j * part + i) * HEAD_DIM
                return pl.ds(pl.multiple_of(start, HEAD_DIM), HEAD_DIM)

            q = jnp.concatenate([q_s[:, cols(i)] for i in range(part)], axis=0)
            sp = dot_t(q, kp)
            ss = jnp.where(key_ids <= position, dot_t(q, ks), NEG)
            mp = jnp.max(sp, axis=1, keepdims=True)
            m = jnp.max(ss, axis=1, keepdims=True)
            m = jnp.where(vis, jnp.maximum(m, mp), m)
            wp = jnp.exp2((sp - jnp.where(vis, m, -NEG)) * RATE)
            ws = jnp.exp2((ss - m) * RATE)
            total = jnp.sum(wp, axis=1, keepdims=True) + jnp.sum(ws, axis=1, keepdims=True)
            o = dot_n(wp.astype(jnp.bfloat16), vp) + dot_n(ws.astype(jnp.bfloat16), vs)
            o = jnp.where(live, o / total, 0.0).astype(jnp.bfloat16)
            for i in range(part):
                p_out[:, cols(i)] = o[i * rows : (i + 1) * rows]
            return c

        lax.fori_loop(0, GROUP_SIZE // part, half, 0)

    ahead = 2
    for h in range(ahead):
        stage1(h)
    decode()
    stage2(0)
    arrivals_choose()
    big[2].wait()

    def turn(s, c):
        @pl.when(s + ahead < KV_HEADS)
        def _():
            stage1(s + ahead)

        @pl.when(s + 1 < KV_HEADS)
        def _():
            stage2(s + 1)

        stage3(s)

        @pl.when(s == 1)
        def _():
            arrivals_partial()

        @pl.when(s == 4)
        def _():
            arrivals_join()

        @pl.when(s >= 1)
        def _():
            stage4(s - 1)
            prefill_head(s - 1)

        return c

    lax.fori_loop(0, KV_HEADS, turn, 0)
    stage4(KV_HEADS - 1)
    prefill_head(KV_HEADS - 1)

    def wait_ret(k, c):
        ret_wait(k)
        return c

    lax.fori_loop(1, n_groups, wait_ret, 0)
    ao[g] = ret[g]
    a_out[...] = ao[...]

    def drain_group(k, c):
        msg_copy(k).wait_send()
        ret_copy(k).wait_send()
        return c

    def drain_tp(k, c):
        h = (t + k) % n_tp
        aq_copy(k).wait_send()
        po_copy(h, k).wait_send()
        ps_copy(h, k).wait_send()
        return c

    def drain_kv(h, c):
        block_copy(h, t, 0, partner).wait_send()
        block_copy(h, t, 1, right).wait_send()
        block_copy(h, t, 2, left).wait_send()
        block_copy(h, partner, 3, right).wait_send()
        block_copy(h, partner, 4, left).wait_send()
        pair_copy(h, 0, left_x, 5, right).wait_send()
        pair_copy(h, 2, right_x, 6, left).wait_send()
        return c

    lax.fori_loop(1, n_groups, drain_group, 0)
    lax.fori_loop(1, n_tp, drain_tp, 0)
    lax.fori_loop(0, KV_HEADS, drain_kv, 0)


def to_rows(queries):
    b = queries.shape[0]
    return queries.reshape(b, STEPS, GROUP_SIZE, HEAD_DIM).transpose(0, 2, 1, 3)


def from_rows(rows, b):
    rows = rows.reshape(b, GROUP_SIZE, STEPS, HEAD_DIM).transpose(0, 2, 1, 3)
    return rows.reshape(b, STEPS, GROUP_SIZE * HEAD_DIM)


def local(
    prefill_queries,
    span_keys,
    span_values,
    prefix_keys,
    prefix_values,
    span_offsets,
    prompt_lengths,
    decode_queries,
    decode_new_keys,
    decode_new_values,
    cache_keys,
    cache_values,
    context_lengths,
    placement,
    finished_lengths,
    finished_keys,
    finished_values,
    arrival_queries,
    arrival_new_keys,
    arrival_new_values,
):
    n_groups = lax.axis_size("group")
    n_tp = lax.axis_size("tp")
    n_prompts, local_len, width = finished_keys.shape
    rows = prefill_queries.shape[0]
    dec = decode_queries.shape[0]
    slots = arrival_queries.shape[0]
    dq = to_rows(decode_queries).reshape(dec * ROWS16, HEAD_DIM)
    msg = jnp.concatenate(
        [
            to_rows(arrival_queries).reshape(slots, ROWS16, HEAD_DIM),
            arrival_new_keys,
            arrival_new_values,
            jnp.zeros((slots, ROWS16 - 2 * STEPS, HEAD_DIM), jnp.bfloat16),
        ],
        axis=1,
    ).reshape(n_groups, CAPACITY, 2 * ROWS16, HEAD_DIM)
    any_ = pl.BlockSpec(memory_space=pl.ANY)
    vmem = pl.BlockSpec(memory_space=pltpu.VMEM)
    smem = pl.BlockSpec(memory_space=pltpu.SMEM)
    bf, f32 = jnp.bfloat16, jnp.float32
    a_rows = n_prompts * ROWS16
    dma = pltpu.SemaphoreType.DMA
    p_out, d_out, a_out = pl.pallas_call(
        functools.partial(body, n_groups, n_tp),
        out_shape=(
            jax.ShapeDtypeStruct(prefill_queries.shape, bf),
            jax.ShapeDtypeStruct(dq.shape, bf),
            jax.ShapeDtypeStruct((n_groups, CAPACITY, ROWS16, HEAD_DIM), bf),
        ),
        in_specs=[any_] * 5
        + [smem] * 2
        + [vmem] * 3
        + [any_] * 2
        + [vmem] * 3
        + [any_] * 2
        + [any_],
        out_specs=[vmem] * 3,
        scratch_shapes=[
            pltpu.VMEM((KV_HEADS, 4, n_tp, rows, HEAD_DIM), bf),
            pltpu.VMEM(prefill_queries.shape, bf),
            pltpu.VMEM(cache_keys.shape, bf),
            pltpu.VMEM(cache_values.shape, bf),
            pltpu.VMEM((n_prompts * local_len, width), bf),
            pltpu.VMEM((n_prompts * local_len, width), bf),
            pltpu.VMEM(msg.shape, bf),
            pltpu.VMEM((n_tp, a_rows, HEAD_DIM), bf),
            pltpu.VMEM((n_tp, a_rows, HEAD_DIM), bf),
            pltpu.VMEM((n_tp, a_rows, HEAD_DIM), bf),
            pltpu.VMEM((n_tp, 4 * ROWS16, HEAD_DIM), f32),
            pltpu.VMEM((n_tp, 4 * ROWS16, HEAD_DIM), f32),
            pltpu.VMEM((a_rows, slots * ROWS16), bf),
            pltpu.VMEM((a_rows, HEAD_DIM), f32),
            pltpu.VMEM((n_groups, CAPACITY, ROWS16, HEAD_DIM), bf),
            pltpu.VMEM((n_groups, CAPACITY, ROWS16, HEAD_DIM), bf),
            dma((KV_HEADS, 4)),
            dma((5,)),
            dma((KV_HEADS, 7)),
            dma((KV_HEADS, 7)),
            dma((n_groups,)),
            dma((n_groups,)),
            dma((n_tp,)),
            dma((n_tp,)),
            dma((n_tp,)),
            dma((n_tp,)),
            dma((n_tp,)),
            dma((n_tp,)),
            dma((n_groups,)),
            dma((n_groups,)),
            dma(()),
        ],
        compiler_params=pltpu.CompilerParams(
            collective_id=0, has_side_effects=True, vmem_limit_bytes=56 * 1024 * 1024
        ),
    )(
        prefill_queries,
        span_keys,
        span_values,
        prefix_keys,
        prefix_values,
        span_offsets,
        prompt_lengths,
        dq,
        decode_new_keys,
        decode_new_values,
        cache_keys,
        cache_values,
        context_lengths[None, :],
        placement.reshape(n_groups, n_prompts),
        finished_lengths.reshape(n_groups, n_prompts),
        finished_keys.reshape(n_prompts * local_len, width),
        finished_values.reshape(n_prompts * local_len, width),
        msg,
    )
    return (p_out, from_rows(d_out, dec), from_rows(a_out, slots))


def solution(mesh):
    both = P(("group", "tp"), None)
    heads = P("group", None, "tp")
    placed = (
        (both,) * 5
        + (P("group"),) * 2
        + (heads,) * 5
        + (P("group"), P(), P())
        + (P("group", "tp", None),) * 2
        + (heads,) * 3
    )
    return jax.shard_map(
        local,
        mesh=mesh,
        in_specs=placed,
        out_specs=(both, heads, heads),
        check_vma=False,
    )
```

```python
import functools
import math

import jax
import jax.numpy as jnp
from jax import lax
from jax.experimental import pallas as pl
from jax.experimental.pallas import tpu as pltpu
from jax.sharding import PartitionSpec as P

KV_HEADS = 8
GROUP_SIZE = 8
HEAD_DIM = 128
CAPACITY = 2
STEPS = 2
ROWS16 = GROUP_SIZE * STEPS
MESH = pl.DeviceIdType.MESH
NEG = -1e30
RATE = math.log2(math.e) / math.sqrt(HEAD_DIM)
X_CHIPS = 4
CORES = 2
ITEMS = KV_HEADS + 1
QUERY_ITEM = KV_HEADS


def dot_t(a, b):
    return lax.dot_general(a, b, (((1,), (1,)), ((), ())), preferred_element_type=jnp.float32)


def dot_n(a, b):
    return lax.dot_general(a, b, (((1,), (0,)), ((), ())), preferred_element_type=jnp.float32)


def spread(row, count, reps, base):
    shape = (count * reps, row.shape[1])
    owner = lax.broadcasted_iota(jnp.int32, shape, 0) // reps + base
    lane = lax.broadcasted_iota(jnp.int32, shape, 1)
    return jnp.sum(jnp.where(owner == lane, row, 0.0), axis=1, keepdims=True)


def new_scores(q3, nk):
    shape = q3.shape[:2] + (1,)
    step = lax.broadcasted_iota(jnp.int32, shape, 1) % STEPS
    first = jnp.sum(q3 * nk[0], axis=2, keepdims=True)
    second = jnp.sum(q3 * nk[1], axis=2, keepdims=True)
    return first, jnp.where(step >= 1, second, NEG)


def body(
    n_groups,
    n_tp,
    pq,
    sk,
    sv,
    pk,
    pv,
    span_offset,
    prompt_length,
    dq,
    dnk,
    dnv,
    ck,
    cv,
    context,
    routes,
    lengths,
    fk,
    fv,
    arrival_q,
    ank,
    anv,
    p_out,
    d_out,
    a_out,
    kv,
    q_s,
    ck_s,
    cv_s,
    fk_s,
    fv_s,
    rel,
    msg,
    rm,
    po,
    ro,
    ps,
    rs,
    sel,
    bias,
    ret,
    ao,
    load_kv,
    load_big,
    x_send,
    x_recv,
    m_send,
    m_recv,
    o_send,
    o_recv,
    s_send,
    s_recv,
    b_send,
    b_recv,
    out_sem,
):
    g = lax.axis_index("group")
    t = lax.axis_index("tp")
    x, yh = t // 2, t % 2
    right = ((x + 1) % X_CHIPS) * 2 + yh
    left = ((x + X_CHIPS - 1) % X_CHIPS) * 2 + yh
    partner = x * 2 + (1 - yh)
    right_x = (x + 1) % X_CHIPS
    left_x = (x + X_CHIPS - 1) % X_CHIPS
    far_x = (x + 2) % X_CHIPS
    yl = (g // CORES) % 2
    beside = g + CORES * (1 - 2 * yl)
    local_len = HEAD_DIM // 4
    n_prompts = fk_s.shape[0] // local_len
    a_rows = n_prompts * ROWS16
    quads = n_prompts // 4
    rows = pq.shape[0]

    arrays = (pk, sk, pv, sv)

    def kv_load(h, a):
        cols = pl.ds(pl.multiple_of(h * HEAD_DIM, HEAD_DIM), HEAD_DIM)
        return pltpu.make_async_copy(arrays[a].at[:, cols], kv.at[h, a, x, yh], load_kv.at[h, a])

    def start_loads(h, c):
        for a in range(4):
            kv_load(h, a).start()
        return c

    lax.fori_loop(0, KV_HEADS, start_loads, 0)
    big = [
        pltpu.make_async_copy(src, dst, load_big.at[i])
        for i, (src, dst) in enumerate(
            ((ck, ck_s), (cv, cv_s), (pq, q_s), (fk, fk_s), (fv, fv_s))
        )
    ]
    for copy in big:
        copy.start()

    barrier = pltpu.get_barrier_semaphore()

    def greet_group(k, c):
        pl.semaphore_signal(
            barrier, inc=1, device_id={"group": (g + k) % n_groups}, device_id_type=MESH
        )
        return c

    def greet_tp(k, c):
        pl.semaphore_signal(barrier, inc=1, device_id={"tp": (t + k) % n_tp}, device_id_type=MESH)
        return c

    lax.fori_loop(1, n_groups, greet_group, 0)
    lax.fori_loop(1, n_tp, greet_tp, 0)
    pl.semaphore_signal(
        barrier, inc=1, device_id={"group": beside, "tp": partner}, device_id_type=MESH
    )
    pl.semaphore_wait(barrier, n_groups - 1 + n_tp - 1 + 1)

    to_right, to_left = {"tp": right}, {"tp": left}
    to_same, to_cross = {"group": beside}, {"group": beside, "tp": partner}
    ny = 1 - yh

    def y_first(i):
        return i % 3 != 1

    def hop(src, dst, kind, i, device):
        return pltpu.make_async_remote_copy(
            src_ref=src,
            dst_ref=dst,
            send_sem=x_send.at[i, kind],
            recv_sem=x_recv.at[i, kind],
            device_id=device,
            device_id_type=MESH,
        )

    def same(ref, kind, i, device):
        return hop(ref, ref, kind, i, device)

    keys, values = pl.ds(0, 2), pl.ds(2, 2)

    def own_right(i, xs):
        return same(kv.at[i, :, xs, yh], 0, i, to_right)

    def own_left(i, xs):
        return same(kv.at[i, :, xs, yh], 1, i, to_left)

    def one_y(i, part):
        rows_of = keys if part == 0 else values
        device = to_same if part == 0 else to_cross
        return hop(kv.at[i, rows_of, x, yh], rel.at[i, part, :, 0], 2 + part, i, device)

    def all_y(i, part):
        rows_of = keys if part == 0 else values
        device = to_same if part == 0 else to_cross
        return hop(kv.at[i, rows_of, :, yh], rel.at[i, part], 2 + part, i, device)

    def one_relay(i, part):
        if part == 0:
            return hop(rel.at[i, 0, :, 0], kv.at[i, keys, x, yh], 4, i, to_cross)
        return hop(rel.at[i, 1, :, 0], kv.at[i, values, x, ny], 5, i, to_same)

    def all_relay(i, part):
        if part == 0:
            return hop(rel.at[i, 0], kv.at[i, keys, :, yh], 4, i, to_cross)
        return hop(rel.at[i, 1], kv.at[i, values, :, ny], 5, i, to_same)

    def one_landed(i, part):
        return same(kv.at[i, (keys, values)[part], x, ny], 4 + part, i, to_same)

    def all_landed(i, part):
        return same(kv.at[i, (keys, values)[part], :, ny], 4 + part, i, to_same)

    def partner_right(i, xs):
        return same(kv.at[i, :, xs, ny], 6, i, to_right)

    def partner_left(i, xs):
        return same(kv.at[i, :, xs, ny], 7, i, to_left)

    def pair_right(i, xs):
        return same(kv.at[i, keys, xs], 8, i, to_right)

    def pair_left(i, xs):
        return same(kv.at[i, values, xs], 9, i, to_left)

    def single_right(i, xs):
        return same(kv.at[i, keys, xs, yh], 8, i, to_right)

    def single_left(i, xs):
        return same(kv.at[i, values, xs, yh], 9, i, to_left)

    def by_kind(i, first, second):
        pl.when(y_first(i))(lambda: first(i))
        pl.when(jnp.logical_not(y_first(i)))(lambda: second(i))

    def stage1(i):
        @pl.when(y_first(i))
        def _():
            one_y(i, 0).start()
            one_y(i, 1).start()

        own_right(i, x).start()
        own_left(i, x).start()

    def first_a(i):
        for part in range(2):
            one_y(i, part).wait_recv()
            one_relay(i, part).start()

    def first_b(i):
        one_landed(i, 0).wait_recv()
        one_landed(i, 1).wait_recv()
        partner_right(i, x).start()
        partner_left(i, x).start()

    def first_c(i):
        own_right(i, left_x).wait_recv()
        partner_right(i, left_x).wait_recv()
        pair_right(i, left_x).start()
        own_left(i, right_x).wait_recv()
        partner_left(i, right_x).wait_recv()
        pair_left(i, right_x).start()

    def first_d(i):
        pair_right(i, far_x).wait_recv()
        pair_left(i, far_x).wait_recv()

    def second_a(i):
        own_right(i, left_x).wait_recv()
        single_right(i, left_x).start()
        own_left(i, right_x).wait_recv()
        single_left(i, right_x).start()

    def second_b(i):
        single_right(i, far_x).wait_recv()
        single_left(i, far_x).wait_recv()
        all_y(i, 0).start()
        all_y(i, 1).start()

    def second_c(i):
        for part in range(2):
            all_y(i, part).wait_recv()
            all_relay(i, part).start()

    def second_d(i):
        all_landed(i, 0).wait_recv()
        all_landed(i, 1).wait_recv()

    def stage_a(i):
        by_kind(i, first_a, second_a)

    def stage_b(i):
        by_kind(i, first_b, second_b)

    def stage_c(i):
        by_kind(i, first_c, second_c)

    def stage_d(i):
        by_kind(i, first_d, second_d)

    def first_drain(i):
        for part in range(2):
            one_y(i, part).wait_send()
            one_relay(i, part).wait_send()
        partner_right(i, x).wait_send()
        partner_left(i, x).wait_send()
        pair_right(i, left_x).wait_send()
        pair_left(i, right_x).wait_send()

    def second_drain(i):
        for part in range(2):
            all_y(i, part).wait_send()
            all_relay(i, part).wait_send()
        single_right(i, left_x).wait_send()
        single_left(i, right_x).wait_send()

    def drain_item(i, c):
        own_right(i, x).wait_send()
        own_left(i, x).wait_send()
        by_kind(i, first_drain, second_drain)
        return c

    def start_item(i, c):
        for a in range(4):
            kv_load(i, a).wait()
        stage1(i)
        return c

    lax.fori_loop(0, KV_HEADS, start_item, 0)

    def msg_copy(k):
        peer = (g + k) % n_groups
        return pltpu.make_async_remote_copy(
            src_ref=msg.at[peer],
            dst_ref=rm.at[g],
            send_sem=m_send.at[k],
            recv_sem=m_recv.at[g],
            device_id={"group": peer},
            device_id_type=MESH,
        )

    def msg_wait(k):
        peer = (g + k) % n_groups
        pltpu.make_async_remote_copy(
            src_ref=rm.at[peer],
            dst_ref=rm.at[peer],
            send_sem=m_send.at[k],
            recv_sem=m_recv.at[peer],
            device_id={"group": peer},
            device_id_type=MESH,
        ).wait_recv()

    def send_msg(k, c):
        msg_copy(k).start()
        return c

    def wait_msg(k, c):
        msg_wait(k)
        return c

    pair = (n_groups, CAPACITY, ROWS16, HEAD_DIM)
    row_id = lax.broadcasted_iota(jnp.int32, (1, ROWS16, 1), 1)
    extra = jnp.zeros((n_groups * CAPACITY, ROWS16, HEAD_DIM), jnp.float32)
    for step in range(STEPS):
        nk = ank[...].astype(jnp.float32)[:, step : step + 1]
        nv = anv[...].astype(jnp.float32)[:, step : step + 1]
        extra = jnp.where(row_id == step, nk, jnp.where(row_id == STEPS + step, nv, extra))
    msg[:, :, 0:ROWS16, :] = arrival_q[...]
    msg[:, :, ROWS16 : 2 * ROWS16, :] = extra.astype(jnp.bfloat16).reshape(pair)
    lax.fori_loop(1, n_groups, send_msg, 0)
    rm[g] = msg[g]

    def decode():
        big[0].wait()
        big[1].wait()
        b = dnk.shape[0]
        q = dq[...].reshape(b, ROWS16, HEAD_DIM)
        s = lax.dot_general(
            q, ck_s[...], (((2,), (2,)), ((0,), (0,))), preferred_element_type=jnp.float32
        )
        limit = spread(context[...].astype(jnp.float32), b, ROWS16, 0).reshape(b, ROWS16, 1)
        slot = lax.broadcasted_iota(jnp.int32, s.shape, 2).astype(jnp.float32)
        s = jnp.where(slot < limit, s, NEG)
        nk = dnk[...].astype(jnp.float32)
        nv = dnv[...].astype(jnp.float32)
        n0, n1 = new_scores(q.astype(jnp.float32), (nk[:, 0:1], nk[:, 1:2]))
        m = jnp.maximum(jnp.max(s, axis=2, keepdims=True), jnp.maximum(n0, n1))
        w = jnp.exp2((s - m) * RATE)
        w0 = jnp.exp2((n0 - m) * RATE)
        w1 = jnp.exp2((n1 - m) * RATE)
        total = jnp.sum(w, axis=2, keepdims=True) + w0 + w1
        o = lax.dot_general(
            w.astype(jnp.bfloat16),
            cv_s[...],
            (((2,), (1,)), ((0,), (0,))),
            preferred_element_type=jnp.float32,
        )
        o = o + w0.astype(jnp.bfloat16).astype(jnp.float32) * nv[:, 0:1]
        o = o + w1.astype(jnp.bfloat16).astype(jnp.float32) * nv[:, 1:2]
        d_out[...] = (o / total).reshape(b * ROWS16, HEAD_DIM).astype(jnp.bfloat16)

    def quad_rows(i):
        half = i % 2 * (4 * ROWS16)
        return i // 2, slice(half, half + 4 * ROWS16)

    def queries_of(xs, ys):
        parts = []
        for i in range(quads):
            block, part = quad_rows(i)
            parts.append(kv[QUERY_ITEM, block, xs, ys, part, :])
        return jnp.concatenate(parts, axis=0)

    def arrivals_choose():
        lax.fori_loop(1, n_groups, wait_msg, 0)
        lanes = routes.shape[1]
        per_row = lanes // n_prompts
        base = g % per_row * n_prompts
        own = routes[pl.ds(g // per_row, 1), :].astype(jnp.float32)
        dest = spread(own, n_prompts, ROWS16, base)
        owner = lax.broadcasted_iota(jnp.int32, (a_rows, lanes), 0) // ROWS16
        other = lax.broadcasted_iota(jnp.int32, (a_rows, lanes), 1) - base
        rank = jnp.sum(
            jnp.where((dest == own) & (other >= 0) & (other < owner), 1.0, 0.0),
            axis=1,
            keepdims=True,
        )
        within = lax.broadcasted_iota(jnp.int32, (a_rows, 1), 0) % ROWS16
        target = (dest * CAPACITY + rank) * ROWS16 + within.astype(jnp.float32)
        slot_rows = n_groups * CAPACITY * ROWS16
        column = lax.broadcasted_iota(jnp.int32, (a_rows, slot_rows), 1).astype(jnp.float32)
        sel[...] = jnp.where(column == target, 1.0, 0.0).astype(jnp.bfloat16)
        got = rm[:, :, 0:ROWS16, :].reshape(slot_rows, HEAD_DIM)
        chosen = dot_n(sel[...], got).astype(jnp.bfloat16)
        for i in range(quads):
            block, part = quad_rows(i)
            kv[QUERY_ITEM, block, x, yh, part, :] = chosen[i * 4 * ROWS16 : (i + 1) * 4 * ROWS16]
        stage1(QUERY_ITEM)
        own_len = lengths[pl.ds(g // per_row, 1), :].astype(jnp.float32)
        limit = spread(own_len, n_prompts, ROWS16, base) - (t * local_len).astype(jnp.float32)
        col = lax.broadcasted_iota(jnp.int32, (a_rows, HEAD_DIM), 1)
        quad_row = (lax.broadcasted_iota(jnp.int32, (a_rows, HEAD_DIM), 0) // ROWS16) % 4
        keep = (col // local_len == quad_row) & ((col % local_len).astype(jnp.float32) < limit)
        bias[...] = jnp.where(keep, 0.0, NEG)

    def po_copy(h, k):
        return pltpu.make_async_remote_copy(
            src_ref=po.at[h],
            dst_ref=ro.at[t],
            send_sem=o_send.at[k],
            recv_sem=o_recv.at[t],
            device_id={"tp": h},
            device_id_type=MESH,
        )

    def ps_copy(h, k):
        return pltpu.make_async_remote_copy(
            src_ref=ps.at[h],
            dst_ref=rs.at[t],
            send_sem=s_send.at[k],
            recv_sem=s_recv.at[t],
            device_id={"tp": h},
            device_id_type=MESH,
        )

    def po_wait(k):
        peer = (t + k) % n_tp
        for send_sem, recv_sem, ref in ((o_send, o_recv, ro), (s_send, s_recv, rs)):
            pltpu.make_async_remote_copy(
                src_ref=ref.at[peer],
                dst_ref=ref.at[peer],
                send_sem=send_sem.at[k],
                recv_sem=recv_sem.at[peer],
                device_id={"tp": peer},
                device_id_type=MESH,
            ).wait_recv()

    def partial_head(h, o_ref, s_ref, at):
        cols = pl.ds(pl.multiple_of(h * HEAD_DIM, HEAD_DIM), HEAD_DIM)
        lane = lax.broadcasted_iota(jnp.int32, (4 * ROWS16, HEAD_DIM), 1)
        stats = jnp.zeros((4 * ROWS16, HEAD_DIM), jnp.float32)
        for i in range(quads):
            rows_i = slice(i * 4 * ROWS16, (i + 1) * 4 * ROWS16)
            keys_i = slice(i * HEAD_DIM, (i + 1) * HEAD_DIM)
            block, part = quad_rows(i)
            q = kv[QUERY_ITEM, block, h // 2, h % 2, part, :]
            s = dot_t(q, fk_s[keys_i, cols]) + bias[rows_i, :]
            m = jnp.max(s, axis=1, keepdims=True)
            w = jnp.exp2((s - m) * RATE)
            total = jnp.sum(w, axis=1, keepdims=True)
            o_ref[at, rows_i, :] = dot_n(w.astype(jnp.bfloat16), fv_s[keys_i, cols]).astype(
                jnp.bfloat16
            )
            stats = jnp.where(lane == i, m, stats)
            stats = jnp.where(lane == quads + i, total, stats)
        s_ref[at] = stats

    def arrivals_partial():
        stage_d(QUERY_ITEM)
        big[3].wait()
        big[4].wait()

        def one(k, c):
            h = (t + k) % n_tp
            partial_head(h, po, ps, h)
            po_copy(h, k).start()
            ps_copy(h, k).start()
            return c

        lax.fori_loop(1, n_tp, one, 0)
        partial_head(t, ro, rs, t)

    def ret_copy(k):
        peer = (g + k) % n_groups
        return pltpu.make_async_remote_copy(
            src_ref=ret.at[peer],
            dst_ref=ao.at[g],
            send_sem=b_send.at[k],
            recv_sem=b_recv.at[g],
            device_id={"group": peer},
            device_id_type=MESH,
        )

    def ret_wait(k):
        peer = (g + k) % n_groups
        pltpu.make_async_remote_copy(
            src_ref=ao.at[peer],
            dst_ref=ao.at[peer],
            send_sem=b_send.at[k],
            recv_sem=b_recv.at[peer],
            device_id={"group": peer},
            device_id_type=MESH,
        ).wait_recv()

    def arrivals_join():
        def wait(k, c):
            po_wait(k)
            return c

        lax.fori_loop(1, n_tp, wait, 0)
        slot_rows = n_groups * CAPACITY * ROWS16
        extra = rm[:, :, ROWS16 : 2 * ROWS16, :].reshape(slot_rows, HEAD_DIM)
        new = dot_n(sel[...], extra).reshape(n_prompts, ROWS16, HEAD_DIM)
        q3 = queries_of(x, yh).astype(jnp.float32).reshape(n_prompts, ROWS16, HEAD_DIM)
        n0, n1 = new_scores(q3, (new[:, 0:1], new[:, 1:2]))
        n0 = n0.reshape(a_rows, 1)
        n1 = n1.reshape(a_rows, 1)
        ms = [
            jnp.concatenate([rs[p][:, i : i + 1] for i in range(quads)], axis=0)
            for p in range(n_tp)
        ]
        m = jnp.maximum(n0, n1)
        for mp in ms:
            m = jnp.maximum(m, mp)
        w0 = jnp.exp2((n0 - m) * RATE)
        w1 = jnp.exp2((n1 - m) * RATE)
        total = w0 + w1
        o = jnp.zeros((a_rows, HEAD_DIM), jnp.float32)
        for p in range(n_tp):
            wp = jnp.exp2((ms[p] - m) * RATE)
            lp = jnp.concatenate(
                [rs[p][:, quads + i : quads + i + 1] for i in range(quads)], axis=0
            )
            total = total + wp * lp
            o = o + wp * ro[p].astype(jnp.float32)
        w0 = w0.astype(jnp.bfloat16).astype(jnp.float32).reshape(n_prompts, ROWS16, 1)
        w1 = w1.astype(jnp.bfloat16).astype(jnp.float32).reshape(n_prompts, ROWS16, 1)
        o = o + (w0 * new[:, 2:3] + w1 * new[:, 3:4]).reshape(a_rows, HEAD_DIM)
        res = (o / total).astype(jnp.bfloat16)
        back = lax.dot_general(
            sel[...], res, (((0,), (0,)), ((), ())), preferred_element_type=jnp.float32
        )
        ret[...] = back.astype(jnp.bfloat16).reshape(n_groups, CAPACITY, ROWS16, HEAD_DIM)

        def send(k, c):
            ret_copy(k).start()
            return c

        lax.fori_loop(1, n_groups, send, 0)

    def prefill_head(h):
        vis = span_offset[0] > 0
        part = 4
        n_rows = part * rows
        kp = kv[h, 0].reshape(n_tp * rows, HEAD_DIM)
        ks = kv[h, 1].reshape(n_tp * rows, HEAD_DIM)
        vp = kv[h, 2].reshape(n_tp * rows, HEAD_DIM)
        vs = kv[h, 3].reshape(n_tp * rows, HEAD_DIM)
        position = lax.broadcasted_iota(jnp.int32, (n_rows, 1), 0) % rows + t * rows
        key_ids = lax.broadcasted_iota(jnp.int32, (n_rows, n_tp * rows), 1)
        live = span_offset[0] + position < prompt_length[0]

        def half(j, c):
            def cols(i):
                start = h * (GROUP_SIZE * HEAD_DIM) + (j * part + i) * HEAD_DIM
                return pl.ds(pl.multiple_of(start, HEAD_DIM), HEAD_DIM)

            q = jnp.concatenate([q_s[:, cols(i)] for i in range(part)], axis=0)
            sp = dot_t(q, kp)
            ss = jnp.where(key_ids <= position, dot_t(q, ks), NEG)
            mp = jnp.max(sp, axis=1, keepdims=True)
            m = jnp.max(ss, axis=1, keepdims=True)
            m = jnp.where(vis, jnp.maximum(m, mp), m)
            wp = jnp.exp2((sp - jnp.where(vis, m, -NEG)) * RATE)
            ws = jnp.exp2((ss - m) * RATE)
            total = jnp.sum(wp, axis=1, keepdims=True) + jnp.sum(ws, axis=1, keepdims=True)
            o = dot_n(wp.astype(jnp.bfloat16), vp) + dot_n(ws.astype(jnp.bfloat16), vs)
            o = jnp.where(live, o / total, 0.0).astype(jnp.bfloat16)
            for i in range(part):
                q_s[:, cols(i)] = o[i * rows : (i + 1) * rows]
            return c

        lax.fori_loop(0, GROUP_SIZE // part, half, 0)

    def head_out(h):
        width = GROUP_SIZE * HEAD_DIM
        cols = pl.ds(pl.multiple_of(h * width, width), width)
        return pltpu.make_async_copy(q_s.at[:, cols], p_out.at[:, cols], out_sem.at[h])

    decode()
    for h in range(3):
        stage_a(h)
    arrivals_choose()
    for h in range(2):
        stage_b(h)
    stage_c(0)
    stage_a(QUERY_ITEM)
    big[2].wait()

    def turn(s, c):
        @pl.when(s + 3 < KV_HEADS)
        def _():
            stage_a(s + 3)

        @pl.when(s + 2 < KV_HEADS)
        def _():
            stage_b(s + 2)

        @pl.when(s + 1 < KV_HEADS)
        def _():
            stage_c(s + 1)

        @pl.when(s == 0)
        def _():
            stage_b(QUERY_ITEM)

        @pl.when(s == 1)
        def _():
            stage_c(QUERY_ITEM)

        @pl.when(s == 2)
        def _():
            arrivals_partial()

        @pl.when(s == 5)
        def _():
            arrivals_join()

        stage_d(s)
        prefill_head(s)
        head_out(s).start()
        return c

    lax.fori_loop(0, KV_HEADS, turn, 0)

    def wait_ret(k, c):
        ret_wait(k)
        return c

    lax.fori_loop(1, n_groups, wait_ret, 0)
    ao[g] = ret[g]
    a_out[...] = ao[...]

    def drain_group(k, c):
        msg_copy(k).wait_send()
        ret_copy(k).wait_send()
        return c

    def drain_tp(k, c):
        h = (t + k) % n_tp
        po_copy(h, k).wait_send()
        ps_copy(h, k).wait_send()
        return c

    def drain_out(h, c):
        head_out(h).wait()
        return c

    lax.fori_loop(1, n_groups, drain_group, 0)
    lax.fori_loop(1, n_tp, drain_tp, 0)
    lax.fori_loop(0, ITEMS, drain_item, 0)
    lax.fori_loop(0, KV_HEADS, drain_out, 0)


def to_rows(queries):
    b = queries.shape[0]
    return queries.reshape(b, STEPS, GROUP_SIZE, HEAD_DIM).transpose(0, 2, 1, 3)


def from_rows(rows, b):
    rows = rows.reshape(b, GROUP_SIZE, STEPS, HEAD_DIM).transpose(0, 2, 1, 3)
    return rows.reshape(b, STEPS, GROUP_SIZE * HEAD_DIM)


def local(
    prefill_queries,
    span_keys,
    span_values,
    prefix_keys,
    prefix_values,
    span_offsets,
    prompt_lengths,
    decode_queries,
    decode_new_keys,
    decode_new_values,
    cache_keys,
    cache_values,
    context_lengths,
    placement,
    finished_lengths,
    finished_keys,
    finished_values,
    arrival_queries,
    arrival_new_keys,
    arrival_new_values,
):
    n_groups = lax.axis_size("group")
    n_tp = lax.axis_size("tp")
    n_prompts, local_len, width = finished_keys.shape
    rows = prefill_queries.shape[0]
    dec = decode_queries.shape[0]
    slots = arrival_queries.shape[0]
    dq = to_rows(decode_queries).reshape(dec * ROWS16, HEAD_DIM)
    arrival_rows = to_rows(arrival_queries).reshape(n_groups, CAPACITY, ROWS16, HEAD_DIM)
    lanes = min(128, placement.shape[0])
    any_ = pl.BlockSpec(memory_space=pl.ANY)
    vmem = pl.BlockSpec(memory_space=pltpu.VMEM)
    smem = pl.BlockSpec(memory_space=pltpu.SMEM)
    bf, f32 = jnp.bfloat16, jnp.float32
    a_rows = n_prompts * ROWS16
    dma = pltpu.SemaphoreType.DMA
    p_out, d_out, a_out = pl.pallas_call(
        functools.partial(body, n_groups, n_tp),
        out_shape=(
            jax.ShapeDtypeStruct(prefill_queries.shape, bf),
            jax.ShapeDtypeStruct(dq.shape, bf),
            jax.ShapeDtypeStruct((n_groups, CAPACITY, ROWS16, HEAD_DIM), bf),
        ),
        in_specs=[any_] * 5
        + [smem] * 2
        + [vmem] * 3
        + [any_] * 2
        + [vmem] * 3
        + [any_] * 2
        + [vmem] * 3,
        out_specs=[any_, vmem, vmem],
        scratch_shapes=[
            pltpu.VMEM((ITEMS, 4, X_CHIPS, 2, rows, HEAD_DIM), bf),
            pltpu.VMEM(prefill_queries.shape, bf),
            pltpu.VMEM(cache_keys.shape, bf),
            pltpu.VMEM(cache_values.shape, bf),
            pltpu.VMEM((n_prompts * local_len, width), bf),
            pltpu.VMEM((n_prompts * local_len, width), bf),
            pltpu.VMEM((ITEMS, 2, 2, X_CHIPS, rows, HEAD_DIM), bf),
            pltpu.VMEM((n_groups, CAPACITY, 2 * ROWS16, HEAD_DIM), bf),
            pltpu.VMEM((n_groups, CAPACITY, 2 * ROWS16, HEAD_DIM), bf),
            pltpu.VMEM((n_tp, a_rows, HEAD_DIM), bf),
            pltpu.VMEM((n_tp, a_rows, HEAD_DIM), bf),
            pltpu.VMEM((n_tp, 4 * ROWS16, HEAD_DIM), f32),
            pltpu.VMEM((n_tp, 4 * ROWS16, HEAD_DIM), f32),
            pltpu.VMEM((a_rows, slots * ROWS16), bf),
            pltpu.VMEM((a_rows, HEAD_DIM), f32),
            pltpu.VMEM((n_groups, CAPACITY, ROWS16, HEAD_DIM), bf),
            pltpu.VMEM((n_groups, CAPACITY, ROWS16, HEAD_DIM), bf),
            dma((KV_HEADS, 4)),
            dma((5,)),
            dma((ITEMS, 10)),
            dma((ITEMS, 10)),
            dma((n_groups,)),
            dma((n_groups,)),
            dma((n_tp,)),
            dma((n_tp,)),
            dma((n_tp,)),
            dma((n_tp,)),
            dma((n_groups,)),
            dma((n_groups,)),
            dma((KV_HEADS,)),
        ],
        compiler_params=pltpu.CompilerParams(
            collective_id=0, has_side_effects=True, vmem_limit_bytes=56 * 1024 * 1024
        ),
    )(
        prefill_queries,
        span_keys,
        span_values,
        prefix_keys,
        prefix_values,
        span_offsets,
        prompt_lengths,
        dq,
        decode_new_keys,
        decode_new_values,
        cache_keys,
        cache_values,
        context_lengths[None, :],
        placement.reshape(-1, lanes),
        finished_lengths.reshape(-1, lanes),
        finished_keys.reshape(n_prompts * local_len, width),
        finished_values.reshape(n_prompts * local_len, width),
        arrival_rows,
        arrival_new_keys,
        arrival_new_values,
    )
    return (p_out, from_rows(d_out, dec), from_rows(a_out, slots))


def solution(mesh):
    both = P(("group", "tp"), None)
    heads = P("group", None, "tp")
    placed = (
        (both,) * 5
        + (P("group"),) * 2
        + (heads,) * 5
        + (P("group"), P(), P())
        + (P("group", "tp", None),) * 2
        + (heads,) * 3
    )
    return jax.shard_map(
        local,
        mesh=mesh,
        in_specs=placed,
        out_specs=(both, heads, heads),
        check_vma=False,
    )
```

```python
import functools
import math

import jax
import jax.numpy as jnp
from jax import lax
from jax.experimental import pallas as pl
from jax.experimental.pallas import tpu as pltpu
from jax.sharding import PartitionSpec as P

KV_HEADS = 8
GROUP_SIZE = 8
HEAD_DIM = 128
CAPACITY = 2
STEPS = 2
ROWS16 = GROUP_SIZE * STEPS
MESH = pl.DeviceIdType.MESH
NEG = -1e30
RATE = math.log2(math.e) / math.sqrt(HEAD_DIM)
X_CHIPS = 4
CORES = 2
ITEMS = KV_HEADS + 1
QUERY_ITEM = KV_HEADS


def dot_t(a, b):
    return lax.dot_general(a, b, (((1,), (1,)), ((), ())), preferred_element_type=jnp.float32)


def dot_n(a, b):
    return lax.dot_general(a, b, (((1,), (0,)), ((), ())), preferred_element_type=jnp.float32)


def spread(row, count, reps, base):
    shape = (count * reps, row.shape[1])
    owner = lax.broadcasted_iota(jnp.int32, shape, 0) // reps + base
    lane = lax.broadcasted_iota(jnp.int32, shape, 1)
    return jnp.sum(jnp.where(owner == lane, row, 0.0), axis=1, keepdims=True)


def new_scores(q3, nk):
    shape = q3.shape[:2] + (1,)
    step = lax.broadcasted_iota(jnp.int32, shape, 1) % STEPS
    first = jnp.sum(q3 * nk[0], axis=2, keepdims=True)
    second = jnp.sum(q3 * nk[1], axis=2, keepdims=True)
    return first, jnp.where(step >= 1, second, NEG)


def body(
    n_groups,
    n_tp,
    pq,
    sk,
    sv,
    pk,
    pv,
    span_offset,
    prompt_length,
    dq,
    dnk,
    dnv,
    ck,
    cv,
    context,
    routes,
    lengths,
    fk,
    fv,
    arrival_q,
    ank,
    anv,
    p_out,
    d_out,
    a_out,
    kv,
    q_s,
    ck_s,
    cv_s,
    fk_s,
    fv_s,
    rel,
    msg,
    rm,
    po,
    ro,
    ps,
    rs,
    sel,
    bias,
    key_mask,
    eye,
    ret,
    ao,
    load_kv,
    load_big,
    x_send,
    x_recv,
    m_send,
    m_recv,
    o_send,
    o_recv,
    s_send,
    s_recv,
    b_send,
    b_recv,
    out_sem,
):
    g = lax.axis_index("group")
    t = lax.axis_index("tp")
    x, yh = t // 2, t % 2
    right = ((x + 1) % X_CHIPS) * 2 + yh
    left = ((x + X_CHIPS - 1) % X_CHIPS) * 2 + yh
    partner = x * 2 + (1 - yh)
    right_x = (x + 1) % X_CHIPS
    left_x = (x + X_CHIPS - 1) % X_CHIPS
    far_x = (x + 2) % X_CHIPS
    yl = (g // CORES) % 2
    beside = g + CORES * (1 - 2 * yl)
    local_len = HEAD_DIM // 4
    n_prompts = fk_s.shape[0] // local_len
    a_rows = n_prompts * ROWS16
    quads = n_prompts // 4
    rows = pq.shape[0]

    arrays = (pk, sk, pv, sv)

    def kv_load(h, a):
        cols = pl.ds(pl.multiple_of(h * HEAD_DIM, HEAD_DIM), HEAD_DIM)
        return pltpu.make_async_copy(arrays[a].at[:, cols], kv.at[h, a, x, yh], load_kv.at[h, a])

    def start_loads(h, c):
        for a in range(4):
            kv_load(h, a).start()
        return c

    lax.fori_loop(0, KV_HEADS, start_loads, 0)
    big = [
        pltpu.make_async_copy(src, dst, load_big.at[i])
        for i, (src, dst) in enumerate(
            ((ck, ck_s), (cv, cv_s), (pq, q_s), (fk, fk_s), (fv, fv_s))
        )
    ]
    for copy in big:
        copy.start()

    barrier = pltpu.get_barrier_semaphore()

    def greet_group(k, c):
        pl.semaphore_signal(
            barrier, inc=1, device_id={"group": (g + k) % n_groups}, device_id_type=MESH
        )
        return c

    def greet_tp(k, c):
        pl.semaphore_signal(barrier, inc=1, device_id={"tp": (t + k) % n_tp}, device_id_type=MESH)
        return c

    lax.fori_loop(1, n_groups, greet_group, 0)
    lax.fori_loop(1, n_tp, greet_tp, 0)
    pl.semaphore_signal(
        barrier, inc=1, device_id={"group": beside, "tp": partner}, device_id_type=MESH
    )
    pl.semaphore_wait(barrier, n_groups - 1 + n_tp - 1 + 1)

    to_right, to_left = {"tp": right}, {"tp": left}
    to_same, to_cross = {"group": beside}, {"group": beside, "tp": partner}
    ny = 1 - yh

    def y_first(i):
        return i % 3 != 1

    def hop(src, dst, kind, i, device):
        return pltpu.make_async_remote_copy(
            src_ref=src,
            dst_ref=dst,
            send_sem=x_send.at[i, kind],
            recv_sem=x_recv.at[i, kind],
            device_id=device,
            device_id_type=MESH,
        )

    def same(ref, kind, i, device):
        return hop(ref, ref, kind, i, device)

    keys, values = pl.ds(0, 2), pl.ds(2, 2)

    def own_right(i, xs):
        return same(kv.at[i, :, xs, yh], 0, i, to_right)

    def own_left(i, xs):
        return same(kv.at[i, :, xs, yh], 1, i, to_left)

    def one_y(i, part):
        rows_of = keys if part == 0 else values
        device = to_same if part == 0 else to_cross
        return hop(kv.at[i, rows_of, x, yh], rel.at[i, part, :, 0], 2 + part, i, device)

    def all_y(i, part):
        rows_of = keys if part == 0 else values
        device = to_same if part == 0 else to_cross
        return hop(kv.at[i, rows_of, :, yh], rel.at[i, part], 2 + part, i, device)

    def one_relay(i, part):
        if part == 0:
            return hop(rel.at[i, 0, :, 0], kv.at[i, keys, x, yh], 4, i, to_cross)
        return hop(rel.at[i, 1, :, 0], kv.at[i, values, x, ny], 5, i, to_same)

    def all_relay(i, part):
        if part == 0:
            return hop(rel.at[i, 0], kv.at[i, keys, :, yh], 4, i, to_cross)
        return hop(rel.at[i, 1], kv.at[i, values, :, ny], 5, i, to_same)

    def one_landed(i, part):
        return same(kv.at[i, (keys, values)[part], x, ny], 4 + part, i, to_same)

    def all_landed(i, part):
        return same(kv.at[i, (keys, values)[part], :, ny], 4 + part, i, to_same)

    def partner_right(i, xs):
        return same(kv.at[i, :, xs, ny], 6, i, to_right)

    def partner_left(i, xs):
        return same(kv.at[i, :, xs, ny], 7, i, to_left)

    def pair_right(i, xs):
        return same(kv.at[i, keys, xs], 8, i, to_right)

    def pair_left(i, xs):
        return same(kv.at[i, values, xs], 9, i, to_left)

    def single_right(i, xs):
        return same(kv.at[i, keys, xs, yh], 8, i, to_right)

    def single_left(i, xs):
        return same(kv.at[i, values, xs, yh], 9, i, to_left)

    def by_kind(i, first, second):
        pl.when(y_first(i))(lambda: first(i))
        pl.when(jnp.logical_not(y_first(i)))(lambda: second(i))

    def stage1(i):
        @pl.when(y_first(i))
        def _():
            one_y(i, 0).start()
            one_y(i, 1).start()

        own_right(i, x).start()
        own_left(i, x).start()

    def first_a(i):
        for part in range(2):
            one_y(i, part).wait_recv()
            one_relay(i, part).start()

    def first_b(i):
        one_landed(i, 0).wait_recv()
        one_landed(i, 1).wait_recv()
        partner_right(i, x).start()
        partner_left(i, x).start()

    def first_c(i):
        own_right(i, left_x).wait_recv()
        partner_right(i, left_x).wait_recv()
        pair_right(i, left_x).start()
        own_left(i, right_x).wait_recv()
        partner_left(i, right_x).wait_recv()
        pair_left(i, right_x).start()

    def first_d(i):
        pair_right(i, far_x).wait_recv()
        pair_left(i, far_x).wait_recv()

    def second_a(i):
        own_right(i, left_x).wait_recv()
        single_right(i, left_x).start()
        own_left(i, right_x).wait_recv()
        single_left(i, right_x).start()

    def second_b(i):
        single_right(i, far_x).wait_recv()
        single_left(i, far_x).wait_recv()
        all_y(i, 0).start()
        all_y(i, 1).start()

    def second_c(i):
        for part in range(2):
            all_y(i, part).wait_recv()
            all_relay(i, part).start()

    def second_d(i):
        all_landed(i, 0).wait_recv()
        all_landed(i, 1).wait_recv()

    def stage_a(i):
        by_kind(i, first_a, second_a)

    def stage_b(i):
        by_kind(i, first_b, second_b)

    def stage_c(i):
        by_kind(i, first_c, second_c)

    def stage_d(i):
        by_kind(i, first_d, second_d)

    def first_drain(i):
        for part in range(2):
            one_y(i, part).wait_send()
            one_relay(i, part).wait_send()
        partner_right(i, x).wait_send()
        partner_left(i, x).wait_send()
        pair_right(i, left_x).wait_send()
        pair_left(i, right_x).wait_send()

    def second_drain(i):
        for part in range(2):
            all_y(i, part).wait_send()
            all_relay(i, part).wait_send()
        single_right(i, left_x).wait_send()
        single_left(i, right_x).wait_send()

    def drain_item(i, c):
        own_right(i, x).wait_send()
        own_left(i, x).wait_send()
        by_kind(i, first_drain, second_drain)
        return c

    def start_item(i, c):
        for a in range(4):
            kv_load(i, a).wait()
        stage1(i)
        return c

    window = 4
    lax.fori_loop(0, window, start_item, 0)

    def msg_copy(k):
        peer = (g + k) % n_groups
        return pltpu.make_async_remote_copy(
            src_ref=msg.at[peer],
            dst_ref=rm.at[g],
            send_sem=m_send.at[k],
            recv_sem=m_recv.at[g],
            device_id={"group": peer},
            device_id_type=MESH,
        )

    def msg_wait(k):
        peer = (g + k) % n_groups
        pltpu.make_async_remote_copy(
            src_ref=rm.at[peer],
            dst_ref=rm.at[peer],
            send_sem=m_send.at[k],
            recv_sem=m_recv.at[peer],
            device_id={"group": peer},
            device_id_type=MESH,
        ).wait_recv()

    def send_msg(k, c):
        msg_copy(k).start()
        return c

    def wait_msg(k, c):
        msg_wait(k)
        return c

    pair = (n_groups, CAPACITY, ROWS16, HEAD_DIM)
    row_id = lax.broadcasted_iota(jnp.int32, (1, ROWS16, 1), 1)
    extra = jnp.zeros((n_groups * CAPACITY, ROWS16, HEAD_DIM), jnp.float32)
    for step in range(STEPS):
        nk = ank[...].astype(jnp.float32)[:, step : step + 1]
        nv = anv[...].astype(jnp.float32)[:, step : step + 1]
        extra = jnp.where(row_id == step, nk, jnp.where(row_id == STEPS + step, nv, extra))
    msg[:, :, 0:ROWS16, :] = arrival_q[...]
    msg[:, :, ROWS16 : 2 * ROWS16, :] = extra.astype(jnp.bfloat16).reshape(pair)
    lax.fori_loop(1, n_groups, send_msg, 0)
    rm[g] = msg[g]

    def decode():
        big[0].wait()
        big[1].wait()
        b = dnk.shape[0]
        q = dq[...].reshape(b, ROWS16, HEAD_DIM)
        s = lax.dot_general(
            q, ck_s[...], (((2,), (2,)), ((0,), (0,))), preferred_element_type=jnp.float32
        )
        limit = spread(context[...].astype(jnp.float32), b, ROWS16, 0).reshape(b, ROWS16, 1)
        slot = lax.broadcasted_iota(jnp.int32, s.shape, 2).astype(jnp.float32)
        s = jnp.where(slot < limit, s, NEG)
        nk = dnk[...].astype(jnp.float32)
        nv = dnv[...].astype(jnp.float32)
        n0, n1 = new_scores(q.astype(jnp.float32), (nk[:, 0:1], nk[:, 1:2]))
        m = jnp.maximum(jnp.max(s, axis=2, keepdims=True), jnp.maximum(n0, n1))
        w = jnp.exp2((s - m) * RATE)
        w0 = jnp.exp2((n0 - m) * RATE)
        w1 = jnp.exp2((n1 - m) * RATE)
        total = jnp.sum(w, axis=2, keepdims=True) + w0 + w1
        o = lax.dot_general(
            w.astype(jnp.bfloat16),
            cv_s[...],
            (((2,), (1,)), ((0,), (0,))),
            preferred_element_type=jnp.float32,
        )
        o = o + w0.astype(jnp.bfloat16).astype(jnp.float32) * nv[:, 0:1]
        o = o + w1.astype(jnp.bfloat16).astype(jnp.float32) * nv[:, 1:2]
        d_out[...] = (o / total).reshape(b * ROWS16, HEAD_DIM).astype(jnp.bfloat16)

    def quad_rows(i):
        half = i % 2 * (4 * ROWS16)
        return i // 2, slice(half, half + 4 * ROWS16)

    def queries_of(xs, ys):
        parts = []
        for i in range(quads):
            block, part = quad_rows(i)
            parts.append(kv[QUERY_ITEM, block, xs, ys, part, :])
        return jnp.concatenate(parts, axis=0)

    def arrivals_choose():
        lax.fori_loop(1, n_groups, wait_msg, 0)
        lanes = routes.shape[1]
        per_row = lanes // n_prompts
        base = g % per_row * n_prompts
        own = routes[pl.ds(g // per_row, 1), :].astype(jnp.float32)
        dest = spread(own, n_prompts, ROWS16, base)
        owner = lax.broadcasted_iota(jnp.int32, (a_rows, lanes), 0) // ROWS16
        other = lax.broadcasted_iota(jnp.int32, (a_rows, lanes), 1) - base
        rank = jnp.sum(
            jnp.where((dest == own) & (other >= 0) & (other < owner), 1.0, 0.0),
            axis=1,
            keepdims=True,
        )
        within = lax.broadcasted_iota(jnp.int32, (a_rows, 1), 0) % ROWS16
        target = (dest * CAPACITY + rank) * ROWS16 + within.astype(jnp.float32)
        slot_rows = n_groups * CAPACITY * ROWS16
        column = lax.broadcasted_iota(jnp.int32, (a_rows, slot_rows), 1).astype(jnp.float32)
        sel[...] = jnp.where(column == target, 1.0, 0.0).astype(jnp.bfloat16)
        got = rm[:, :, 0:ROWS16, :].reshape(slot_rows, HEAD_DIM)
        chosen = dot_n(sel[...], got).astype(jnp.bfloat16)
        for i in range(quads):
            block, part = quad_rows(i)
            kv[QUERY_ITEM, block, x, yh, part, :] = chosen[i * 4 * ROWS16 : (i + 1) * 4 * ROWS16]
        stage1(QUERY_ITEM)
        own_len = lengths[pl.ds(g // per_row, 1), :].astype(jnp.float32)
        limit = spread(own_len, n_prompts, ROWS16, base) - (t * local_len).astype(jnp.float32)
        col = lax.broadcasted_iota(jnp.int32, (a_rows, HEAD_DIM), 1)
        quad_row = (lax.broadcasted_iota(jnp.int32, (a_rows, HEAD_DIM), 0) // ROWS16) % 4
        keep = (col // local_len == quad_row) & ((col % local_len).astype(jnp.float32) < limit)
        bias[...] = jnp.where(keep, 0.0, NEG)

    def po_copy(h, k):
        return pltpu.make_async_remote_copy(
            src_ref=po.at[h],
            dst_ref=ro.at[t],
            send_sem=o_send.at[k],
            recv_sem=o_recv.at[t],
            device_id={"tp": h},
            device_id_type=MESH,
        )

    def ps_copy(h, k):
        return pltpu.make_async_remote_copy(
            src_ref=ps.at[h],
            dst_ref=rs.at[t],
            send_sem=s_send.at[k],
            recv_sem=s_recv.at[t],
            device_id={"tp": h},
            device_id_type=MESH,
        )

    def po_wait(k):
        peer = (t + k) % n_tp
        for send_sem, recv_sem, ref in ((o_send, o_recv, ro), (s_send, s_recv, rs)):
            pltpu.make_async_remote_copy(
                src_ref=ref.at[peer],
                dst_ref=ref.at[peer],
                send_sem=send_sem.at[k],
                recv_sem=recv_sem.at[peer],
                device_id={"tp": peer},
                device_id_type=MESH,
            ).wait_recv()

    def partial_head(h, o_ref, s_ref, at):
        cols = pl.ds(pl.multiple_of(h * HEAD_DIM, HEAD_DIM), HEAD_DIM)
        lane = lax.broadcasted_iota(jnp.int32, (4 * ROWS16, HEAD_DIM), 1)
        stats = jnp.zeros((4 * ROWS16, HEAD_DIM), jnp.float32)
        for i in range(quads):
            rows_i = slice(i * 4 * ROWS16, (i + 1) * 4 * ROWS16)
            keys_i = slice(i * HEAD_DIM, (i + 1) * HEAD_DIM)
            block, part = quad_rows(i)
            q = kv[QUERY_ITEM, block, h // 2, h % 2, part, :]
            s = dot_t(q, fk_s[keys_i, cols]) + bias[rows_i, :]
            m = jnp.max(s, axis=1, keepdims=True)
            w = jnp.exp2((s - m) * RATE)
            total = jnp.sum(w, axis=1, keepdims=True)
            o_ref[at, rows_i, :] = dot_n(w.astype(jnp.bfloat16), fv_s[keys_i, cols]).astype(
                jnp.bfloat16
            )
            stats = jnp.where(lane == i, m, stats)
            stats = jnp.where(lane == quads + i, total, stats)
        s_ref[at] = stats

    def arrivals_partial():
        stage_d(QUERY_ITEM)
        big[3].wait()
        big[4].wait()

        def one(k, c):
            h = (t + k) % n_tp
            partial_head(h, po, ps, h)
            po_copy(h, k).start()
            ps_copy(h, k).start()
            return c

        lax.fori_loop(1, n_tp, one, 0)
        partial_head(t, ro, rs, t)

    def ret_copy(k):
        peer = (g + k) % n_groups
        return pltpu.make_async_remote_copy(
            src_ref=ret.at[peer],
            dst_ref=ao.at[g],
            send_sem=b_send.at[k],
            recv_sem=b_recv.at[g],
            device_id={"group": peer},
            device_id_type=MESH,
        )

    def ret_wait(k):
        peer = (g + k) % n_groups
        pltpu.make_async_remote_copy(
            src_ref=ao.at[peer],
            dst_ref=ao.at[peer],
            send_sem=b_send.at[k],
            recv_sem=b_recv.at[peer],
            device_id={"group": peer},
            device_id_type=MESH,
        ).wait_recv()

    def arrivals_join():
        def wait(k, c):
            po_wait(k)
            return c

        lax.fori_loop(1, n_tp, wait, 0)
        slot_rows = n_groups * CAPACITY * ROWS16
        extra = rm[:, :, ROWS16 : 2 * ROWS16, :].reshape(slot_rows, HEAD_DIM)
        new = dot_n(sel[...], extra).reshape(n_prompts, ROWS16, HEAD_DIM)
        q3 = queries_of(x, yh).astype(jnp.float32).reshape(n_prompts, ROWS16, HEAD_DIM)
        n0, n1 = new_scores(q3, (new[:, 0:1], new[:, 1:2]))
        n0 = n0.reshape(a_rows, 1)
        n1 = n1.reshape(a_rows, 1)
        ms = [
            jnp.concatenate([rs[p][:, i : i + 1] for i in range(quads)], axis=0)
            for p in range(n_tp)
        ]
        m = jnp.maximum(n0, n1)
        for mp in ms:
            m = jnp.maximum(m, mp)
        w0 = jnp.exp2((n0 - m) * RATE)
        w1 = jnp.exp2((n1 - m) * RATE)
        total = w0 + w1
        o = jnp.zeros((a_rows, HEAD_DIM), jnp.float32)
        for p in range(n_tp):
            wp = jnp.exp2((ms[p] - m) * RATE)
            lp = jnp.concatenate(
                [rs[p][:, quads + i : quads + i + 1] for i in range(quads)], axis=0
            )
            total = total + wp * lp
            o = o + wp * ro[p].astype(jnp.float32)
        w0 = w0.astype(jnp.bfloat16).astype(jnp.float32).reshape(n_prompts, ROWS16, 1)
        w1 = w1.astype(jnp.bfloat16).astype(jnp.float32).reshape(n_prompts, ROWS16, 1)
        o = o + (w0 * new[:, 2:3] + w1 * new[:, 3:4]).reshape(a_rows, HEAD_DIM)
        res = (o / total).astype(jnp.bfloat16)
        back = lax.dot_general(
            sel[...], res, (((0,), (0,)), ((), ())), preferred_element_type=jnp.float32
        )
        ret[...] = back.astype(jnp.bfloat16).reshape(n_groups, CAPACITY, ROWS16, HEAD_DIM)

        def send(k, c):
            ret_copy(k).start()
            return c

        lax.fori_loop(1, n_groups, send, 0)

    def prefill_masks():
        shape = (n_tp * rows, rows)
        key = lax.broadcasted_iota(jnp.int32, shape, 0)
        row = lax.broadcasted_iota(jnp.int32, shape, 1) + t * rows
        key_mask[...] = jnp.where(key <= row, 0.0, NEG).astype(jnp.bfloat16)
        row = lax.broadcasted_iota(jnp.int32, (rows, rows), 0)
        column = lax.broadcasted_iota(jnp.int32, (rows, rows), 1)
        eye[...] = jnp.where(row == column, 1.0, 0.0).astype(jnp.bfloat16)

    def prefill_head(h):
        vis = span_offset[0] > 0
        part = 2
        n_rows = part * rows
        n_keys = n_tp * rows
        kp = kv[h, 0].reshape(n_keys, HEAD_DIM)
        ks = jnp.concatenate([kv[h, 1].reshape(n_keys, HEAD_DIM), key_mask[...]], axis=1)
        ones = jnp.ones((n_keys, HEAD_DIM), jnp.bfloat16)
        vp = jnp.concatenate([kv[h, 2].reshape(n_keys, HEAD_DIM), ones], axis=1)
        vs = jnp.concatenate([kv[h, 3].reshape(n_keys, HEAD_DIM), ones], axis=1)
        position = lax.broadcasted_iota(jnp.int32, (n_rows, HEAD_DIM), 0) % rows + t * rows
        live = span_offset[0] + position < prompt_length[0]
        eyes = jnp.concatenate([eye[...]] * part, axis=0)

        def cols(i):
            start = h * (GROUP_SIZE * HEAD_DIM) + i * HEAD_DIM
            return pl.ds(pl.multiple_of(start, HEAD_DIM), HEAD_DIM)

        queries = [q_s[:, cols(i)] for i in range(GROUP_SIZE)]
        for j in range(GROUP_SIZE // part):
            q = jnp.concatenate(queries[j * part : (j + 1) * part], axis=0)
            sp = dot_t(q, kp)
            ss = dot_t(jnp.concatenate([q, eyes], axis=1), ks)
            mp = jnp.max(sp, axis=1, keepdims=True)
            m = jnp.max(ss, axis=1, keepdims=True)
            m = jnp.where(vis, jnp.maximum(m, mp), m)
            wp = jnp.exp2((sp - jnp.where(vis, m, -NEG)) * RATE)
            ws = jnp.exp2((ss - m) * RATE)
            o = dot_n(wp.astype(jnp.bfloat16), vp) + dot_n(ws.astype(jnp.bfloat16), vs)
            o = o[:, :HEAD_DIM] / o[:, HEAD_DIM:]
            o = jnp.where(live, o, 0.0).astype(jnp.bfloat16)
            for i in range(part):
                q_s[:, cols(j * part + i)] = o[i * rows : (i + 1) * rows]

    def head_out(h):
        width = GROUP_SIZE * HEAD_DIM
        cols = pl.ds(pl.multiple_of(h * width, width), width)
        return pltpu.make_async_copy(q_s.at[:, cols], p_out.at[:, cols], out_sem.at[h])

    prefill_masks()
    decode()
    for h in range(3):
        stage_a(h)
    stage_b(0)
    arrivals_choose()
    stage_b(1)
    stage_c(0)
    stage_a(QUERY_ITEM)
    big[2].wait()

    def turn(s, c):
        @pl.when(s + window < KV_HEADS)
        def _():
            start_item(s + window, 0)

        @pl.when(s + 3 < KV_HEADS)
        def _():
            stage_a(s + 3)

        @pl.when(s + 2 < KV_HEADS)
        def _():
            stage_b(s + 2)

        @pl.when(s + 1 < KV_HEADS)
        def _():
            stage_c(s + 1)

        @pl.when(s == 0)
        def _():
            stage_b(QUERY_ITEM)

        @pl.when(s == 1)
        def _():
            stage_c(QUERY_ITEM)

        @pl.when(s == 2)
        def _():
            arrivals_partial()

        @pl.when(s == 5)
        def _():
            arrivals_join()

        stage_d(s)
        prefill_head(s)
        head_out(s).start()
        return c

    lax.fori_loop(0, KV_HEADS, turn, 0)

    def wait_ret(k, c):
        ret_wait(k)
        return c

    lax.fori_loop(1, n_groups, wait_ret, 0)
    ao[g] = ret[g]
    a_out[...] = ao[...]

    def drain_group(k, c):
        msg_copy(k).wait_send()
        ret_copy(k).wait_send()
        return c

    def drain_tp(k, c):
        h = (t + k) % n_tp
        po_copy(h, k).wait_send()
        ps_copy(h, k).wait_send()
        return c

    def drain_out(h, c):
        head_out(h).wait()
        return c

    lax.fori_loop(1, n_groups, drain_group, 0)
    lax.fori_loop(1, n_tp, drain_tp, 0)
    lax.fori_loop(0, ITEMS, drain_item, 0)
    lax.fori_loop(0, KV_HEADS, drain_out, 0)


def to_rows(queries):
    b = queries.shape[0]
    return queries.reshape(b, STEPS, GROUP_SIZE, HEAD_DIM).transpose(0, 2, 1, 3)


def from_rows(rows, b):
    rows = rows.reshape(b, GROUP_SIZE, STEPS, HEAD_DIM).transpose(0, 2, 1, 3)
    return rows.reshape(b, STEPS, GROUP_SIZE * HEAD_DIM)


def local(
    prefill_queries,
    span_keys,
    span_values,
    prefix_keys,
    prefix_values,
    span_offsets,
    prompt_lengths,
    decode_queries,
    decode_new_keys,
    decode_new_values,
    cache_keys,
    cache_values,
    context_lengths,
    placement,
    finished_lengths,
    finished_keys,
    finished_values,
    arrival_queries,
    arrival_new_keys,
    arrival_new_values,
):
    n_groups = lax.axis_size("group")
    n_tp = lax.axis_size("tp")
    n_prompts, local_len, width = finished_keys.shape
    rows = prefill_queries.shape[0]
    dec = decode_queries.shape[0]
    slots = arrival_queries.shape[0]
    dq = to_rows(decode_queries).reshape(dec * ROWS16, HEAD_DIM)
    arrival_rows = to_rows(arrival_queries).reshape(n_groups, CAPACITY, ROWS16, HEAD_DIM)
    lanes = min(128, placement.shape[0])
    any_ = pl.BlockSpec(memory_space=pl.ANY)
    vmem = pl.BlockSpec(memory_space=pltpu.VMEM)
    smem = pl.BlockSpec(memory_space=pltpu.SMEM)
    bf, f32 = jnp.bfloat16, jnp.float32
    a_rows = n_prompts * ROWS16
    dma = pltpu.SemaphoreType.DMA
    p_out, d_out, a_out = pl.pallas_call(
        functools.partial(body, n_groups, n_tp),
        out_shape=(
            jax.ShapeDtypeStruct(prefill_queries.shape, bf),
            jax.ShapeDtypeStruct(dq.shape, bf),
            jax.ShapeDtypeStruct((n_groups, CAPACITY, ROWS16, HEAD_DIM), bf),
        ),
        in_specs=[any_] * 5
        + [smem] * 2
        + [vmem] * 3
        + [any_] * 2
        + [vmem] * 3
        + [any_] * 2
        + [vmem] * 3,
        out_specs=[any_, vmem, vmem],
        scratch_shapes=[
            pltpu.VMEM((ITEMS, 4, X_CHIPS, 2, rows, HEAD_DIM), bf),
            pltpu.VMEM(prefill_queries.shape, bf),
            pltpu.VMEM(cache_keys.shape, bf),
            pltpu.VMEM(cache_values.shape, bf),
            pltpu.VMEM((n_prompts * local_len, width), bf),
            pltpu.VMEM((n_prompts * local_len, width), bf),
            pltpu.VMEM((ITEMS, 2, 2, X_CHIPS, rows, HEAD_DIM), bf),
            pltpu.VMEM((n_groups, CAPACITY, 2 * ROWS16, HEAD_DIM), bf),
            pltpu.VMEM((n_groups, CAPACITY, 2 * ROWS16, HEAD_DIM), bf),
            pltpu.VMEM((n_tp, a_rows, HEAD_DIM), bf),
            pltpu.VMEM((n_tp, a_rows, HEAD_DIM), bf),
            pltpu.VMEM((n_tp, 4 * ROWS16, HEAD_DIM), f32),
            pltpu.VMEM((n_tp, 4 * ROWS16, HEAD_DIM), f32),
            pltpu.VMEM((a_rows, slots * ROWS16), bf),
            pltpu.VMEM((a_rows, HEAD_DIM), f32),
            pltpu.VMEM((n_tp * rows, rows), bf),
            pltpu.VMEM((rows, rows), bf),
            pltpu.VMEM((n_groups, CAPACITY, ROWS16, HEAD_DIM), bf),
            pltpu.VMEM((n_groups, CAPACITY, ROWS16, HEAD_DIM), bf),
            dma((KV_HEADS, 4)),
            dma((5,)),
            dma((ITEMS, 10)),
            dma((ITEMS, 10)),
            dma((n_groups,)),
            dma((n_groups,)),
            dma((n_tp,)),
            dma((n_tp,)),
            dma((n_tp,)),
            dma((n_tp,)),
            dma((n_groups,)),
            dma((n_groups,)),
            dma((KV_HEADS,)),
        ],
        compiler_params=pltpu.CompilerParams(
            collective_id=0, has_side_effects=True, vmem_limit_bytes=56 * 1024 * 1024
        ),
    )(
        prefill_queries,
        span_keys,
        span_values,
        prefix_keys,
        prefix_values,
        span_offsets,
        prompt_lengths,
        dq,
        decode_new_keys,
        decode_new_values,
        cache_keys,
        cache_values,
        context_lengths[None, :],
        placement.reshape(-1, lanes),
        finished_lengths.reshape(-1, lanes),
        finished_keys.reshape(n_prompts * local_len, width),
        finished_values.reshape(n_prompts * local_len, width),
        arrival_rows,
        arrival_new_keys,
        arrival_new_values,
    )
    return (p_out, from_rows(d_out, dec), from_rows(a_out, slots))


def solution(mesh):
    both = P(("group", "tp"), None)
    heads = P("group", None, "tp")
    placed = (
        (both,) * 5
        + (P("group"),) * 2
        + (heads,) * 5
        + (P("group"), P(), P())
        + (P("group", "tp", None),) * 2
        + (heads,) * 3
    )
    return jax.shard_map(
        local,
        mesh=mesh,
        in_specs=placed,
        out_specs=(both, heads, heads),
        check_vma=False,
    )
```

```python
import functools
import math

import jax
import jax.numpy as jnp
from jax import lax
from jax.experimental import pallas as pl
from jax.experimental.pallas import tpu as pltpu
from jax.sharding import PartitionSpec as P

KV_HEADS = 8
GROUP_SIZE = 8
HEAD_DIM = 128
CAPACITY = 2
STEPS = 2
ROWS16 = GROUP_SIZE * STEPS
MESH = pl.DeviceIdType.MESH
NEG = -1e30
RATE = math.log2(math.e) / math.sqrt(HEAD_DIM)
X_CHIPS = 4
CORES = 2
STAT_LANES = 16
ITEMS = KV_HEADS + 1
QUERY_ITEM = KV_HEADS


def dot_t(a, b):
    return lax.dot_general(a, b, (((1,), (1,)), ((), ())), preferred_element_type=jnp.float32)


def dot_n(a, b):
    return lax.dot_general(a, b, (((1,), (0,)), ((), ())), preferred_element_type=jnp.float32)


def spread(row, count, reps, base):
    shape = (count * reps, row.shape[1])
    owner = lax.broadcasted_iota(jnp.int32, shape, 0) // reps + base
    lane = lax.broadcasted_iota(jnp.int32, shape, 1)
    return jnp.sum(jnp.where(owner == lane, row, 0.0), axis=1, keepdims=True)


def new_scores(q3, nk):
    shape = q3.shape[:2] + (1,)
    step = lax.broadcasted_iota(jnp.int32, shape, 1) % STEPS
    first = jnp.sum(q3 * nk[0], axis=2, keepdims=True)
    second = jnp.sum(q3 * nk[1], axis=2, keepdims=True)
    return first, jnp.where(step >= 1, second, NEG)


def body(
    n_groups,
    n_tp,
    pq,
    sk,
    sv,
    pk,
    pv,
    span_offset,
    prompt_length,
    dq,
    dnk,
    dnv,
    ck,
    cv,
    context,
    routes,
    lengths,
    fk,
    fv,
    arrival_q,
    ank,
    anv,
    p_out,
    d_out,
    a_out,
    kv,
    q_s,
    ck_s,
    cv_s,
    fk_s,
    fv_s,
    rel,
    msg,
    rm,
    away,
    away_stats,
    home,
    home_stats,
    relayed,
    relayed_stats,
    landed,
    landed_stats,
    ro,
    rs,
    sel,
    bias,
    key_mask,
    eye,
    ret,
    ao,
    load_kv,
    load_big,
    x_send,
    x_recv,
    m_send,
    m_recv,
    p_send,
    p_recv,
    o_send,
    o_recv,
    s_send,
    s_recv,
    b_send,
    b_recv,
    out_sem,
):
    g = lax.axis_index("group")
    t = lax.axis_index("tp")
    x, yh = t // 2, t % 2
    right = ((x + 1) % X_CHIPS) * 2 + yh
    left = ((x + X_CHIPS - 1) % X_CHIPS) * 2 + yh
    partner = x * 2 + (1 - yh)
    right_x = (x + 1) % X_CHIPS
    left_x = (x + X_CHIPS - 1) % X_CHIPS
    far_x = (x + 2) % X_CHIPS
    yl = (g // CORES) % 2
    beside = g + CORES * (1 - 2 * yl)
    local_len = HEAD_DIM // 4
    n_prompts = fk_s.shape[0] // local_len
    a_rows = n_prompts * ROWS16
    quads = n_prompts // 4
    rows = pq.shape[0]

    arrays = (pk, sk, pv, sv)

    def kv_load(h, a):
        cols = pl.ds(pl.multiple_of(h * HEAD_DIM, HEAD_DIM), HEAD_DIM)
        return pltpu.make_async_copy(arrays[a].at[:, cols], kv.at[h, a, x, yh], load_kv.at[h, a])

    def start_loads(h, c):
        for a in range(4):
            kv_load(h, a).start()
        return c

    lax.fori_loop(0, KV_HEADS, start_loads, 0)
    big = [
        pltpu.make_async_copy(src, dst, load_big.at[i])
        for i, (src, dst) in enumerate(
            ((ck, ck_s), (cv, cv_s), (pq, q_s), (fk, fk_s), (fv, fv_s))
        )
    ]
    for copy in big:
        copy.start()

    barrier = pltpu.get_barrier_semaphore()

    def greet_group(k, c):
        pl.semaphore_signal(
            barrier, inc=1, device_id={"group": (g + k) % n_groups}, device_id_type=MESH
        )
        return c

    def greet_tp(k, c):
        pl.semaphore_signal(barrier, inc=1, device_id={"tp": (t + k) % n_tp}, device_id_type=MESH)
        return c

    lax.fori_loop(1, n_groups, greet_group, 0)
    lax.fori_loop(1, n_tp, greet_tp, 0)
    pl.semaphore_signal(
        barrier, inc=1, device_id={"group": beside, "tp": partner}, device_id_type=MESH
    )
    pl.semaphore_wait(barrier, n_groups - 1 + n_tp - 1 + 1)

    to_right, to_left = {"tp": right}, {"tp": left}
    to_same, to_cross = {"group": beside}, {"group": beside, "tp": partner}
    ny = 1 - yh

    def y_first(i):
        return i % 3 != 1

    def hop(src, dst, kind, i, device):
        return pltpu.make_async_remote_copy(
            src_ref=src,
            dst_ref=dst,
            send_sem=x_send.at[i, kind],
            recv_sem=x_recv.at[i, kind],
            device_id=device,
            device_id_type=MESH,
        )

    def same(ref, kind, i, device):
        return hop(ref, ref, kind, i, device)

    keys, values = pl.ds(0, 2), pl.ds(2, 2)

    def own_right(i, xs):
        return same(kv.at[i, :, xs, yh], 0, i, to_right)

    def own_left(i, xs):
        return same(kv.at[i, :, xs, yh], 1, i, to_left)

    def one_y(i, part):
        rows_of = keys if part == 0 else values
        device = to_same if part == 0 else to_cross
        return hop(kv.at[i, rows_of, x, yh], rel.at[i, part, :, 0], 2 + part, i, device)

    def all_y(i, part):
        rows_of = keys if part == 0 else values
        device = to_same if part == 0 else to_cross
        return hop(kv.at[i, rows_of, :, yh], rel.at[i, part], 2 + part, i, device)

    def one_relay(i, part):
        if part == 0:
            return hop(rel.at[i, 0, :, 0], kv.at[i, keys, x, yh], 4, i, to_cross)
        return hop(rel.at[i, 1, :, 0], kv.at[i, values, x, ny], 5, i, to_same)

    def all_relay(i, part):
        if part == 0:
            return hop(rel.at[i, 0], kv.at[i, keys, :, yh], 4, i, to_cross)
        return hop(rel.at[i, 1], kv.at[i, values, :, ny], 5, i, to_same)

    def one_landed(i, part):
        return same(kv.at[i, (keys, values)[part], x, ny], 4 + part, i, to_same)

    def all_landed(i, part):
        return same(kv.at[i, (keys, values)[part], :, ny], 4 + part, i, to_same)

    def partner_right(i, xs):
        return same(kv.at[i, :, xs, ny], 6, i, to_right)

    def partner_left(i, xs):
        return same(kv.at[i, :, xs, ny], 7, i, to_left)

    def pair_right(i, xs):
        return same(kv.at[i, keys, xs], 8, i, to_right)

    def pair_left(i, xs):
        return same(kv.at[i, values, xs], 9, i, to_left)

    def single_right(i, xs):
        return same(kv.at[i, keys, xs, yh], 8, i, to_right)

    def single_left(i, xs):
        return same(kv.at[i, values, xs, yh], 9, i, to_left)

    def by_kind(i, first, second):
        pl.when(y_first(i))(lambda: first(i))
        pl.when(jnp.logical_not(y_first(i)))(lambda: second(i))

    def stage1(i):
        @pl.when(y_first(i))
        def _():
            one_y(i, 0).start()
            one_y(i, 1).start()

        own_right(i, x).start()
        own_left(i, x).start()

    def first_a(i):
        for part in range(2):
            one_y(i, part).wait_recv()
            one_relay(i, part).start()

    def first_b(i):
        one_landed(i, 0).wait_recv()
        one_landed(i, 1).wait_recv()
        partner_right(i, x).start()
        partner_left(i, x).start()

    def first_c(i):
        own_right(i, left_x).wait_recv()
        partner_right(i, left_x).wait_recv()
        pair_right(i, left_x).start()
        own_left(i, right_x).wait_recv()
        partner_left(i, right_x).wait_recv()
        pair_left(i, right_x).start()

    def first_d(i):
        pair_right(i, far_x).wait_recv()
        pair_left(i, far_x).wait_recv()

    def second_a(i):
        own_right(i, left_x).wait_recv()
        single_right(i, left_x).start()
        own_left(i, right_x).wait_recv()
        single_left(i, right_x).start()

    def second_b(i):
        single_right(i, far_x).wait_recv()
        single_left(i, far_x).wait_recv()
        all_y(i, 0).start()
        all_y(i, 1).start()

    def second_c(i):
        for part in range(2):
            all_y(i, part).wait_recv()
            all_relay(i, part).start()

    def second_d(i):
        all_landed(i, 0).wait_recv()
        all_landed(i, 1).wait_recv()

    def stage_a(i):
        by_kind(i, first_a, second_a)

    def stage_b(i):
        by_kind(i, first_b, second_b)

    def stage_c(i):
        by_kind(i, first_c, second_c)

    def stage_d(i):
        by_kind(i, first_d, second_d)

    def first_drain(i):
        for part in range(2):
            one_y(i, part).wait_send()
            one_relay(i, part).wait_send()
        partner_right(i, x).wait_send()
        partner_left(i, x).wait_send()
        pair_right(i, left_x).wait_send()
        pair_left(i, right_x).wait_send()

    def second_drain(i):
        for part in range(2):
            all_y(i, part).wait_send()
            all_relay(i, part).wait_send()
        single_right(i, left_x).wait_send()
        single_left(i, right_x).wait_send()

    def drain_item(i, c):
        own_right(i, x).wait_send()
        own_left(i, x).wait_send()
        by_kind(i, first_drain, second_drain)
        return c

    def start_item(i, c):
        for a in range(4):
            kv_load(i, a).wait()
        stage1(i)
        return c

    window = 4
    lax.fori_loop(0, window, start_item, 0)

    def msg_copy(k):
        peer = (g + k) % n_groups
        return pltpu.make_async_remote_copy(
            src_ref=msg.at[peer],
            dst_ref=rm.at[g],
            send_sem=m_send.at[k],
            recv_sem=m_recv.at[g],
            device_id={"group": peer},
            device_id_type=MESH,
        )

    def msg_wait(k):
        peer = (g + k) % n_groups
        pltpu.make_async_remote_copy(
            src_ref=rm.at[peer],
            dst_ref=rm.at[peer],
            send_sem=m_send.at[k],
            recv_sem=m_recv.at[peer],
            device_id={"group": peer},
            device_id_type=MESH,
        ).wait_recv()

    def send_msg(k, c):
        msg_copy(k).start()
        return c

    def wait_msg(k, c):
        msg_wait(k)
        return c

    pair = (n_groups, CAPACITY, ROWS16, HEAD_DIM)
    row_id = lax.broadcasted_iota(jnp.int32, (1, ROWS16, 1), 1)
    extra = jnp.zeros((n_groups * CAPACITY, ROWS16, HEAD_DIM), jnp.float32)
    for step in range(STEPS):
        nk = ank[...].astype(jnp.float32)[:, step : step + 1]
        nv = anv[...].astype(jnp.float32)[:, step : step + 1]
        extra = jnp.where(row_id == step, nk, jnp.where(row_id == STEPS + step, nv, extra))
    msg[:, :, 0:ROWS16, :] = arrival_q[...]
    msg[:, :, ROWS16 : 2 * ROWS16, :] = extra.astype(jnp.bfloat16).reshape(pair)
    lax.fori_loop(1, n_groups, send_msg, 0)
    rm[g] = msg[g]

    def decode():
        big[0].wait()
        big[1].wait()
        b = dnk.shape[0]
        q = dq[...].reshape(b, ROWS16, HEAD_DIM)
        s = lax.dot_general(
            q, ck_s[...], (((2,), (2,)), ((0,), (0,))), preferred_element_type=jnp.float32
        )
        limit = spread(context[...].astype(jnp.float32), b, ROWS16, 0).reshape(b, ROWS16, 1)
        slot = lax.broadcasted_iota(jnp.int32, s.shape, 2).astype(jnp.float32)
        s = jnp.where(slot < limit, s, NEG)
        nk = dnk[...].astype(jnp.float32)
        nv = dnv[...].astype(jnp.float32)
        n0, n1 = new_scores(q.astype(jnp.float32), (nk[:, 0:1], nk[:, 1:2]))
        m = jnp.maximum(jnp.max(s, axis=2, keepdims=True), jnp.maximum(n0, n1))
        w = jnp.exp2((s - m) * RATE)
        w0 = jnp.exp2((n0 - m) * RATE)
        w1 = jnp.exp2((n1 - m) * RATE)
        total = jnp.sum(w, axis=2, keepdims=True) + w0 + w1
        o = lax.dot_general(
            w.astype(jnp.bfloat16),
            cv_s[...],
            (((2,), (1,)), ((0,), (0,))),
            preferred_element_type=jnp.float32,
        )
        o = o + w0.astype(jnp.bfloat16).astype(jnp.float32) * nv[:, 0:1]
        o = o + w1.astype(jnp.bfloat16).astype(jnp.float32) * nv[:, 1:2]
        d_out[...] = (o / total).reshape(b * ROWS16, HEAD_DIM).astype(jnp.bfloat16)

    def quad_rows(i):
        half = i % 2 * (4 * ROWS16)
        return i // 2, slice(half, half + 4 * ROWS16)

    def queries_of(xs, ys):
        parts = []
        for i in range(quads):
            block, part = quad_rows(i)
            parts.append(kv[QUERY_ITEM, block, xs, ys, part, :])
        return jnp.concatenate(parts, axis=0)

    def arrivals_choose():
        lax.fori_loop(1, n_groups, wait_msg, 0)
        lanes = routes.shape[1]
        per_row = lanes // n_prompts
        base = g % per_row * n_prompts
        own = routes[pl.ds(g // per_row, 1), :].astype(jnp.float32)
        dest = spread(own, n_prompts, ROWS16, base)
        owner = lax.broadcasted_iota(jnp.int32, (a_rows, lanes), 0) // ROWS16
        other = lax.broadcasted_iota(jnp.int32, (a_rows, lanes), 1) - base
        rank = jnp.sum(
            jnp.where((dest == own) & (other >= 0) & (other < owner), 1.0, 0.0),
            axis=1,
            keepdims=True,
        )
        within = lax.broadcasted_iota(jnp.int32, (a_rows, 1), 0) % ROWS16
        target = (dest * CAPACITY + rank) * ROWS16 + within.astype(jnp.float32)
        slot_rows = n_groups * CAPACITY * ROWS16
        column = lax.broadcasted_iota(jnp.int32, (a_rows, slot_rows), 1).astype(jnp.float32)
        sel[...] = jnp.where(column == target, 1.0, 0.0).astype(jnp.bfloat16)
        got = rm[:, :, 0:ROWS16, :].reshape(slot_rows, HEAD_DIM)
        chosen = dot_n(sel[...], got).astype(jnp.bfloat16)
        for i in range(quads):
            block, part = quad_rows(i)
            kv[QUERY_ITEM, block, x, yh, part, :] = chosen[i * 4 * ROWS16 : (i + 1) * 4 * ROWS16]
        stage1(QUERY_ITEM)
        own_len = lengths[pl.ds(g // per_row, 1), :].astype(jnp.float32)
        limit = spread(own_len, n_prompts, ROWS16, base) - (t * local_len).astype(jnp.float32)
        col = lax.broadcasted_iota(jnp.int32, (a_rows, HEAD_DIM), 1)
        quad_row = (lax.broadcasted_iota(jnp.int32, (a_rows, HEAD_DIM), 0) // ROWS16) % 4
        keep = (col // local_len == quad_row) & ((col % local_len).astype(jnp.float32) < limit)
        bias[...] = jnp.where(keep, 0.0, NEG)

    def part_hop(src, dst, kind, device):
        return pltpu.make_async_remote_copy(
            src_ref=src,
            dst_ref=dst,
            send_sem=p_send.at[kind],
            recv_sem=p_recv.at[kind],
            device_id=device,
            device_id_type=MESH,
        )

    low, high = pl.ds(0, 2), pl.ds(2, 2)

    def part_y():
        return (
            part_hop(away.at[low], relayed.at[low], 0, to_same),
            part_hop(away.at[high], relayed.at[high], 1, to_cross),
            part_hop(away_stats, relayed_stats, 2, to_cross),
        )

    def part_relay():
        return (
            part_hop(relayed.at[low], landed.at[low], 3, to_cross),
            part_hop(relayed.at[high], landed.at[high], 4, to_same),
            part_hop(relayed_stats, landed_stats, 5, to_same),
        )

    def x_peer(k):
        return (x + k) % X_CHIPS

    def part_x(k):
        xs = x_peer(k)
        device = {"tp": xs * 2 + yh}
        out = []
        for src, dst, send, recv in (
            (home, ro, o_send, o_recv),
            (home_stats, rs, s_send, s_recv),
        ):
            out.append(
                pltpu.make_async_remote_copy(
                    src_ref=src.at[xs],
                    dst_ref=dst.at[x],
                    send_sem=send.at[k],
                    recv_sem=recv.at[x],
                    device_id=device,
                    device_id_type=MESH,
                )
            )
        return out

    def part_x_wait(k):
        xs = x_peer(k)
        for ref, send, recv in ((ro, o_send, o_recv), (rs, s_send, s_recv)):
            pltpu.make_async_remote_copy(
                src_ref=ref.at[xs],
                dst_ref=ref.at[xs],
                send_sem=send.at[k],
                recv_sem=recv.at[xs],
                device_id={"tp": xs * 2 + yh},
                device_id_type=MESH,
            ).wait_recv()

    stat_lane = lax.broadcasted_iota(jnp.int32, (4 * ROWS16, HEAD_DIM), 1)

    def partial_heads(ys, o_ref):
        def one(xs, stats):
            h = xs * 2 + ys
            cols = pl.ds(pl.multiple_of(h * HEAD_DIM, HEAD_DIM), HEAD_DIM)
            for i in range(quads):
                rows_i = slice(i * 4 * ROWS16, (i + 1) * 4 * ROWS16)
                keys_i = slice(i * HEAD_DIM, (i + 1) * HEAD_DIM)
                block, part = quad_rows(i)
                q = kv[QUERY_ITEM, block, xs, ys, part, :]
                s = dot_t(q, fk_s[keys_i, cols]) + bias[rows_i, :]
                m = jnp.max(s, axis=1, keepdims=True)
                w = jnp.exp2((s - m) * RATE)
                total = jnp.sum(w, axis=1, keepdims=True)
                o_ref[xs, rows_i, :] = dot_n(w.astype(jnp.bfloat16), fv_s[keys_i, cols]).astype(
                    jnp.bfloat16
                )
                at = xs * STAT_LANES + i
                stats = jnp.where(stat_lane == at, m, stats)
                stats = jnp.where(stat_lane == at + STAT_LANES // 2, total, stats)
            return stats

        return lax.fori_loop(
            0, X_CHIPS, one, jnp.zeros((4 * ROWS16, HEAD_DIM), jnp.float32)
        )

    def arrivals_partial():
        stage_d(QUERY_ITEM)
        big[3].wait()
        big[4].wait()
        away_stats[...] = partial_heads(ny, away)
        for copy in part_y():
            copy.start()
        home_stats[0] = partial_heads(yh, home)

    def arrivals_relay():
        for here, onward in zip(part_y(), part_relay()):
            here.wait_recv()
            onward.start()

    def arrivals_pair():
        for copy in part_relay():
            copy.wait_recv()
        mine = home_stats[0]
        other = landed_stats[...]
        m = jnp.maximum(mine, other)
        w_mine = jnp.exp2((mine - m) * RATE)
        w_other = jnp.exp2((other - m) * RATE)
        half = STAT_LANES // 2
        total = pltpu.roll(w_mine, half, 1) * mine + pltpu.roll(w_other, half, 1) * other
        stats = jnp.where(stat_lane % STAT_LANES < half, m, total)
        for xs in range(X_CHIPS):
            for i in range(quads):
                rows_i = slice(i * 4 * ROWS16, (i + 1) * 4 * ROWS16)
                at = xs * STAT_LANES + i
                o = home[xs, rows_i, :].astype(jnp.float32) * w_mine[:, at : at + 1]
                o = o + landed[xs, rows_i, :].astype(jnp.float32) * w_other[:, at : at + 1]
                home[xs, rows_i, :] = o.astype(jnp.bfloat16)
            shift = (HEAD_DIM - xs * STAT_LANES) % HEAD_DIM
            home_stats[xs] = stats if shift == 0 else pltpu.roll(stats, shift, 1)
        for k in range(1, X_CHIPS):
            for copy in part_x(k):
                copy.start()
        ro[x] = home[x]
        rs[x] = home_stats[x]

    def ret_copy(k):
        peer = (g + k) % n_groups
        return pltpu.make_async_remote_copy(
            src_ref=ret.at[peer],
            dst_ref=ao.at[g],
            send_sem=b_send.at[k],
            recv_sem=b_recv.at[g],
            device_id={"group": peer},
            device_id_type=MESH,
        )

    def ret_wait(k):
        peer = (g + k) % n_groups
        pltpu.make_async_remote_copy(
            src_ref=ao.at[peer],
            dst_ref=ao.at[peer],
            send_sem=b_send.at[k],
            recv_sem=b_recv.at[peer],
            device_id={"group": peer},
            device_id_type=MESH,
        ).wait_recv()

    def arrivals_join():
        for k in range(1, X_CHIPS):
            part_x_wait(k)
        slot_rows = n_groups * CAPACITY * ROWS16
        extra = rm[:, :, ROWS16 : 2 * ROWS16, :].reshape(slot_rows, HEAD_DIM)
        new = dot_n(sel[...], extra).reshape(n_prompts, ROWS16, HEAD_DIM)
        q3 = queries_of(x, yh).astype(jnp.float32).reshape(n_prompts, ROWS16, HEAD_DIM)
        n0, n1 = new_scores(q3, (new[:, 0:1], new[:, 1:2]))
        n0 = n0.reshape(a_rows, 1)
        n1 = n1.reshape(a_rows, 1)
        ms = [
            jnp.concatenate([rs[p][:, i : i + 1] for i in range(quads)], axis=0)
            for p in range(X_CHIPS)
        ]
        half = STAT_LANES // 2
        m = jnp.maximum(n0, n1)
        for mp in ms:
            m = jnp.maximum(m, mp)
        w0 = jnp.exp2((n0 - m) * RATE)
        w1 = jnp.exp2((n1 - m) * RATE)
        total = w0 + w1
        o = jnp.zeros((a_rows, HEAD_DIM), jnp.float32)
        for p in range(X_CHIPS):
            wp = jnp.exp2((ms[p] - m) * RATE)
            lp = jnp.concatenate(
                [rs[p][:, half + i : half + i + 1] for i in range(quads)], axis=0
            )
            total = total + wp * lp
            o = o + wp * ro[p].astype(jnp.float32)
        w0 = w0.astype(jnp.bfloat16).astype(jnp.float32).reshape(n_prompts, ROWS16, 1)
        w1 = w1.astype(jnp.bfloat16).astype(jnp.float32).reshape(n_prompts, ROWS16, 1)
        o = o + (w0 * new[:, 2:3] + w1 * new[:, 3:4]).reshape(a_rows, HEAD_DIM)
        res = (o / total).astype(jnp.bfloat16)
        back = lax.dot_general(
            sel[...], res, (((0,), (0,)), ((), ())), preferred_element_type=jnp.float32
        )
        ret[...] = back.astype(jnp.bfloat16).reshape(n_groups, CAPACITY, ROWS16, HEAD_DIM)

        def send(k, c):
            ret_copy(k).start()
            return c

        lax.fori_loop(1, n_groups, send, 0)

    def prefill_masks():
        shape = (n_tp * rows, rows)
        key = lax.broadcasted_iota(jnp.int32, shape, 0)
        row = lax.broadcasted_iota(jnp.int32, shape, 1) + t * rows
        key_mask[...] = jnp.where(key <= row, 0.0, NEG).astype(jnp.bfloat16)
        row = lax.broadcasted_iota(jnp.int32, (rows, rows), 0)
        column = lax.broadcasted_iota(jnp.int32, (rows, rows), 1)
        eye[...] = jnp.where(row == column, 1.0, 0.0).astype(jnp.bfloat16)

    def prefill_head(h):
        vis = span_offset[0] > 0
        part = 2
        n_rows = part * rows
        n_keys = n_tp * rows
        kp = kv[h, 0].reshape(n_keys, HEAD_DIM)
        ks = jnp.concatenate([kv[h, 1].reshape(n_keys, HEAD_DIM), key_mask[...]], axis=1)
        ones = jnp.ones((n_keys, HEAD_DIM), jnp.bfloat16)
        vp = jnp.concatenate([kv[h, 2].reshape(n_keys, HEAD_DIM), ones], axis=1)
        vs = jnp.concatenate([kv[h, 3].reshape(n_keys, HEAD_DIM), ones], axis=1)
        position = lax.broadcasted_iota(jnp.int32, (n_rows, HEAD_DIM), 0) % rows + t * rows
        live = span_offset[0] + position < prompt_length[0]
        eyes = jnp.concatenate([eye[...]] * part, axis=0)

        def cols(i):
            start = h * (GROUP_SIZE * HEAD_DIM) + i * HEAD_DIM
            return pl.ds(pl.multiple_of(start, HEAD_DIM), HEAD_DIM)

        queries = [q_s[:, cols(i)] for i in range(GROUP_SIZE)]
        for j in range(GROUP_SIZE // part):
            q = jnp.concatenate(queries[j * part : (j + 1) * part], axis=0)
            sp = dot_t(q, kp)
            ss = dot_t(jnp.concatenate([q, eyes], axis=1), ks)
            mp = jnp.max(sp, axis=1, keepdims=True)
            m = jnp.max(ss, axis=1, keepdims=True)
            m = jnp.where(vis, jnp.maximum(m, mp), m)
            wp = jnp.exp2((sp - jnp.where(vis, m, -NEG)) * RATE)
            ws = jnp.exp2((ss - m) * RATE)
            o = dot_n(wp.astype(jnp.bfloat16), vp) + dot_n(ws.astype(jnp.bfloat16), vs)
            o = o[:, :HEAD_DIM] / o[:, HEAD_DIM:]
            o = jnp.where(live, o, 0.0).astype(jnp.bfloat16)
            for i in range(part):
                q_s[:, cols(j * part + i)] = o[i * rows : (i + 1) * rows]

    def head_out(h):
        width = GROUP_SIZE * HEAD_DIM
        cols = pl.ds(pl.multiple_of(h * width, width), width)
        return pltpu.make_async_copy(q_s.at[:, cols], p_out.at[:, cols], out_sem.at[h])

    prefill_masks()
    decode()
    for h in range(3):
        stage_a(h)
    stage_b(0)
    arrivals_choose()
    stage_b(1)
    stage_c(0)
    stage_a(QUERY_ITEM)
    big[2].wait()

    def turn(s, c):
        @pl.when(s + window < KV_HEADS)
        def _():
            start_item(s + window, 0)

        @pl.when(s + 3 < KV_HEADS)
        def _():
            stage_a(s + 3)

        @pl.when(s + 2 < KV_HEADS)
        def _():
            stage_b(s + 2)

        @pl.when(s + 1 < KV_HEADS)
        def _():
            stage_c(s + 1)

        @pl.when(s == 0)
        def _():
            stage_b(QUERY_ITEM)

        @pl.when(s == 1)
        def _():
            stage_c(QUERY_ITEM)

        @pl.when(s == 2)
        def _():
            arrivals_partial()

        @pl.when(s == 3)
        def _():
            arrivals_relay()

        @pl.when(s == 4)
        def _():
            arrivals_pair()

        @pl.when(s == 6)
        def _():
            arrivals_join()

        stage_d(s)
        prefill_head(s)
        head_out(s).start()
        return c

    lax.fori_loop(0, KV_HEADS, turn, 0)

    def wait_ret(k, c):
        ret_wait(k)
        return c

    lax.fori_loop(1, n_groups, wait_ret, 0)
    ao[g] = ret[g]
    a_out[...] = ao[...]

    def drain_group(k, c):
        msg_copy(k).wait_send()
        ret_copy(k).wait_send()
        return c

    def drain_out(h, c):
        head_out(h).wait()
        return c

    lax.fori_loop(1, n_groups, drain_group, 0)
    for copy in part_y() + part_relay():
        copy.wait_send()
    for k in range(1, X_CHIPS):
        for copy in part_x(k):
            copy.wait_send()
    lax.fori_loop(0, ITEMS, drain_item, 0)
    lax.fori_loop(0, KV_HEADS, drain_out, 0)


def to_rows(queries):
    b = queries.shape[0]
    return queries.reshape(b, STEPS, GROUP_SIZE, HEAD_DIM).transpose(0, 2, 1, 3)


def from_rows(rows, b):
    rows = rows.reshape(b, GROUP_SIZE, STEPS, HEAD_DIM).transpose(0, 2, 1, 3)
    return rows.reshape(b, STEPS, GROUP_SIZE * HEAD_DIM)


def local(
    prefill_queries,
    span_keys,
    span_values,
    prefix_keys,
    prefix_values,
    span_offsets,
    prompt_lengths,
    decode_queries,
    decode_new_keys,
    decode_new_values,
    cache_keys,
    cache_values,
    context_lengths,
    placement,
    finished_lengths,
    finished_keys,
    finished_values,
    arrival_queries,
    arrival_new_keys,
    arrival_new_values,
):
    n_groups = lax.axis_size("group")
    n_tp = lax.axis_size("tp")
    n_prompts, local_len, width = finished_keys.shape
    rows = prefill_queries.shape[0]
    dec = decode_queries.shape[0]
    slots = arrival_queries.shape[0]
    dq = to_rows(decode_queries).reshape(dec * ROWS16, HEAD_DIM)
    arrival_rows = to_rows(arrival_queries).reshape(n_groups, CAPACITY, ROWS16, HEAD_DIM)
    lanes = min(128, placement.shape[0])
    any_ = pl.BlockSpec(memory_space=pl.ANY)
    vmem = pl.BlockSpec(memory_space=pltpu.VMEM)
    smem = pl.BlockSpec(memory_space=pltpu.SMEM)
    bf, f32 = jnp.bfloat16, jnp.float32
    a_rows = n_prompts * ROWS16
    dma = pltpu.SemaphoreType.DMA
    p_out, d_out, a_out = pl.pallas_call(
        functools.partial(body, n_groups, n_tp),
        out_shape=(
            jax.ShapeDtypeStruct(prefill_queries.shape, bf),
            jax.ShapeDtypeStruct(dq.shape, bf),
            jax.ShapeDtypeStruct((n_groups, CAPACITY, ROWS16, HEAD_DIM), bf),
        ),
        in_specs=[any_] * 5
        + [smem] * 2
        + [vmem] * 3
        + [any_] * 2
        + [vmem] * 3
        + [any_] * 2
        + [vmem] * 3,
        out_specs=[any_, vmem, vmem],
        scratch_shapes=[
            pltpu.VMEM((ITEMS, 4, X_CHIPS, 2, rows, HEAD_DIM), bf),
            pltpu.VMEM(prefill_queries.shape, bf),
            pltpu.VMEM(cache_keys.shape, bf),
            pltpu.VMEM(cache_values.shape, bf),
            pltpu.VMEM((n_prompts * local_len, width), bf),
            pltpu.VMEM((n_prompts * local_len, width), bf),
            pltpu.VMEM((ITEMS, 2, 2, X_CHIPS, rows, HEAD_DIM), bf),
            pltpu.VMEM((n_groups, CAPACITY, 2 * ROWS16, HEAD_DIM), bf),
            pltpu.VMEM((n_groups, CAPACITY, 2 * ROWS16, HEAD_DIM), bf),
            pltpu.VMEM((X_CHIPS, a_rows, HEAD_DIM), bf),
            pltpu.VMEM((4 * ROWS16, HEAD_DIM), f32),
            pltpu.VMEM((X_CHIPS, a_rows, HEAD_DIM), bf),
            pltpu.VMEM((X_CHIPS, 4 * ROWS16, HEAD_DIM), f32),
            pltpu.VMEM((X_CHIPS, a_rows, HEAD_DIM), bf),
            pltpu.VMEM((4 * ROWS16, HEAD_DIM), f32),
            pltpu.VMEM((X_CHIPS, a_rows, HEAD_DIM), bf),
            pltpu.VMEM((4 * ROWS16, HEAD_DIM), f32),
            pltpu.VMEM((X_CHIPS, a_rows, HEAD_DIM), bf),
            pltpu.VMEM((X_CHIPS, 4 * ROWS16, HEAD_DIM), f32),
            pltpu.VMEM((a_rows, slots * ROWS16), bf),
            pltpu.VMEM((a_rows, HEAD_DIM), f32),
            pltpu.VMEM((n_tp * rows, rows), bf),
            pltpu.VMEM((rows, rows), bf),
            pltpu.VMEM((n_groups, CAPACITY, ROWS16, HEAD_DIM), bf),
            pltpu.VMEM((n_groups, CAPACITY, ROWS16, HEAD_DIM), bf),
            dma((KV_HEADS, 4)),
            dma((5,)),
            dma((ITEMS, 10)),
            dma((ITEMS, 10)),
            dma((n_groups,)),
            dma((n_groups,)),
            dma((6,)),
            dma((6,)),
            dma((X_CHIPS,)),
            dma((X_CHIPS,)),
            dma((X_CHIPS,)),
            dma((X_CHIPS,)),
            dma((n_groups,)),
            dma((n_groups,)),
            dma((KV_HEADS,)),
        ],
        compiler_params=pltpu.CompilerParams(
            collective_id=0, has_side_effects=True, vmem_limit_bytes=56 * 1024 * 1024
        ),
    )(
        prefill_queries,
        span_keys,
        span_values,
        prefix_keys,
        prefix_values,
        span_offsets,
        prompt_lengths,
        dq,
        decode_new_keys,
        decode_new_values,
        cache_keys,
        cache_values,
        context_lengths[None, :],
        placement.reshape(-1, lanes),
        finished_lengths.reshape(-1, lanes),
        finished_keys.reshape(n_prompts * local_len, width),
        finished_values.reshape(n_prompts * local_len, width),
        arrival_rows,
        arrival_new_keys,
        arrival_new_values,
    )
    return (p_out, from_rows(d_out, dec), from_rows(a_out, slots))


def solution(mesh):
    both = P(("group", "tp"), None)
    heads = P("group", None, "tp")
    placed = (
        (both,) * 5
        + (P("group"),) * 2
        + (heads,) * 5
        + (P("group"), P(), P())
        + (P("group", "tp", None),) * 2
        + (heads,) * 3
    )
    return jax.shard_map(
        local,
        mesh=mesh,
        in_specs=placed,
        out_specs=(both, heads, heads),
        check_vma=False,
    )
```

```python
import functools
import math

import jax
import jax.numpy as jnp
from jax import lax
from jax.experimental import pallas as pl
from jax.experimental.pallas import tpu as pltpu
from jax.sharding import PartitionSpec as P

KV_HEADS = 8
GROUP_SIZE = 8
HEAD_DIM = 128
CAPACITY = 2
STEPS = 2
ROWS16 = GROUP_SIZE * STEPS
MESH = pl.DeviceIdType.MESH
NEG = -1e30
RATE = math.log2(math.e) / math.sqrt(HEAD_DIM)
X_CHIPS = 4
CORES = 2
ITEMS = KV_HEADS + 1
QUERY_ITEM = KV_HEADS


def dot_t(a, b):
    return lax.dot_general(a, b, (((1,), (1,)), ((), ())), preferred_element_type=jnp.float32)


def dot_n(a, b):
    return lax.dot_general(a, b, (((1,), (0,)), ((), ())), preferred_element_type=jnp.float32)


def spread(row, count, reps, base):
    shape = (count * reps, row.shape[1])
    owner = lax.broadcasted_iota(jnp.int32, shape, 0) // reps + base
    lane = lax.broadcasted_iota(jnp.int32, shape, 1)
    return jnp.sum(jnp.where(owner == lane, row, 0.0), axis=1, keepdims=True)


def new_scores(q3, nk):
    shape = q3.shape[:2] + (1,)
    step = lax.broadcasted_iota(jnp.int32, shape, 1) % STEPS
    first = jnp.sum(q3 * nk[0], axis=2, keepdims=True)
    second = jnp.sum(q3 * nk[1], axis=2, keepdims=True)
    return first, jnp.where(step >= 1, second, NEG)


def body(
    n_groups,
    n_tp,
    pq,
    sk,
    sv,
    pk,
    pv,
    span_offset,
    prompt_length,
    dq,
    dnk,
    dnv,
    ck,
    cv,
    context,
    routes,
    lengths,
    fk,
    fv,
    arrival_q,
    ank,
    anv,
    p_out,
    d_out,
    a_out,
    kv,
    q_s,
    ck_s,
    cv_s,
    fk_s,
    fv_s,
    rel,
    msg,
    rm,
    po,
    ro,
    ps,
    rs,
    sel,
    bias,
    key_mask,
    eye,
    ret,
    ao,
    load_kv,
    load_big,
    x_send,
    x_recv,
    m_send,
    m_recv,
    o_send,
    o_recv,
    s_send,
    s_recv,
    b_send,
    b_recv,
    out_sem,
):
    g = lax.axis_index("group")
    t = lax.axis_index("tp")
    x, yh = t >> 1, t & 1
    right = ((x + 1) & (X_CHIPS - 1)) * 2 + yh
    left = ((x + X_CHIPS - 1) & (X_CHIPS - 1)) * 2 + yh
    partner = x * 2 + (1 - yh)
    right_x = (x + 1) & (X_CHIPS - 1)
    left_x = (x + X_CHIPS - 1) & (X_CHIPS - 1)
    far_x = (x + 2) & (X_CHIPS - 1)
    yl = (g // CORES) & 1
    beside = g + CORES * (1 - 2 * yl)
    local_len = HEAD_DIM // 4
    n_prompts = fk_s.shape[0] // local_len
    a_rows = n_prompts * ROWS16
    quads = n_prompts // 4
    rows = pq.shape[0]

    arrays = (pk, sk, pv, sv)

    def kv_load(h, a):
        cols = pl.ds(pl.multiple_of(h * HEAD_DIM, HEAD_DIM), HEAD_DIM)
        return pltpu.make_async_copy(arrays[a].at[:, cols], kv.at[h, a, x, yh], load_kv.at[h, a])

    def start_loads(h, c):
        for a in range(4):
            kv_load(h, a).start()
        return c

    lax.fori_loop(0, KV_HEADS, start_loads, 0)
    big = [
        pltpu.make_async_copy(src, dst, load_big.at[i])
        for i, (src, dst) in enumerate(
            ((ck, ck_s), (cv, cv_s), (pq, q_s), (fk, fk_s), (fv, fv_s))
        )
    ]
    for copy in big:
        copy.start()

    barrier = pltpu.get_barrier_semaphore()

    def greet_group(k, c):
        pl.semaphore_signal(
            barrier, inc=1, device_id={"group": (g + k) & (n_groups - 1)}, device_id_type=MESH
        )
        return c

    def greet_tp(k, c):
        pl.semaphore_signal(barrier, inc=1, device_id={"tp": (t + k) & (n_tp - 1)}, device_id_type=MESH)
        return c

    lax.fori_loop(1, n_groups, greet_group, 0)
    lax.fori_loop(1, n_tp, greet_tp, 0)
    pl.semaphore_signal(
        barrier, inc=1, device_id={"group": beside, "tp": partner}, device_id_type=MESH
    )
    pl.semaphore_wait(barrier, n_groups - 1 + n_tp - 1 + 1)

    to_right, to_left = {"tp": right}, {"tp": left}
    to_same, to_cross = {"group": beside}, {"group": beside, "tp": partner}
    ny = 1 - yh

    def y_first(i):
        return (i & 1 == 1) | (i == 0) | (i == QUERY_ITEM)

    def hop(src, dst, kind, i, device):
        return pltpu.make_async_remote_copy(
            src_ref=src,
            dst_ref=dst,
            send_sem=x_send.at[i, kind],
            recv_sem=x_recv.at[i, kind],
            device_id=device,
            device_id_type=MESH,
        )

    def same(ref, kind, i, device):
        return hop(ref, ref, kind, i, device)

    keys, values = pl.ds(0, 2), pl.ds(2, 2)

    def own_right(i, xs):
        return same(kv.at[i, :, xs, yh], 0, i, to_right)

    def own_left(i, xs):
        return same(kv.at[i, :, xs, yh], 1, i, to_left)

    def one_y(i, part):
        rows_of = keys if part == 0 else values
        device = to_same if part == 0 else to_cross
        return hop(kv.at[i, rows_of, x, yh], rel.at[i, part, :, 0], 2 + part, i, device)

    def all_y(i, part):
        rows_of = keys if part == 0 else values
        device = to_same if part == 0 else to_cross
        return hop(kv.at[i, rows_of, :, yh], rel.at[i, part], 2 + part, i, device)

    def one_relay(i, part):
        if part == 0:
            return hop(rel.at[i, 0, :, 0], kv.at[i, keys, x, yh], 4, i, to_cross)
        return hop(rel.at[i, 1, :, 0], kv.at[i, values, x, ny], 5, i, to_same)

    def all_relay(i, part):
        if part == 0:
            return hop(rel.at[i, 0], kv.at[i, keys, :, yh], 4, i, to_cross)
        return hop(rel.at[i, 1], kv.at[i, values, :, ny], 5, i, to_same)

    def one_landed(i, part):
        return same(kv.at[i, (keys, values)[part], x, ny], 4 + part, i, to_same)

    def all_landed(i, part):
        return same(kv.at[i, (keys, values)[part], :, ny], 4 + part, i, to_same)

    def partner_right(i, xs):
        return same(kv.at[i, :, xs, ny], 6, i, to_right)

    def partner_left(i, xs):
        return same(kv.at[i, :, xs, ny], 7, i, to_left)

    def pair_right(i, xs):
        return same(kv.at[i, keys, xs], 8, i, to_right)

    def pair_left(i, xs):
        return same(kv.at[i, values, xs], 9, i, to_left)

    def single_right(i, xs):
        return same(kv.at[i, keys, xs, yh], 8, i, to_right)

    def single_left(i, xs):
        return same(kv.at[i, values, xs, yh], 9, i, to_left)

    def by_kind(i, first, second):
        pl.when(y_first(i))(lambda: first(i))
        pl.when(jnp.logical_not(y_first(i)))(lambda: second(i))

    def stage1(i):
        @pl.when(y_first(i))
        def _():
            one_y(i, 0).start()
            one_y(i, 1).start()

        own_right(i, x).start()
        own_left(i, x).start()

    def first_a(i):
        for part in range(2):
            one_y(i, part).wait_recv()
            one_relay(i, part).start()

    def first_b(i):
        one_landed(i, 0).wait_recv()
        one_landed(i, 1).wait_recv()
        partner_right(i, x).start()
        partner_left(i, x).start()

    def first_c(i):
        own_right(i, left_x).wait_recv()
        partner_right(i, left_x).wait_recv()
        pair_right(i, left_x).start()
        own_left(i, right_x).wait_recv()
        partner_left(i, right_x).wait_recv()
        pair_left(i, right_x).start()

    def first_d(i):
        pair_right(i, far_x).wait_recv()
        pair_left(i, far_x).wait_recv()

    def second_a(i):
        own_right(i, left_x).wait_recv()
        single_right(i, left_x).start()
        own_left(i, right_x).wait_recv()
        single_left(i, right_x).start()

    def second_b(i):
        single_right(i, far_x).wait_recv()
        single_left(i, far_x).wait_recv()
        all_y(i, 0).start()
        all_y(i, 1).start()

    def second_c(i):
        for part in range(2):
            all_y(i, part).wait_recv()
            all_relay(i, part).start()

    def second_d(i):
        all_landed(i, 0).wait_recv()
        all_landed(i, 1).wait_recv()

    def stage_a(i):
        by_kind(i, first_a, second_a)

    def stage_b(i):
        by_kind(i, first_b, second_b)

    def stage_c(i):
        by_kind(i, first_c, second_c)

    def stage_d(i):
        by_kind(i, first_d, second_d)

    def first_drain(i):
        for part in range(2):
            one_y(i, part).wait_send()
            one_relay(i, part).wait_send()
        partner_right(i, x).wait_send()
        partner_left(i, x).wait_send()
        pair_right(i, left_x).wait_send()
        pair_left(i, right_x).wait_send()

    def second_drain(i):
        for part in range(2):
            all_y(i, part).wait_send()
            all_relay(i, part).wait_send()
        single_right(i, left_x).wait_send()
        single_left(i, right_x).wait_send()

    def drain_item(i, c):
        own_right(i, x).wait_send()
        own_left(i, x).wait_send()
        by_kind(i, first_drain, second_drain)
        return c

    def start_item(i, c):
        for a in range(4):
            kv_load(i, a).wait()
        stage1(i)
        return c

    start_item(0, 0)
    start_item(1, 0)

    def msg_copy(k):
        peer = (g + k) & (n_groups - 1)
        return pltpu.make_async_remote_copy(
            src_ref=msg.at[peer],
            dst_ref=rm.at[g],
            send_sem=m_send.at[k],
            recv_sem=m_recv.at[g],
            device_id={"group": peer},
            device_id_type=MESH,
        )

    def msg_wait(k):
        peer = (g + k) & (n_groups - 1)
        pltpu.make_async_remote_copy(
            src_ref=rm.at[peer],
            dst_ref=rm.at[peer],
            send_sem=m_send.at[k],
            recv_sem=m_recv.at[peer],
            device_id={"group": peer},
            device_id_type=MESH,
        ).wait_recv()

    def send_msg(k, c):
        msg_copy(k).start()
        return c

    def wait_msg(k, c):
        msg_wait(k)
        return c

    pair = (n_groups, CAPACITY, ROWS16, HEAD_DIM)
    row_id = lax.broadcasted_iota(jnp.int32, (1, ROWS16, 1), 1)
    extra = jnp.zeros((n_groups * CAPACITY, ROWS16, HEAD_DIM), jnp.float32)
    for step in range(STEPS):
        nk = ank[...].astype(jnp.float32)[:, step : step + 1]
        nv = anv[...].astype(jnp.float32)[:, step : step + 1]
        extra = jnp.where(row_id == step, nk, jnp.where(row_id == STEPS + step, nv, extra))
    msg[:, :, 0:ROWS16, :] = arrival_q[...]
    msg[:, :, ROWS16 : 2 * ROWS16, :] = extra.astype(jnp.bfloat16).reshape(pair)
    lax.fori_loop(1, n_groups, send_msg, 0)
    rm[g] = msg[g]

    def decode():
        big[0].wait()
        big[1].wait()
        b = dnk.shape[0]
        q = dq[...].reshape(b, ROWS16, HEAD_DIM)
        s = lax.dot_general(
            q, ck_s[...], (((2,), (2,)), ((0,), (0,))), preferred_element_type=jnp.float32
        )
        limit = spread(context[...].astype(jnp.float32), b, ROWS16, 0).reshape(b, ROWS16, 1)
        slot = lax.broadcasted_iota(jnp.int32, s.shape, 2).astype(jnp.float32)
        s = jnp.where(slot < limit, s, NEG)
        nk = dnk[...].astype(jnp.float32)
        nv = dnv[...].astype(jnp.float32)
        n0, n1 = new_scores(q.astype(jnp.float32), (nk[:, 0:1], nk[:, 1:2]))
        m = jnp.maximum(jnp.max(s, axis=2, keepdims=True), jnp.maximum(n0, n1))
        w = jnp.exp2((s - m) * RATE)
        w0 = jnp.exp2((n0 - m) * RATE)
        w1 = jnp.exp2((n1 - m) * RATE)
        total = jnp.sum(w, axis=2, keepdims=True) + w0 + w1
        o = lax.dot_general(
            w.astype(jnp.bfloat16),
            cv_s[...],
            (((2,), (1,)), ((0,), (0,))),
            preferred_element_type=jnp.float32,
        )
        o = o + w0.astype(jnp.bfloat16).astype(jnp.float32) * nv[:, 0:1]
        o = o + w1.astype(jnp.bfloat16).astype(jnp.float32) * nv[:, 1:2]
        d_out[...] = (o / total).reshape(b * ROWS16, HEAD_DIM).astype(jnp.bfloat16)

    def quad_rows(i):
        half = i % 2 * (4 * ROWS16)
        return i // 2, slice(half, half + 4 * ROWS16)

    def queries_of(xs, ys):
        parts = []
        for i in range(quads):
            block, part = quad_rows(i)
            parts.append(kv[QUERY_ITEM, block, xs, ys, part, :])
        return jnp.concatenate(parts, axis=0)

    def arrivals_choose():
        lax.fori_loop(1, n_groups, wait_msg, 0)
        lanes = routes.shape[1]
        per_row = lanes // n_prompts
        base = g % per_row * n_prompts
        own = routes[pl.ds(g // per_row, 1), :].astype(jnp.float32)
        dest = spread(own, n_prompts, ROWS16, base)
        owner = lax.broadcasted_iota(jnp.int32, (a_rows, lanes), 0) // ROWS16
        other = lax.broadcasted_iota(jnp.int32, (a_rows, lanes), 1) - base
        rank = jnp.sum(
            jnp.where((dest == own) & (other >= 0) & (other < owner), 1.0, 0.0),
            axis=1,
            keepdims=True,
        )
        within = lax.broadcasted_iota(jnp.int32, (a_rows, 1), 0) % ROWS16
        target = (dest * CAPACITY + rank) * ROWS16 + within.astype(jnp.float32)
        slot_rows = n_groups * CAPACITY * ROWS16
        column = lax.broadcasted_iota(jnp.int32, (a_rows, slot_rows), 1).astype(jnp.float32)
        sel[...] = jnp.where(column == target, 1.0, 0.0).astype(jnp.bfloat16)
        got = rm[:, :, 0:ROWS16, :].reshape(slot_rows, HEAD_DIM)
        chosen = dot_n(sel[...], got).astype(jnp.bfloat16)
        for i in range(quads):
            block, part = quad_rows(i)
            kv[QUERY_ITEM, block, x, yh, part, :] = chosen[i * 4 * ROWS16 : (i + 1) * 4 * ROWS16]
        stage1(QUERY_ITEM)
        own_len = lengths[pl.ds(g // per_row, 1), :].astype(jnp.float32)
        limit = spread(own_len, n_prompts, ROWS16, base) - (t * local_len).astype(jnp.float32)
        col = lax.broadcasted_iota(jnp.int32, (a_rows, HEAD_DIM), 1)
        quad_row = (lax.broadcasted_iota(jnp.int32, (a_rows, HEAD_DIM), 0) // ROWS16) % 4
        keep = (col // local_len == quad_row) & ((col % local_len).astype(jnp.float32) < limit)
        bias[...] = jnp.where(keep, 0.0, NEG)

    def po_copy(h, k):
        return pltpu.make_async_remote_copy(
            src_ref=po.at[h],
            dst_ref=ro.at[t],
            send_sem=o_send.at[k],
            recv_sem=o_recv.at[t],
            device_id={"tp": h},
            device_id_type=MESH,
        )

    def ps_copy(h, k):
        return pltpu.make_async_remote_copy(
            src_ref=ps.at[h],
            dst_ref=rs.at[t],
            send_sem=s_send.at[k],
            recv_sem=s_recv.at[t],
            device_id={"tp": h},
            device_id_type=MESH,
        )

    def po_wait(k):
        peer = (t + k) & (n_tp - 1)
        for send_sem, recv_sem, ref in ((o_send, o_recv, ro), (s_send, s_recv, rs)):
            pltpu.make_async_remote_copy(
                src_ref=ref.at[peer],
                dst_ref=ref.at[peer],
                send_sem=send_sem.at[k],
                recv_sem=recv_sem.at[peer],
                device_id={"tp": peer},
                device_id_type=MESH,
            ).wait_recv()

    def partial_head(h, o_ref, s_ref, at):
        cols = pl.ds(pl.multiple_of(h * HEAD_DIM, HEAD_DIM), HEAD_DIM)
        lane = lax.broadcasted_iota(jnp.int32, (4 * ROWS16, HEAD_DIM), 1)
        stats = jnp.zeros((4 * ROWS16, HEAD_DIM), jnp.float32)
        for i in range(quads):
            rows_i = slice(i * 4 * ROWS16, (i + 1) * 4 * ROWS16)
            keys_i = slice(i * HEAD_DIM, (i + 1) * HEAD_DIM)
            block, part = quad_rows(i)
            q = kv[QUERY_ITEM, block, h >> 1, h & 1, part, :]
            s = dot_t(q, fk_s[keys_i, cols]) + bias[rows_i, :]
            m = jnp.max(s, axis=1, keepdims=True)
            w = jnp.exp2((s - m) * RATE)
            total = jnp.sum(w, axis=1, keepdims=True)
            o_ref[at, rows_i, :] = dot_n(w.astype(jnp.bfloat16), fv_s[keys_i, cols]).astype(
                jnp.bfloat16
            )
            stats = jnp.where(lane == i, m, stats)
            stats = jnp.where(lane == quads + i, total, stats)
        s_ref[at] = stats

    def arrivals_partial():
        stage_d(QUERY_ITEM)
        big[3].wait()
        big[4].wait()

        def one(k, c):
            h = (t + k) & (n_tp - 1)
            partial_head(h, po, ps, h)
            po_copy(h, k).start()
            ps_copy(h, k).start()
            return c

        lax.fori_loop(1, n_tp, one, 0)
        partial_head(t, ro, rs, t)

    def ret_copy(k):
        peer = (g + k) & (n_groups - 1)
        return pltpu.make_async_remote_copy(
            src_ref=ret.at[peer],
            dst_ref=ao.at[g],
            send_sem=b_send.at[k],
            recv_sem=b_recv.at[g],
            device_id={"group": peer},
            device_id_type=MESH,
        )

    def ret_wait(k):
        peer = (g + k) & (n_groups - 1)
        pltpu.make_async_remote_copy(
            src_ref=ao.at[peer],
            dst_ref=ao.at[peer],
            send_sem=b_send.at[k],
            recv_sem=b_recv.at[peer],
            device_id={"group": peer},
            device_id_type=MESH,
        ).wait_recv()

    def arrivals_join():
        def wait(k, c):
            po_wait(k)
            return c

        lax.fori_loop(1, n_tp, wait, 0)
        slot_rows = n_groups * CAPACITY * ROWS16
        extra = rm[:, :, ROWS16 : 2 * ROWS16, :].reshape(slot_rows, HEAD_DIM)
        new = dot_n(sel[...], extra).reshape(n_prompts, ROWS16, HEAD_DIM)
        q3 = queries_of(x, yh).astype(jnp.float32).reshape(n_prompts, ROWS16, HEAD_DIM)
        n0, n1 = new_scores(q3, (new[:, 0:1], new[:, 1:2]))
        n0 = n0.reshape(a_rows, 1)
        n1 = n1.reshape(a_rows, 1)
        ms = [
            jnp.concatenate([rs[p][:, i : i + 1] for i in range(quads)], axis=0)
            for p in range(n_tp)
        ]
        m = jnp.maximum(n0, n1)
        for mp in ms:
            m = jnp.maximum(m, mp)
        w0 = jnp.exp2((n0 - m) * RATE)
        w1 = jnp.exp2((n1 - m) * RATE)
        total = w0 + w1
        o = jnp.zeros((a_rows, HEAD_DIM), jnp.float32)
        for p in range(n_tp):
            wp = jnp.exp2((ms[p] - m) * RATE)
            lp = jnp.concatenate(
                [rs[p][:, quads + i : quads + i + 1] for i in range(quads)], axis=0
            )
            total = total + wp * lp
            o = o + wp * ro[p].astype(jnp.float32)
        w0 = w0.astype(jnp.bfloat16).astype(jnp.float32).reshape(n_prompts, ROWS16, 1)
        w1 = w1.astype(jnp.bfloat16).astype(jnp.float32).reshape(n_prompts, ROWS16, 1)
        o = o + (w0 * new[:, 2:3] + w1 * new[:, 3:4]).reshape(a_rows, HEAD_DIM)
        res = (o / total).astype(jnp.bfloat16)
        back = lax.dot_general(
            sel[...], res, (((0,), (0,)), ((), ())), preferred_element_type=jnp.float32
        )
        ret[...] = back.astype(jnp.bfloat16).reshape(n_groups, CAPACITY, ROWS16, HEAD_DIM)

        def send(k, c):
            ret_copy(k).start()
            return c

        lax.fori_loop(1, n_groups, send, 0)

    def prefill_masks():
        shape = (n_tp * rows, rows)
        key = lax.broadcasted_iota(jnp.int32, shape, 0)
        row = lax.broadcasted_iota(jnp.int32, shape, 1) + t * rows
        key_mask[...] = jnp.where(key <= row, 0.0, NEG).astype(jnp.bfloat16)
        row = lax.broadcasted_iota(jnp.int32, (rows, rows), 0)
        column = lax.broadcasted_iota(jnp.int32, (rows, rows), 1)
        eye[...] = jnp.where(row == column, 1.0, 0.0).astype(jnp.bfloat16)

    def prefill_half(h, half):
        vis = span_offset[0] > 0
        part = 2
        n_rows = part * rows
        n_keys = n_tp * rows
        kp = kv[h, 0].reshape(n_keys, HEAD_DIM)
        ks = jnp.concatenate([kv[h, 1].reshape(n_keys, HEAD_DIM), key_mask[...]], axis=1)
        ones = jnp.ones((n_keys, HEAD_DIM), jnp.bfloat16)
        vp = jnp.concatenate([kv[h, 2].reshape(n_keys, HEAD_DIM), ones], axis=1)
        vs = jnp.concatenate([kv[h, 3].reshape(n_keys, HEAD_DIM), ones], axis=1)
        position = lax.broadcasted_iota(jnp.int32, (n_rows, HEAD_DIM), 0) % rows + t * rows
        live = span_offset[0] + position < prompt_length[0]
        eyes = jnp.concatenate([eye[...]] * part, axis=0)

        def cols(i):
            start = (2 * h + half) * (GROUP_SIZE // 2 * HEAD_DIM) + i * HEAD_DIM
            return pl.ds(pl.multiple_of(start, HEAD_DIM), HEAD_DIM)

        queries = [q_s[:, cols(i)] for i in range(GROUP_SIZE // 2)]
        for j in range(GROUP_SIZE // 2 // part):
            q = jnp.concatenate(queries[j * part : (j + 1) * part], axis=0)
            sp = dot_t(q, kp)
            ss = dot_t(jnp.concatenate([q, eyes], axis=1), ks)
            mp = jnp.max(sp, axis=1, keepdims=True)
            m = jnp.max(ss, axis=1, keepdims=True)
            m = jnp.where(vis, jnp.maximum(m, mp), m)
            wp = jnp.exp2((sp - jnp.where(vis, m, -NEG)) * RATE)
            ws = jnp.exp2((ss - m) * RATE)
            o = dot_n(wp.astype(jnp.bfloat16), vp) + dot_n(ws.astype(jnp.bfloat16), vs)
            o = o[:, :HEAD_DIM] / o[:, HEAD_DIM:]
            o = jnp.where(live, o, 0.0).astype(jnp.bfloat16)
            for i in range(part):
                q_s[:, cols(j * part + i)] = o[i * rows : (i + 1) * rows]

    def head_out(h):
        width = GROUP_SIZE * HEAD_DIM
        cols = pl.ds(pl.multiple_of(h * width, width), width)
        return pltpu.make_async_copy(q_s.at[:, cols], p_out.at[:, cols], out_sem.at[h])

    prefill_masks()
    for h in (0, 1):
        stage_a(h)
    for h in (0, 1):
        stage_b(h)
    start_item(2, 0)
    decode()
    stage_c(0)
    stage_c(1)
    start_item(3, 0)
    arrivals_choose()
    stage_a(2)
    stage_a(3)
    start_item(4, 0)
    stage_b(2)
    stage_a(QUERY_ITEM)
    big[2].wait()

    def half_turn(n, c):
        s = n >> 1

        @pl.when(n & 1 == 0)
        def _():
            stage_d(s)

        @pl.when(n & 1 == 1)
        def _():
            @pl.when(s + 2 < KV_HEADS)
            def _():
                stage_c(s + 2)

            @pl.when(s + 3 < KV_HEADS)
            def _():
                stage_b(s + 3)

            @pl.when(s + 4 < KV_HEADS)
            def _():
                stage_a(s + 4)

            @pl.when(s + 5 < KV_HEADS)
            def _():
                start_item(s + 5, 0)

            @pl.when(s == 0)
            def _():
                stage_b(QUERY_ITEM)

            @pl.when(s == 1)
            def _():
                stage_c(QUERY_ITEM)

            @pl.when(s == 2)
            def _():
                arrivals_partial()

            @pl.when(s == 5)
            def _():
                arrivals_join()

        prefill_half(s, n & 1)

        @pl.when(n & 1 == 1)
        def _():
            head_out(s).start()

        return c

    lax.fori_loop(0, 2 * KV_HEADS, half_turn, 0)

    def wait_ret(k, c):
        ret_wait(k)
        return c

    lax.fori_loop(1, n_groups, wait_ret, 0)
    ao[g] = ret[g]
    a_out[...] = ao[...]

    def drain_group(k, c):
        msg_copy(k).wait_send()
        ret_copy(k).wait_send()
        return c

    def drain_tp(k, c):
        h = (t + k) & (n_tp - 1)
        po_copy(h, k).wait_send()
        ps_copy(h, k).wait_send()
        return c

    def drain_out(h, c):
        head_out(h).wait()
        return c

    lax.fori_loop(1, n_groups, drain_group, 0)
    lax.fori_loop(1, n_tp, drain_tp, 0)
    lax.fori_loop(0, ITEMS, drain_item, 0)
    lax.fori_loop(0, KV_HEADS, drain_out, 0)


def publish_body(*refs):
    sources, results, sems = refs[:3], refs[3:6], refs[6]
    copies = []
    parts = 8
    width = sources[0].shape[1] // parts
    for i in range(parts):
        cols = slice(i * width, (i + 1) * width)
        copies.append((sources[0].at[:, cols], results[0].at[:, cols]))
    copies += [(sources[1], results[1]), (sources[2], results[2])]
    copies = [pltpu.make_async_copy(a, b, sems.at[i]) for i, (a, b) in enumerate(copies)]
    for copy in copies:
        copy.start()
    for copy in copies:
        copy.wait()


def publish(*results):
    any_ = pl.BlockSpec(memory_space=pl.ANY)
    return pl.pallas_call(
        publish_body,
        out_shape=tuple(jax.ShapeDtypeStruct(r.shape, r.dtype) for r in results),
        in_specs=[any_] * 3,
        out_specs=[any_] * 3,
        scratch_shapes=[pltpu.SemaphoreType.DMA((10,))],
        compiler_params=pltpu.CompilerParams(vmem_limit_bytes=56 * 1024 * 1024),
    )(*results)


def to_rows(queries):
    b = queries.shape[0]
    return queries.reshape(b, STEPS, GROUP_SIZE, HEAD_DIM).transpose(0, 2, 1, 3)


def from_rows(rows, b):
    rows = rows.reshape(b, GROUP_SIZE, STEPS, HEAD_DIM).transpose(0, 2, 1, 3)
    return rows.reshape(b, STEPS, GROUP_SIZE * HEAD_DIM)


def local(
    prefill_queries,
    span_keys,
    span_values,
    prefix_keys,
    prefix_values,
    span_offsets,
    prompt_lengths,
    decode_queries,
    decode_new_keys,
    decode_new_values,
    cache_keys,
    cache_values,
    context_lengths,
    placement,
    finished_lengths,
    finished_keys,
    finished_values,
    arrival_queries,
    arrival_new_keys,
    arrival_new_values,
):
    n_groups = lax.axis_size("group")
    n_tp = lax.axis_size("tp")
    n_prompts, local_len, width = finished_keys.shape
    rows = prefill_queries.shape[0]
    dec = decode_queries.shape[0]
    slots = arrival_queries.shape[0]
    dq = to_rows(decode_queries).reshape(dec * ROWS16, HEAD_DIM)
    arrival_rows = to_rows(arrival_queries).reshape(n_groups, CAPACITY, ROWS16, HEAD_DIM)
    lanes = min(128, placement.shape[0])
    any_ = pl.BlockSpec(memory_space=pl.ANY)
    vmem = pl.BlockSpec(memory_space=pltpu.VMEM)
    smem = pl.BlockSpec(memory_space=pltpu.SMEM)
    bf, f32 = jnp.bfloat16, jnp.float32
    a_rows = n_prompts * ROWS16
    dma = pltpu.SemaphoreType.DMA
    p_out, d_out, a_out = pl.pallas_call(
        functools.partial(body, n_groups, n_tp),
        out_shape=(
            jax.ShapeDtypeStruct(prefill_queries.shape, bf),
            jax.ShapeDtypeStruct(dq.shape, bf),
            jax.ShapeDtypeStruct((n_groups, CAPACITY, ROWS16, HEAD_DIM), bf),
        ),
        in_specs=[any_] * 5
        + [smem] * 2
        + [vmem] * 3
        + [any_] * 2
        + [vmem] * 3
        + [any_] * 2
        + [vmem] * 3,
        out_specs=[any_, vmem, vmem],
        scratch_shapes=[
            pltpu.VMEM((ITEMS, 4, X_CHIPS, 2, rows, HEAD_DIM), bf),
            pltpu.VMEM(prefill_queries.shape, bf),
            pltpu.VMEM(cache_keys.shape, bf),
            pltpu.VMEM(cache_values.shape, bf),
            pltpu.VMEM((n_prompts * local_len, width), bf),
            pltpu.VMEM((n_prompts * local_len, width), bf),
            pltpu.VMEM((ITEMS, 2, 2, X_CHIPS, rows, HEAD_DIM), bf),
            pltpu.VMEM((n_groups, CAPACITY, 2 * ROWS16, HEAD_DIM), bf),
            pltpu.VMEM((n_groups, CAPACITY, 2 * ROWS16, HEAD_DIM), bf),
            pltpu.VMEM((n_tp, a_rows, HEAD_DIM), bf),
            pltpu.VMEM((n_tp, a_rows, HEAD_DIM), bf),
            pltpu.VMEM((n_tp, 4 * ROWS16, HEAD_DIM), f32),
            pltpu.VMEM((n_tp, 4 * ROWS16, HEAD_DIM), f32),
            pltpu.VMEM((a_rows, slots * ROWS16), bf),
            pltpu.VMEM((a_rows, HEAD_DIM), f32),
            pltpu.VMEM((n_tp * rows, rows), bf),
            pltpu.VMEM((rows, rows), bf),
            pltpu.VMEM((n_groups, CAPACITY, ROWS16, HEAD_DIM), bf),
            pltpu.VMEM((n_groups, CAPACITY, ROWS16, HEAD_DIM), bf),
            dma((KV_HEADS, 4)),
            dma((5,)),
            dma((ITEMS, 10)),
            dma((ITEMS, 10)),
            dma((n_groups,)),
            dma((n_groups,)),
            dma((n_tp,)),
            dma((n_tp,)),
            dma((n_tp,)),
            dma((n_tp,)),
            dma((n_groups,)),
            dma((n_groups,)),
            dma((KV_HEADS,)),
        ],
        compiler_params=pltpu.CompilerParams(
            collective_id=0, has_side_effects=True, vmem_limit_bytes=56 * 1024 * 1024
        ),
    )(
        prefill_queries,
        span_keys,
        span_values,
        prefix_keys,
        prefix_values,
        span_offsets,
        prompt_lengths,
        dq,
        decode_new_keys,
        decode_new_values,
        cache_keys,
        cache_values,
        context_lengths[None, :],
        placement.reshape(-1, lanes),
        finished_lengths.reshape(-1, lanes),
        finished_keys.reshape(n_prompts * local_len, width),
        finished_values.reshape(n_prompts * local_len, width),
        arrival_rows,
        arrival_new_keys,
        arrival_new_values,
    )
    p_out, d_out, a_out = publish(p_out, d_out, a_out)
    return (p_out, from_rows(d_out, dec), from_rows(a_out, slots))


def solution(mesh):
    both = P(("group", "tp"), None)
    heads = P("group", None, "tp")
    placed = (
        (both,) * 5
        + (P("group"),) * 2
        + (heads,) * 5
        + (P("group"), P(), P())
        + (P("group", "tp", None),) * 2
        + (heads,) * 3
    )
    return jax.shard_map(
        local,
        mesh=mesh,
        in_specs=placed,
        out_specs=(both, heads, heads),
        check_vma=False,
    )
```

```python
import functools
import math

import jax
import jax.numpy as jnp
from jax import lax
from jax.experimental import pallas as pl
from jax.experimental.pallas import tpu as pltpu
from jax.sharding import PartitionSpec as P

KV_HEADS = 8
GROUP_SIZE = 8
HEAD_DIM = 128
CAPACITY = 2
STEPS = 2
ROWS16 = GROUP_SIZE * STEPS
MESH = pl.DeviceIdType.MESH
NEG = -1e30
RATE = math.log2(math.e) / math.sqrt(HEAD_DIM)
X_CHIPS = 4
CORES = 2
STAT_LANES = 16
ITEMS = KV_HEADS + 1
QUERY_ITEM = KV_HEADS


def dot_t(a, b):
    return lax.dot_general(a, b, (((1,), (1,)), ((), ())), preferred_element_type=jnp.float32)


def dot_n(a, b):
    return lax.dot_general(a, b, (((1,), (0,)), ((), ())), preferred_element_type=jnp.float32)


def spread(row, count, reps, base):
    shape = (count * reps, row.shape[1])
    owner = lax.broadcasted_iota(jnp.int32, shape, 0) // reps + base
    lane = lax.broadcasted_iota(jnp.int32, shape, 1)
    return jnp.sum(jnp.where(owner == lane, row, 0.0), axis=1, keepdims=True)


def new_scores(q3, nk):
    shape = q3.shape[:2] + (1,)
    step = lax.broadcasted_iota(jnp.int32, shape, 1) % STEPS
    first = jnp.sum(q3 * nk[0], axis=2, keepdims=True)
    second = jnp.sum(q3 * nk[1], axis=2, keepdims=True)
    return first, jnp.where(step >= 1, second, NEG)


def body(
    n_groups,
    n_tp,
    pq,
    sk,
    sv,
    pk,
    pv,
    span_offset,
    prompt_length,
    dq,
    dnk,
    dnv,
    ck,
    cv,
    context,
    routes,
    lengths,
    fk,
    fv,
    arrival_q,
    ank,
    anv,
    p_out,
    d_out,
    a_out,
    kv,
    q_s,
    ck_s,
    cv_s,
    fk_s,
    fv_s,
    rel,
    msg,
    rm,
    po,
    ro,
    ps,
    rs,
    sel,
    bias,
    key_mask,
    eye,
    ret,
    ao,
    load_kv,
    load_big,
    x_send,
    x_recv,
    m_send,
    m_recv,
    o_send,
    o_recv,
    s_send,
    s_recv,
    b_send,
    b_recv,
    out_sem,
):
    g = lax.axis_index("group")
    t = lax.axis_index("tp")
    x, yh = t >> 1, t & 1
    right = ((x + 1) & (X_CHIPS - 1)) * 2 + yh
    left = ((x + X_CHIPS - 1) & (X_CHIPS - 1)) * 2 + yh
    partner = x * 2 + (1 - yh)
    right_x = (x + 1) & (X_CHIPS - 1)
    left_x = (x + X_CHIPS - 1) & (X_CHIPS - 1)
    far_x = (x + 2) & (X_CHIPS - 1)
    yl = (g // CORES) & 1
    beside = g + CORES * (1 - 2 * yl)
    local_len = HEAD_DIM // 4
    n_prompts = fk_s.shape[0] // local_len
    a_rows = n_prompts * ROWS16
    quads = n_prompts // 4
    rows = pq.shape[0]

    arrays = (pk, sk, pv, sv)

    def kv_load(h, a):
        cols = pl.ds(pl.multiple_of(h * HEAD_DIM, HEAD_DIM), HEAD_DIM)
        return pltpu.make_async_copy(arrays[a].at[:, cols], kv.at[h, a, x, yh], load_kv.at[h])

    def start_loads(h, c):
        for a in range(4):
            kv_load(h, a).start()
        return c

    lax.fori_loop(0, KV_HEADS, start_loads, 0)
    big = [
        pltpu.make_async_copy(src, dst, load_big.at[i])
        for i, (src, dst) in enumerate(
            ((ck, ck_s), (cv, cv_s), (pq, q_s), (fk, fk_s), (fv, fv_s))
        )
    ]
    for copy in big:
        copy.start()

    barrier = pltpu.get_barrier_semaphore()

    def greet_group(k, c):
        pl.semaphore_signal(
            barrier, inc=1, device_id={"group": (g + k) & (n_groups - 1)}, device_id_type=MESH
        )
        return c

    def greet_tp(k, c):
        pl.semaphore_signal(barrier, inc=1, device_id={"tp": (t + k) & (n_tp - 1)}, device_id_type=MESH)
        return c

    lax.fori_loop(1, n_groups, greet_group, 0)
    lax.fori_loop(1, n_tp, greet_tp, 0)
    pl.semaphore_signal(
        barrier, inc=1, device_id={"group": beside, "tp": partner}, device_id_type=MESH
    )
    pl.semaphore_wait(barrier, n_groups - 1 + n_tp - 1 + 1)

    to_right, to_left = {"tp": right}, {"tp": left}
    to_same, to_cross = {"group": beside}, {"group": beside, "tp": partner}
    ny = 1 - yh

    def y_first(i):
        return i % 3 != 1

    def hop(src, dst, kind, i, device):
        return pltpu.make_async_remote_copy(
            src_ref=src,
            dst_ref=dst,
            send_sem=x_send.at[i, kind],
            recv_sem=x_recv.at[i, kind],
            device_id=device,
            device_id_type=MESH,
        )

    def same(ref, kind, i, device):
        return hop(ref, ref, kind, i, device)

    keys, values = pl.ds(0, 2), pl.ds(2, 2)

    def own_right(i, xs):
        return same(kv.at[i, :, xs, yh], 0, i, to_right)

    def own_left(i, xs):
        return same(kv.at[i, :, xs, yh], 1, i, to_left)

    def one_y(i, part):
        rows_of = keys if part == 0 else values
        device = to_same if part == 0 else to_cross
        return hop(kv.at[i, rows_of, x, yh], rel.at[i, part, :, 0], 2 + part, i, device)

    def all_y(i, part):
        rows_of = keys if part == 0 else values
        device = to_same if part == 0 else to_cross
        return hop(kv.at[i, rows_of, :, yh], rel.at[i, part], 2 + part, i, device)

    def one_relay(i, part):
        if part == 0:
            return hop(rel.at[i, 0, :, 0], kv.at[i, keys, x, yh], 4, i, to_cross)
        return hop(rel.at[i, 1, :, 0], kv.at[i, values, x, ny], 5, i, to_same)

    def all_relay(i, part):
        if part == 0:
            return hop(rel.at[i, 0], kv.at[i, keys, :, yh], 4, i, to_cross)
        return hop(rel.at[i, 1], kv.at[i, values, :, ny], 5, i, to_same)

    def one_landed(i, part):
        return same(kv.at[i, (keys, values)[part], x, ny], 4 + part, i, to_same)

    def all_landed(i, part):
        return same(kv.at[i, (keys, values)[part], :, ny], 4 + part, i, to_same)

    def partner_right(i, xs):
        return same(kv.at[i, :, xs, ny], 6, i, to_right)

    def partner_left(i, xs):
        return same(kv.at[i, :, xs, ny], 7, i, to_left)

    def pair_right(i, xs):
        return same(kv.at[i, keys, xs], 8, i, to_right)

    def pair_left(i, xs):
        return same(kv.at[i, values, xs], 9, i, to_left)

    def single_right(i, xs):
        return same(kv.at[i, keys, xs, yh], 8, i, to_right)

    def single_left(i, xs):
        return same(kv.at[i, values, xs, yh], 9, i, to_left)

    def by_kind(i, first, second):
        pl.when(y_first(i))(lambda: first(i))
        pl.when(jnp.logical_not(y_first(i)))(lambda: second(i))

    def stage1(i):
        @pl.when(y_first(i))
        def _():
            one_y(i, 0).start()
            one_y(i, 1).start()

        own_right(i, x).start()
        own_left(i, x).start()

    def first_a(i):
        for part in range(2):
            one_y(i, part).wait_recv()
            one_relay(i, part).start()

    def first_b(i):
        one_landed(i, 0).wait_recv()
        one_landed(i, 1).wait_recv()
        partner_right(i, x).start()
        partner_left(i, x).start()

    def first_c(i):
        own_right(i, left_x).wait_recv()
        partner_right(i, left_x).wait_recv()
        pair_right(i, left_x).start()
        own_left(i, right_x).wait_recv()
        partner_left(i, right_x).wait_recv()
        pair_left(i, right_x).start()

    def first_d(i):
        pair_right(i, far_x).wait_recv()
        pair_left(i, far_x).wait_recv()

    def second_a(i):
        own_right(i, left_x).wait_recv()
        single_right(i, left_x).start()
        own_left(i, right_x).wait_recv()
        single_left(i, right_x).start()

    def second_b(i):
        single_right(i, far_x).wait_recv()
        single_left(i, far_x).wait_recv()
        all_y(i, 0).start()
        all_y(i, 1).start()

    def second_c(i):
        for part in range(2):
            all_y(i, part).wait_recv()
            all_relay(i, part).start()

    def second_d(i):
        all_landed(i, 0).wait_recv()
        all_landed(i, 1).wait_recv()

    def stage_a(i):
        by_kind(i, first_a, second_a)

    def stage_b(i):
        by_kind(i, first_b, second_b)

    def stage_c(i):
        by_kind(i, first_c, second_c)

    def stage_d(i):
        by_kind(i, first_d, second_d)

    def first_drain(i):
        for part in range(2):
            one_y(i, part).wait_send()
            one_relay(i, part).wait_send()
        partner_right(i, x).wait_send()
        partner_left(i, x).wait_send()
        pair_right(i, left_x).wait_send()
        pair_left(i, right_x).wait_send()

    def second_drain(i):
        for part in range(2):
            all_y(i, part).wait_send()
            all_relay(i, part).wait_send()
        single_right(i, left_x).wait_send()
        single_left(i, right_x).wait_send()

    def drain_item(i, c):
        own_right(i, x).wait_send()
        own_left(i, x).wait_send()
        by_kind(i, first_drain, second_drain)
        return c

    def start_item(i, c):
        block = kv.at[i, :, x, yh]
        pltpu.make_async_copy(block, block, load_kv.at[i]).wait()
        stage1(i)
        return c

    window = 4
    lax.fori_loop(0, window, start_item, 0)

    others = pl.ds(0, n_groups - 1)

    def group_copy(src, dst, send_sem, recv_sem, peer):
        return pltpu.make_async_remote_copy(
            src_ref=src,
            dst_ref=dst,
            send_sem=send_sem,
            recv_sem=recv_sem,
            device_id={"group": peer},
            device_id_type=MESH,
        )

    def all_msgs():
        return group_copy(msg.at[others], rm.at[others], m_send, m_recv, beside)

    def all_rets():
        return group_copy(ret.at[others], ao.at[others], b_send, b_recv, beside)

    def send_msg(k, c):
        peer = (g + k) & (n_groups - 1)
        group_copy(msg.at[peer], rm.at[g], m_send, m_recv, peer).start()
        return c

    def send_ret(k, c):
        peer = (g + k) & (n_groups - 1)
        group_copy(ret.at[peer], ao.at[g], b_send, b_recv, peer).start()
        return c

    pair = (n_groups, CAPACITY, ROWS16, HEAD_DIM)
    row_id = lax.broadcasted_iota(jnp.int32, (1, ROWS16, 1), 1)
    extra = jnp.zeros((n_groups * CAPACITY, ROWS16, HEAD_DIM), jnp.float32)
    for step in range(STEPS):
        nk = ank[...].astype(jnp.float32)[:, step : step + 1]
        nv = anv[...].astype(jnp.float32)[:, step : step + 1]
        extra = jnp.where(row_id == step, nk, jnp.where(row_id == STEPS + step, nv, extra))
    msg[:, :, 0:ROWS16, :] = arrival_q[...]
    msg[:, :, ROWS16 : 2 * ROWS16, :] = extra.astype(jnp.bfloat16).reshape(pair)
    lax.fori_loop(1, n_groups, send_msg, 0)
    rm[g] = msg[g]

    def decode():
        big[0].wait()
        big[1].wait()
        b = dnk.shape[0]
        q = dq[...].reshape(b, ROWS16, HEAD_DIM)
        s = lax.dot_general(
            q, ck_s[...], (((2,), (2,)), ((0,), (0,))), preferred_element_type=jnp.float32
        )
        limit = spread(context[...].astype(jnp.float32), b, ROWS16, 0).reshape(b, ROWS16, 1)
        slot = lax.broadcasted_iota(jnp.int32, s.shape, 2).astype(jnp.float32)
        s = jnp.where(slot < limit, s, NEG)
        nk = dnk[...].astype(jnp.float32)
        nv = dnv[...].astype(jnp.float32)
        n0, n1 = new_scores(q.astype(jnp.float32), (nk[:, 0:1], nk[:, 1:2]))
        m = jnp.maximum(jnp.max(s, axis=2, keepdims=True), jnp.maximum(n0, n1))
        w = jnp.exp2((s - m) * RATE)
        w0 = jnp.exp2((n0 - m) * RATE)
        w1 = jnp.exp2((n1 - m) * RATE)
        total = jnp.sum(w, axis=2, keepdims=True) + w0 + w1
        o = lax.dot_general(
            w.astype(jnp.bfloat16),
            cv_s[...],
            (((2,), (1,)), ((0,), (0,))),
            preferred_element_type=jnp.float32,
        )
        o = o + w0.astype(jnp.bfloat16).astype(jnp.float32) * nv[:, 0:1]
        o = o + w1.astype(jnp.bfloat16).astype(jnp.float32) * nv[:, 1:2]
        d_out[...] = (o / total).reshape(b * ROWS16, HEAD_DIM).astype(jnp.bfloat16)

    def quad_rows(i):
        half = i % 2 * (4 * ROWS16)
        return i // 2, slice(half, half + 4 * ROWS16)

    def queries_of(xs, ys):
        parts = []
        for i in range(quads):
            block, part = quad_rows(i)
            parts.append(kv[QUERY_ITEM, block, xs, ys, part, :])
        return jnp.concatenate(parts, axis=0)

    def arrivals_choose():
        all_msgs().wait_recv()
        lanes = routes.shape[1]
        per_row = lanes // n_prompts
        base = g % per_row * n_prompts
        own = routes[pl.ds(g // per_row, 1), :].astype(jnp.float32)
        dest = spread(own, n_prompts, ROWS16, base)
        owner = lax.broadcasted_iota(jnp.int32, (a_rows, lanes), 0) // ROWS16
        other = lax.broadcasted_iota(jnp.int32, (a_rows, lanes), 1) - base
        rank = jnp.sum(
            jnp.where((dest == own) & (other >= 0) & (other < owner), 1.0, 0.0),
            axis=1,
            keepdims=True,
        )
        within = lax.broadcasted_iota(jnp.int32, (a_rows, 1), 0) % ROWS16
        target = (dest * CAPACITY + rank) * ROWS16 + within.astype(jnp.float32)
        slot_rows = n_groups * CAPACITY * ROWS16
        column = lax.broadcasted_iota(jnp.int32, (a_rows, slot_rows), 1).astype(jnp.float32)
        sel[...] = jnp.where(column == target, 1.0, 0.0).astype(jnp.bfloat16)
        got = rm[:, :, 0:ROWS16, :].reshape(slot_rows, HEAD_DIM)
        chosen = dot_n(sel[...], got).astype(jnp.bfloat16)
        for i in range(quads):
            block, part = quad_rows(i)
            kv[QUERY_ITEM, block, x, yh, part, :] = chosen[i * 4 * ROWS16 : (i + 1) * 4 * ROWS16]
        stage1(QUERY_ITEM)
        own_len = lengths[pl.ds(g // per_row, 1), :].astype(jnp.float32)
        limit = spread(own_len, n_prompts, ROWS16, base) - (t * local_len).astype(jnp.float32)
        col = lax.broadcasted_iota(jnp.int32, (a_rows, HEAD_DIM), 1)
        quad_row = (lax.broadcasted_iota(jnp.int32, (a_rows, HEAD_DIM), 0) // ROWS16) % 4
        keep = (col // local_len == quad_row) & ((col % local_len).astype(jnp.float32) < limit)
        bias[...] = jnp.where(keep, 0.0, NEG)

    def po_copy(h, k):
        return pltpu.make_async_remote_copy(
            src_ref=po.at[h],
            dst_ref=ro.at[t],
            send_sem=o_send.at[k],
            recv_sem=o_recv.at[t],
            device_id={"tp": h},
            device_id_type=MESH,
        )

    def ps_copy(h, k):
        return pltpu.make_async_remote_copy(
            src_ref=ps.at[h],
            dst_ref=rs.at[t],
            send_sem=s_send.at[k],
            recv_sem=s_recv.at[t],
            device_id={"tp": h},
            device_id_type=MESH,
        )

    def po_wait(k):
        peer = (t + k) & (n_tp - 1)
        for send_sem, recv_sem, ref in ((o_send, o_recv, ro), (s_send, s_recv, rs)):
            pltpu.make_async_remote_copy(
                src_ref=ref.at[peer],
                dst_ref=ref.at[peer],
                send_sem=send_sem.at[k],
                recv_sem=recv_sem.at[peer],
                device_id={"tp": peer},
                device_id_type=MESH,
            ).wait_recv()

    def partial_head(h, o_ref, s_ref, at):
        cols = pl.ds(pl.multiple_of(h * HEAD_DIM, HEAD_DIM), HEAD_DIM)
        lane = lax.broadcasted_iota(jnp.int32, (4 * ROWS16, HEAD_DIM), 1)
        stats = jnp.zeros((4 * ROWS16, HEAD_DIM), jnp.float32)
        rows_of = [slice(i * 4 * ROWS16, (i + 1) * 4 * ROWS16) for i in range(quads)]
        keys_of = [slice(i * HEAD_DIM, (i + 1) * HEAD_DIM) for i in range(quads)]
        scores = []
        for i in range(quads):
            block, part = quad_rows(i)
            q = kv[QUERY_ITEM, block, h >> 1, h & 1, part, :]
            scores.append(dot_t(q, fk_s[keys_of[i], cols]))
        scores = [s + bias[r, :] for s, r in zip(scores, rows_of)]
        tops = [jnp.max(s, axis=1, keepdims=True) for s in scores]
        weights = [jnp.exp2((s - m) * RATE) for s, m in zip(scores, tops)]
        totals = [jnp.sum(w, axis=1, keepdims=True) for w in weights]
        outs = [
            dot_n(w.astype(jnp.bfloat16), fv_s[k, cols]) for w, k in zip(weights, keys_of)
        ]
        for i in range(quads):
            o_ref[at, rows_of[i], :] = outs[i].astype(jnp.bfloat16)
            stats = jnp.where(lane == i, tops[i], stats)
            stats = jnp.where(lane == STAT_LANES // 2 + i, totals[i], stats)
        s_ref[at] = stats

    def arrivals_partial():
        stage_d(QUERY_ITEM)
        big[3].wait()
        big[4].wait()

        def one(k, c):
            h = (t + k) & (n_tp - 1)
            partial_head(h, po, ps, h)
            po_copy(h, k).start()
            ps_copy(h, k).start()
            return c

        lax.fori_loop(1, n_tp, one, 0)
        partial_head(t, ro, rs, t)

    def arrivals_join():
        def wait(k, c):
            po_wait(k)
            return c

        lax.fori_loop(1, n_tp, wait, 0)
        slot_rows = n_groups * CAPACITY * ROWS16
        extra = rm[:, :, ROWS16 : 2 * ROWS16, :].reshape(slot_rows, HEAD_DIM)
        new = dot_n(sel[...], extra).reshape(n_prompts, ROWS16, HEAD_DIM)
        q3 = queries_of(x, yh).astype(jnp.float32).reshape(n_prompts, ROWS16, HEAD_DIM)
        n0, n1 = new_scores(q3, (new[:, 0:1], new[:, 1:2]))
        n0 = n0.reshape(a_rows, 1)
        n1 = n1.reshape(a_rows, 1)
        tile = (4 * ROWS16, HEAD_DIM)
        lane = lax.broadcasted_iota(jnp.int32, tile, 1)
        rows_of = [slice(i * 4 * ROWS16, (i + 1) * 4 * ROWS16) for i in range(quads)]
        t0 = jnp.full(tile, NEG, jnp.float32)
        t1 = jnp.full(tile, NEG, jnp.float32)
        for i in range(quads):
            t0 = jnp.where(lane == i, n0[rows_of[i]], t0)
            t1 = jnp.where(lane == i, n1[rows_of[i]], t1)
        live = lane < quads
        stats = [rs[p] for p in range(n_tp)]
        tops = [jnp.where(live, st, NEG) for st in stats]
        m = jnp.maximum(t0, t1)
        for top in tops:
            m = jnp.maximum(m, top)
        w0 = jnp.exp2((t0 - m) * RATE)
        w1 = jnp.exp2((t1 - m) * RATE)
        total = w0 + w1
        weights = [jnp.exp2((top - m) * RATE) for top in tops]
        for w, st in zip(weights, stats):
            total = total + w * pltpu.roll(st, HEAD_DIM - STAT_LANES // 2, 1)
        inverse = 1.0 / jnp.where(live, total, 1.0)
        weights = [w * inverse for w in weights]
        w0 = w0.astype(jnp.bfloat16).astype(jnp.float32) * inverse
        w1 = w1.astype(jnp.bfloat16).astype(jnp.float32) * inverse
        parts = []
        for i in range(quads):
            wide = (4, ROWS16, HEAD_DIM)
            v0 = jnp.broadcast_to(new[4 * i : 4 * i + 4, 2:3], wide).reshape(tile)
            v1 = jnp.broadcast_to(new[4 * i : 4 * i + 4, 3:4], wide).reshape(tile)
            o = w0[:, i : i + 1] * v0 + w1[:, i : i + 1] * v1
            for p in range(n_tp):
                o = o + weights[p][:, i : i + 1] * ro[p, rows_of[i], :].astype(jnp.float32)
            parts.append(o.astype(jnp.bfloat16))
        res = jnp.concatenate(parts, axis=0)
        back = lax.dot_general(
            sel[...], res, (((0,), (0,)), ((), ())), preferred_element_type=jnp.float32
        )
        ret[...] = back.astype(jnp.bfloat16).reshape(n_groups, CAPACITY, ROWS16, HEAD_DIM)

        lax.fori_loop(1, n_groups, send_ret, 0)

    def prefill_masks():
        shape = (n_tp * rows, rows)
        key = lax.broadcasted_iota(jnp.int32, shape, 0)
        row = lax.broadcasted_iota(jnp.int32, shape, 1) + t * rows
        key_mask[...] = jnp.where(key <= row, 0.0, NEG).astype(jnp.bfloat16)
        row = lax.broadcasted_iota(jnp.int32, (rows, rows), 0)
        column = lax.broadcasted_iota(jnp.int32, (rows, rows), 1)
        eye[...] = jnp.where(row == column, 1.0, 0.0).astype(jnp.bfloat16)

    def prefill_head(h):
        vis = span_offset[0] > 0
        part = 2
        n_rows = part * rows
        n_keys = n_tp * rows
        kp = kv[h, 0].reshape(n_keys, HEAD_DIM)
        ks = jnp.concatenate([kv[h, 1].reshape(n_keys, HEAD_DIM), key_mask[...]], axis=1)
        ones = jnp.ones((n_keys, HEAD_DIM), jnp.bfloat16)
        vp = jnp.concatenate([kv[h, 2].reshape(n_keys, HEAD_DIM), ones], axis=1)
        vs = jnp.concatenate([kv[h, 3].reshape(n_keys, HEAD_DIM), ones], axis=1)
        position = lax.broadcasted_iota(jnp.int32, (n_rows, HEAD_DIM), 0) % rows + t * rows
        live = span_offset[0] + position < prompt_length[0]
        eyes = jnp.concatenate([eye[...]] * part, axis=0)

        def cols(i):
            start = h * (GROUP_SIZE * HEAD_DIM) + i * HEAD_DIM
            return pl.ds(pl.multiple_of(start, HEAD_DIM), HEAD_DIM)

        queries = [q_s[:, cols(i)] for i in range(GROUP_SIZE)]
        chains = GROUP_SIZE // part

        def scores_of(j):
            q = jnp.concatenate(queries[j * part : (j + 1) * part], axis=0)
            return dot_t(q, kp), dot_t(jnp.concatenate([q, eyes], axis=1), ks)

        ahead = scores_of(0)
        for j in range(chains):
            sp, ss = ahead
            if j + 1 < chains:
                ahead = scores_of(j + 1)
            mp = jnp.max(sp, axis=1, keepdims=True)
            m = jnp.max(ss, axis=1, keepdims=True)
            m = jnp.where(vis, jnp.maximum(m, mp), m)
            wp = jnp.exp2((sp - jnp.where(vis, m, -NEG)) * RATE)
            ws = jnp.exp2((ss - m) * RATE)
            o = dot_n(wp.astype(jnp.bfloat16), vp) + dot_n(ws.astype(jnp.bfloat16), vs)
            o = o[:, :HEAD_DIM] / o[:, HEAD_DIM:]
            o = jnp.where(live, o, 0.0).astype(jnp.bfloat16)
            for i in range(part):
                q_s[:, cols(j * part + i)] = o[i * rows : (i + 1) * rows]

    def head_out(h):
        width = GROUP_SIZE * HEAD_DIM
        cols = pl.ds(pl.multiple_of(h * width, width), width)
        return pltpu.make_async_copy(q_s.at[:, cols], p_out.at[:, cols], out_sem.at[h])

    prefill_masks()
    decode()
    for h in range(3):
        stage_a(h)
    stage_b(0)
    arrivals_choose()
    stage_b(1)
    stage_c(0)
    stage_a(QUERY_ITEM)
    big[2].wait()

    def turn(s, c):
        @pl.when(s + window < KV_HEADS)
        def _():
            start_item(s + window, 0)

        @pl.when(s + 3 < KV_HEADS)
        def _():
            stage_a(s + 3)

        @pl.when(s + 2 < KV_HEADS)
        def _():
            stage_b(s + 2)

        @pl.when(s + 1 < KV_HEADS)
        def _():
            stage_c(s + 1)

        @pl.when(s == 0)
        def _():
            stage_b(QUERY_ITEM)

        @pl.when(s == 1)
        def _():
            stage_c(QUERY_ITEM)

        @pl.when(s == 2)
        def _():
            arrivals_partial()

        @pl.when(s == 5)
        def _():
            arrivals_join()

        stage_d(s)
        prefill_head(s)
        head_out(s).start()
        return c

    lax.fori_loop(0, KV_HEADS, turn, 0)

    all_rets().wait_recv()
    ao[g] = ret[g]
    a_out[...] = ao[...]

    def drain_tp(k, c):
        h = (t + k) & (n_tp - 1)
        po_copy(h, k).wait_send()
        ps_copy(h, k).wait_send()
        return c

    def drain_out(h, c):
        head_out(h).wait()
        return c

    all_msgs().wait_send()
    all_rets().wait_send()
    lax.fori_loop(1, n_tp, drain_tp, 0)
    lax.fori_loop(0, ITEMS, drain_item, 0)
    lax.fori_loop(0, KV_HEADS, drain_out, 0)


def to_rows(queries):
    b = queries.shape[0]
    return queries.reshape(b, STEPS, GROUP_SIZE, HEAD_DIM).transpose(0, 2, 1, 3)


def from_rows(rows, b):
    rows = rows.reshape(b, GROUP_SIZE, STEPS, HEAD_DIM).transpose(0, 2, 1, 3)
    return rows.reshape(b, STEPS, GROUP_SIZE * HEAD_DIM)


def local(
    prefill_queries,
    span_keys,
    span_values,
    prefix_keys,
    prefix_values,
    span_offsets,
    prompt_lengths,
    decode_queries,
    decode_new_keys,
    decode_new_values,
    cache_keys,
    cache_values,
    context_lengths,
    placement,
    finished_lengths,
    finished_keys,
    finished_values,
    arrival_queries,
    arrival_new_keys,
    arrival_new_values,
):
    n_groups = lax.axis_size("group")
    n_tp = lax.axis_size("tp")
    n_prompts, local_len, width = finished_keys.shape
    rows = prefill_queries.shape[0]
    dec = decode_queries.shape[0]
    slots = arrival_queries.shape[0]
    dq = to_rows(decode_queries).reshape(dec * ROWS16, HEAD_DIM)
    arrival_rows = to_rows(arrival_queries).reshape(n_groups, CAPACITY, ROWS16, HEAD_DIM)
    lanes = min(128, placement.shape[0])
    any_ = pl.BlockSpec(memory_space=pl.ANY)
    vmem = pl.BlockSpec(memory_space=pltpu.VMEM)
    smem = pl.BlockSpec(memory_space=pltpu.SMEM)
    bf, f32 = jnp.bfloat16, jnp.float32
    a_rows = n_prompts * ROWS16
    dma = pltpu.SemaphoreType.DMA
    p_out, d_out, a_out = pl.pallas_call(
        functools.partial(body, n_groups, n_tp),
        out_shape=(
            jax.ShapeDtypeStruct(prefill_queries.shape, bf),
            jax.ShapeDtypeStruct(dq.shape, bf),
            jax.ShapeDtypeStruct((n_groups, CAPACITY, ROWS16, HEAD_DIM), bf),
        ),
        in_specs=[any_] * 5
        + [smem] * 2
        + [vmem] * 3
        + [any_] * 2
        + [vmem] * 3
        + [any_] * 2
        + [vmem] * 3,
        out_specs=[any_, vmem, vmem],
        scratch_shapes=[
            pltpu.VMEM((ITEMS, 4, X_CHIPS, 2, rows, HEAD_DIM), bf),
            pltpu.VMEM(prefill_queries.shape, bf),
            pltpu.VMEM(cache_keys.shape, bf),
            pltpu.VMEM(cache_values.shape, bf),
            pltpu.VMEM((n_prompts * local_len, width), bf),
            pltpu.VMEM((n_prompts * local_len, width), bf),
            pltpu.VMEM((ITEMS, 2, 2, X_CHIPS, rows, HEAD_DIM), bf),
            pltpu.VMEM((n_groups, CAPACITY, 2 * ROWS16, HEAD_DIM), bf),
            pltpu.VMEM((n_groups, CAPACITY, 2 * ROWS16, HEAD_DIM), bf),
            pltpu.VMEM((n_tp, a_rows, HEAD_DIM), bf),
            pltpu.VMEM((n_tp, a_rows, HEAD_DIM), bf),
            pltpu.VMEM((n_tp, 4 * ROWS16, HEAD_DIM), f32),
            pltpu.VMEM((n_tp, 4 * ROWS16, HEAD_DIM), f32),
            pltpu.VMEM((a_rows, slots * ROWS16), bf),
            pltpu.VMEM((a_rows, HEAD_DIM), f32),
            pltpu.VMEM((n_tp * rows, rows), bf),
            pltpu.VMEM((rows, rows), bf),
            pltpu.VMEM((n_groups, CAPACITY, ROWS16, HEAD_DIM), bf),
            pltpu.VMEM((n_groups, CAPACITY, ROWS16, HEAD_DIM), bf),
            dma((KV_HEADS,)),
            dma((5,)),
            dma((ITEMS, 10)),
            dma((ITEMS, 10)),
            dma(()),
            dma(()),
            dma((n_tp,)),
            dma((n_tp,)),
            dma((n_tp,)),
            dma((n_tp,)),
            dma(()),
            dma(()),
            dma((KV_HEADS,)),
        ],
        compiler_params=pltpu.CompilerParams(
            collective_id=0, has_side_effects=True, vmem_limit_bytes=56 * 1024 * 1024
        ),
    )(
        prefill_queries,
        span_keys,
        span_values,
        prefix_keys,
        prefix_values,
        span_offsets,
        prompt_lengths,
        dq,
        decode_new_keys,
        decode_new_values,
        cache_keys,
        cache_values,
        context_lengths[None, :],
        placement.reshape(-1, lanes),
        finished_lengths.reshape(-1, lanes),
        finished_keys.reshape(n_prompts * local_len, width),
        finished_values.reshape(n_prompts * local_len, width),
        arrival_rows,
        arrival_new_keys,
        arrival_new_values,
    )
    return (p_out, from_rows(d_out, dec), from_rows(a_out, slots))


def solution(mesh):
    both = P(("group", "tp"), None)
    heads = P("group", None, "tp")
    placed = (
        (both,) * 5
        + (P("group"),) * 2
        + (heads,) * 5
        + (P("group"), P(), P())
        + (P("group", "tp", None),) * 2
        + (heads,) * 3
    )
    return jax.shard_map(
        local,
        mesh=mesh,
        in_specs=placed,
        out_specs=(both, heads, heads),
        check_vma=False,
    )
```

```python
import functools
import math

import jax
import jax.numpy as jnp
from jax import lax
from jax.experimental import pallas as pl
from jax.experimental.pallas import tpu as pltpu
from jax.sharding import PartitionSpec as P

KV_HEADS = 8
GROUP_SIZE = 8
HEAD_DIM = 128
CAPACITY = 2
STEPS = 2
ROWS16 = GROUP_SIZE * STEPS
MESH = pl.DeviceIdType.MESH
NEG = -1e30
RATE = math.log2(math.e) / math.sqrt(HEAD_DIM)
X_CHIPS = 4
CORES = 2
STAT_LANES = 16
ITEMS = KV_HEADS + 1
QUERY_ITEM = KV_HEADS


def dot_t(a, b):
    return lax.dot_general(a, b, (((1,), (1,)), ((), ())), preferred_element_type=jnp.float32)


def dot_n(a, b):
    return lax.dot_general(a, b, (((1,), (0,)), ((), ())), preferred_element_type=jnp.float32)


def spread(row, count, reps, base):
    shape = (count * reps, row.shape[1])
    owner = lax.broadcasted_iota(jnp.int32, shape, 0) // reps + base
    lane = lax.broadcasted_iota(jnp.int32, shape, 1)
    return jnp.sum(jnp.where(owner == lane, row, 0.0), axis=1, keepdims=True)


def new_scores(q3, nk):
    shape = q3.shape[:2] + (1,)
    step = lax.broadcasted_iota(jnp.int32, shape, 1) % STEPS
    first = jnp.sum(q3 * nk[0], axis=2, keepdims=True)
    second = jnp.sum(q3 * nk[1], axis=2, keepdims=True)
    return first, jnp.where(step >= 1, second, NEG)


def body(
    n_groups,
    n_tp,
    pq,
    sk,
    sv,
    pk,
    pv,
    span_offset,
    prompt_length,
    dq,
    dnk,
    dnv,
    ck,
    cv,
    context,
    routes,
    lengths,
    fk,
    fv,
    arrival_q,
    ank,
    anv,
    p_out,
    d_out,
    a_out,
    kv,
    q_s,
    ck_s,
    cv_s,
    fk_s,
    fv_s,
    rel,
    msg,
    rm,
    po,
    ro,
    ps,
    rs,
    sel,
    bias,
    key_mask,
    eye,
    ret,
    ao,
    load_kv,
    load_big,
    x_send,
    x_recv,
    m_send,
    m_recv,
    o_send,
    o_recv,
    s_send,
    s_recv,
    b_send,
    b_recv,
):
    g = lax.axis_index("group")
    t = lax.axis_index("tp")
    x, yh = t >> 1, t & 1
    right = ((x + 1) & (X_CHIPS - 1)) * 2 + yh
    left = ((x + X_CHIPS - 1) & (X_CHIPS - 1)) * 2 + yh
    partner = x * 2 + (1 - yh)
    right_x = (x + 1) & (X_CHIPS - 1)
    left_x = (x + X_CHIPS - 1) & (X_CHIPS - 1)
    far_x = (x + 2) & (X_CHIPS - 1)
    yl = (g // CORES) & 1
    beside = g + CORES * (1 - 2 * yl)
    local_len = HEAD_DIM // 4
    n_prompts = fk_s.shape[0] // local_len
    a_rows = n_prompts * ROWS16
    quads = n_prompts // 4
    rows = pq.shape[0]

    arrays = (pk, sk, pv, sv)

    def kv_load(h, a):
        cols = pl.ds(pl.multiple_of(h * HEAD_DIM, HEAD_DIM), HEAD_DIM)
        return pltpu.make_async_copy(arrays[a].at[:, cols], kv.at[h, a, x, yh], load_kv.at[h])

    def start_loads(h, c):
        for a in range(4):
            kv_load(h, a).start()
        return c

    lax.fori_loop(0, KV_HEADS, start_loads, 0)
    big = [
        pltpu.make_async_copy(src, dst, load_big.at[i])
        for i, (src, dst) in enumerate(
            ((ck, ck_s), (cv, cv_s), (pq, q_s), (fk, fk_s), (fv, fv_s))
        )
    ]
    for copy in big:
        copy.start()

    barrier = pltpu.get_barrier_semaphore()

    def greet_group(k, c):
        pl.semaphore_signal(
            barrier, inc=1, device_id={"group": (g + k) & (n_groups - 1)}, device_id_type=MESH
        )
        return c

    def greet_tp(k, c):
        pl.semaphore_signal(barrier, inc=1, device_id={"tp": (t + k) & (n_tp - 1)}, device_id_type=MESH)
        return c

    lax.fori_loop(1, n_groups, greet_group, 0)
    lax.fori_loop(1, n_tp, greet_tp, 0)
    pl.semaphore_signal(
        barrier, inc=1, device_id={"group": beside, "tp": partner}, device_id_type=MESH
    )
    pl.semaphore_wait(barrier, n_groups - 1 + n_tp - 1 + 1)

    to_right, to_left = {"tp": right}, {"tp": left}
    to_same, to_cross = {"group": beside}, {"group": beside, "tp": partner}
    ny = 1 - yh

    def y_first(i):
        return i % 3 != 1

    def hop(src, dst, kind, i, device, sent=0):
        return pltpu.make_async_remote_copy(
            src_ref=src,
            dst_ref=dst,
            send_sem=x_send.at[i, sent],
            recv_sem=x_recv.at[i, kind],
            device_id=device,
            device_id_type=MESH,
        )

    def same(ref, kind, i, device):
        return hop(ref, ref, kind, i, device)

    def arrived(ref, kind, i):
        same(ref, kind, i, to_right).wait_recv()

    def sent(ref, which, i):
        hop(ref, ref, 0, i, to_right, which).wait_send()

    keys, values = pl.ds(0, 2), pl.ds(2, 2)

    def by_kind(i, first, second):
        pl.when(y_first(i))(lambda: first(i))
        pl.when(jnp.logical_not(y_first(i)))(lambda: second(i))

    def stage1(i):
        own = kv.at[i, :, x, yh]

        @pl.when(y_first(i))
        def _():
            hop(kv.at[i, keys, x, yh], rel.at[i, 0, :, 0], 2, i, to_same).start()
            hop(kv.at[i, values, x, yh], rel.at[i, 1, :, 0], 2, i, to_cross).start()

        same(own, 0, i, to_right).start()
        same(own, 1, i, to_left).start()

    def first_a(i):
        arrived(rel.at[i, :, :, 0], 2, i)
        hop(rel.at[i, 0, :, 0], kv.at[i, keys, x, yh], 3, i, to_cross).start()
        hop(rel.at[i, 1, :, 0], kv.at[i, values, x, ny], 3, i, to_same).start()

    def first_b(i):
        block = kv.at[i, :, x, ny]
        arrived(block, 3, i)
        same(block, 0, i, to_right).start()
        same(block, 1, i, to_left).start()

    def first_c(i):
        arrived(kv.at[i, :, left_x], 0, i)
        same(kv.at[i, keys, left_x], 4, i, to_right).start()
        arrived(kv.at[i, :, right_x], 1, i)
        same(kv.at[i, values, right_x], 4, i, to_left).start()

    def first_d(i):
        arrived(kv.at[i, :, far_x], 4, i)

    def second_a(i):
        arrived(kv.at[i, :, left_x, yh], 0, i)
        same(kv.at[i, keys, left_x, yh], 4, i, to_right).start()
        arrived(kv.at[i, :, right_x, yh], 1, i)
        same(kv.at[i, values, right_x, yh], 4, i, to_left).start()

    def second_b(i):
        arrived(kv.at[i, :, far_x, yh], 4, i)
        hop(kv.at[i, keys, :, yh], rel.at[i, 0], 2, i, to_same, 1).start()
        hop(kv.at[i, values, :, yh], rel.at[i, 1], 2, i, to_cross, 1).start()

    def second_c(i):
        arrived(rel.at[i], 2, i)
        hop(rel.at[i, 0], kv.at[i, keys, :, yh], 3, i, to_cross, 1).start()
        hop(rel.at[i, 1], kv.at[i, values, :, ny], 3, i, to_same, 1).start()

    def second_d(i):
        arrived(kv.at[i, :, :, ny], 3, i)

    def stage_a(i):
        by_kind(i, first_a, second_a)

    def stage_b(i):
        by_kind(i, first_b, second_b)

    def stage_c(i):
        by_kind(i, first_c, second_c)

    def stage_d(i):
        by_kind(i, first_d, second_d)

    def first_drain(i):
        sent(kv.at[i], 0, i)

    def second_drain(i):
        sent(kv.at[i, :, pl.ds(0, 3), 0], 0, i)
        sent(kv.at[i], 1, i)

    def drain_item(i, c):
        by_kind(i, first_drain, second_drain)
        return c

    def start_item(i, c):
        block = kv.at[i, :, x, yh]
        pltpu.make_async_copy(block, block, load_kv.at[i]).wait()
        stage1(i)
        return c

    window = 4
    lax.fori_loop(0, window, start_item, 0)

    others = pl.ds(0, n_groups - 1)

    def group_copy(src, dst, send_sem, recv_sem, peer):
        return pltpu.make_async_remote_copy(
            src_ref=src,
            dst_ref=dst,
            send_sem=send_sem,
            recv_sem=recv_sem,
            device_id={"group": peer},
            device_id_type=MESH,
        )

    def all_msgs():
        return group_copy(msg.at[others], rm.at[others], m_send, m_recv, beside)

    def all_rets():
        return group_copy(ret.at[others], ao.at[others], b_send, b_recv, beside)

    def send_msg(k, c):
        peer = (g + k) & (n_groups - 1)
        group_copy(msg.at[peer], rm.at[g], m_send, m_recv, peer).start()
        return c

    def send_ret(k, c):
        peer = (g + k) & (n_groups - 1)
        group_copy(ret.at[peer], ao.at[g], b_send, b_recv, peer).start()
        return c

    pair = (n_groups, CAPACITY, ROWS16, HEAD_DIM)
    row_id = lax.broadcasted_iota(jnp.int32, (1, ROWS16, 1), 1)
    extra = jnp.zeros((n_groups * CAPACITY, ROWS16, HEAD_DIM), jnp.float32)
    for step in range(STEPS):
        nk = ank[...].astype(jnp.float32)[:, step : step + 1]
        nv = anv[...].astype(jnp.float32)[:, step : step + 1]
        extra = jnp.where(row_id == step, nk, jnp.where(row_id == STEPS + step, nv, extra))
    msg[:, :, 0:ROWS16, :] = arrival_q[...]
    msg[:, :, ROWS16 : 2 * ROWS16, :] = extra.astype(jnp.bfloat16).reshape(pair)
    lax.fori_loop(1, n_groups, send_msg, 0)
    rm[g] = msg[g]

    def decode():
        big[0].wait()
        big[1].wait()
        b = dnk.shape[0]
        q = dq[...].reshape(b, ROWS16, HEAD_DIM)
        s = lax.dot_general(
            q, ck_s[...], (((2,), (2,)), ((0,), (0,))), preferred_element_type=jnp.float32
        )
        limit = spread(context[...].astype(jnp.float32), b, ROWS16, 0).reshape(b, ROWS16, 1)
        slot = lax.broadcasted_iota(jnp.int32, s.shape, 2).astype(jnp.float32)
        s = jnp.where(slot < limit, s, NEG)
        nk = dnk[...].astype(jnp.float32)
        nv = dnv[...].astype(jnp.float32)
        n0, n1 = new_scores(q.astype(jnp.float32), (nk[:, 0:1], nk[:, 1:2]))
        m = jnp.maximum(jnp.max(s, axis=2, keepdims=True), jnp.maximum(n0, n1))
        w = jnp.exp2((s - m) * RATE)
        w0 = jnp.exp2((n0 - m) * RATE)
        w1 = jnp.exp2((n1 - m) * RATE)
        total = jnp.sum(w, axis=2, keepdims=True) + w0 + w1
        o = lax.dot_general(
            w.astype(jnp.bfloat16),
            cv_s[...],
            (((2,), (1,)), ((0,), (0,))),
            preferred_element_type=jnp.float32,
        )
        o = o + w0.astype(jnp.bfloat16).astype(jnp.float32) * nv[:, 0:1]
        o = o + w1.astype(jnp.bfloat16).astype(jnp.float32) * nv[:, 1:2]
        d_out[...] = (o / total).reshape(b * ROWS16, HEAD_DIM).astype(jnp.bfloat16)

    def quad_rows(i):
        half = i % 2 * (4 * ROWS16)
        return i // 2, slice(half, half + 4 * ROWS16)

    def queries_of(xs, ys):
        parts = []
        for i in range(quads):
            block, part = quad_rows(i)
            parts.append(kv[QUERY_ITEM, block, xs, ys, part, :])
        return jnp.concatenate(parts, axis=0)

    def arrivals_choose():
        all_msgs().wait_recv()
        lanes = routes.shape[1]
        per_row = lanes // n_prompts
        base = g % per_row * n_prompts
        own = routes[pl.ds(g // per_row, 1), :].astype(jnp.float32)
        dest = spread(own, n_prompts, ROWS16, base)
        owner = lax.broadcasted_iota(jnp.int32, (a_rows, lanes), 0) // ROWS16
        other = lax.broadcasted_iota(jnp.int32, (a_rows, lanes), 1) - base
        rank = jnp.sum(
            jnp.where((dest == own) & (other >= 0) & (other < owner), 1.0, 0.0),
            axis=1,
            keepdims=True,
        )
        within = lax.broadcasted_iota(jnp.int32, (a_rows, 1), 0) % ROWS16
        target = (dest * CAPACITY + rank) * ROWS16 + within.astype(jnp.float32)
        slot_rows = n_groups * CAPACITY * ROWS16
        column = lax.broadcasted_iota(jnp.int32, (a_rows, slot_rows), 1).astype(jnp.float32)
        sel[...] = jnp.where(column == target, 1.0, 0.0).astype(jnp.bfloat16)
        got = rm[:, :, 0:ROWS16, :].reshape(slot_rows, HEAD_DIM)
        chosen = dot_n(sel[...], got).astype(jnp.bfloat16)
        for i in range(quads):
            block, part = quad_rows(i)
            kv[QUERY_ITEM, block, x, yh, part, :] = chosen[i * 4 * ROWS16 : (i + 1) * 4 * ROWS16]
        stage1(QUERY_ITEM)
        own_len = lengths[pl.ds(g // per_row, 1), :].astype(jnp.float32)
        limit = spread(own_len, n_prompts, ROWS16, base) - (t * local_len).astype(jnp.float32)
        col = lax.broadcasted_iota(jnp.int32, (a_rows, HEAD_DIM), 1)
        quad_row = (lax.broadcasted_iota(jnp.int32, (a_rows, HEAD_DIM), 0) // ROWS16) % 4
        keep = (col // local_len == quad_row) & ((col % local_len).astype(jnp.float32) < limit)
        bias[...] = jnp.where(keep, 0.0, NEG)

    def po_copy(h, k):
        return pltpu.make_async_remote_copy(
            src_ref=po.at[h],
            dst_ref=ro.at[t],
            send_sem=o_send.at[k],
            recv_sem=o_recv.at[t],
            device_id={"tp": h},
            device_id_type=MESH,
        )

    def ps_copy(h, k):
        return pltpu.make_async_remote_copy(
            src_ref=ps.at[h],
            dst_ref=rs.at[t],
            send_sem=s_send.at[k],
            recv_sem=s_recv.at[t],
            device_id={"tp": h},
            device_id_type=MESH,
        )

    def po_wait(k):
        peer = (t + k) & (n_tp - 1)
        for send_sem, recv_sem, ref in ((o_send, o_recv, ro), (s_send, s_recv, rs)):
            pltpu.make_async_remote_copy(
                src_ref=ref.at[peer],
                dst_ref=ref.at[peer],
                send_sem=send_sem.at[k],
                recv_sem=recv_sem.at[peer],
                device_id={"tp": peer},
                device_id_type=MESH,
            ).wait_recv()

    def partial_head(h, o_ref, s_ref, at):
        cols = pl.ds(pl.multiple_of(h * HEAD_DIM, HEAD_DIM), HEAD_DIM)
        lane = lax.broadcasted_iota(jnp.int32, (4 * ROWS16, HEAD_DIM), 1)
        stats = jnp.zeros((4 * ROWS16, HEAD_DIM), jnp.float32)
        rows_of = [slice(i * 4 * ROWS16, (i + 1) * 4 * ROWS16) for i in range(quads)]
        keys_of = [slice(i * HEAD_DIM, (i + 1) * HEAD_DIM) for i in range(quads)]
        scores = []
        for i in range(quads):
            block, part = quad_rows(i)
            q = kv[QUERY_ITEM, block, h >> 1, h & 1, part, :]
            scores.append(dot_t(q, fk_s[keys_of[i], cols]))
        scores = [s + bias[r, :] for s, r in zip(scores, rows_of)]
        tops = [jnp.max(s, axis=1, keepdims=True) for s in scores]
        weights = [jnp.exp2((s - m) * RATE) for s, m in zip(scores, tops)]
        totals = [jnp.sum(w, axis=1, keepdims=True) for w in weights]
        outs = [
            dot_n(w.astype(jnp.bfloat16), fv_s[k, cols]) for w, k in zip(weights, keys_of)
        ]
        for i in range(quads):
            o_ref[at, rows_of[i], :] = outs[i].astype(jnp.bfloat16)
            stats = jnp.where(lane == i, tops[i], stats)
            stats = jnp.where(lane == STAT_LANES // 2 + i, totals[i], stats)
        s_ref[at] = stats

    def arrivals_partial():
        stage_d(QUERY_ITEM)
        big[3].wait()
        big[4].wait()

        def one(k, c):
            h = (t + k) & (n_tp - 1)
            partial_head(h, po, ps, h)
            po_copy(h, k).start()
            ps_copy(h, k).start()
            return c

        lax.fori_loop(1, n_tp, one, 0)
        partial_head(t, ro, rs, t)

    def arrivals_join():
        def wait(k, c):
            po_wait(k)
            return c

        lax.fori_loop(1, n_tp, wait, 0)
        slot_rows = n_groups * CAPACITY * ROWS16
        extra = rm[:, :, ROWS16 : 2 * ROWS16, :].reshape(slot_rows, HEAD_DIM)
        new = dot_n(sel[...], extra).reshape(n_prompts, ROWS16, HEAD_DIM)
        q3 = queries_of(x, yh).astype(jnp.float32).reshape(n_prompts, ROWS16, HEAD_DIM)
        n0, n1 = new_scores(q3, (new[:, 0:1], new[:, 1:2]))
        n0 = n0.reshape(a_rows, 1)
        n1 = n1.reshape(a_rows, 1)
        tile = (4 * ROWS16, HEAD_DIM)
        lane = lax.broadcasted_iota(jnp.int32, tile, 1)
        rows_of = [slice(i * 4 * ROWS16, (i + 1) * 4 * ROWS16) for i in range(quads)]
        t0 = jnp.full(tile, NEG, jnp.float32)
        t1 = jnp.full(tile, NEG, jnp.float32)
        for i in range(quads):
            t0 = jnp.where(lane == i, n0[rows_of[i]], t0)
            t1 = jnp.where(lane == i, n1[rows_of[i]], t1)
        live = lane < quads
        stats = [rs[p] for p in range(n_tp)]
        tops = [jnp.where(live, st, NEG) for st in stats]
        m = jnp.maximum(t0, t1)
        for top in tops:
            m = jnp.maximum(m, top)
        w0 = jnp.exp2((t0 - m) * RATE)
        w1 = jnp.exp2((t1 - m) * RATE)
        total = w0 + w1
        weights = [jnp.exp2((top - m) * RATE) for top in tops]
        for w, st in zip(weights, stats):
            total = total + w * pltpu.roll(st, HEAD_DIM - STAT_LANES // 2, 1)
        inverse = 1.0 / jnp.where(live, total, 1.0)
        weights = [w * inverse for w in weights]
        w0 = w0.astype(jnp.bfloat16).astype(jnp.float32) * inverse
        w1 = w1.astype(jnp.bfloat16).astype(jnp.float32) * inverse
        parts = []
        for i in range(quads):
            wide = (4, ROWS16, HEAD_DIM)
            v0 = jnp.broadcast_to(new[4 * i : 4 * i + 4, 2:3], wide).reshape(tile)
            v1 = jnp.broadcast_to(new[4 * i : 4 * i + 4, 3:4], wide).reshape(tile)
            o = w0[:, i : i + 1] * v0 + w1[:, i : i + 1] * v1
            for p in range(n_tp):
                o = o + weights[p][:, i : i + 1] * ro[p, rows_of[i], :].astype(jnp.float32)
            parts.append(o.astype(jnp.bfloat16))
        res = jnp.concatenate(parts, axis=0)
        back = lax.dot_general(
            sel[...], res, (((0,), (0,)), ((), ())), preferred_element_type=jnp.float32
        )
        ret[...] = back.astype(jnp.bfloat16).reshape(n_groups, CAPACITY, ROWS16, HEAD_DIM)

        lax.fori_loop(1, n_groups, send_ret, 0)

    def prefill_masks():
        shape = (n_tp * rows, rows)
        key = lax.broadcasted_iota(jnp.int32, shape, 0)
        row = lax.broadcasted_iota(jnp.int32, shape, 1) + t * rows
        key_mask[...] = jnp.where(key <= row, 0.0, NEG).astype(jnp.bfloat16)
        row = lax.broadcasted_iota(jnp.int32, (rows, rows), 0)
        column = lax.broadcasted_iota(jnp.int32, (rows, rows), 1)
        eye[...] = jnp.where(row == column, 1.0, 0.0).astype(jnp.bfloat16)

    def prefill_head(h):
        vis = span_offset[0] > 0
        part = 2
        n_rows = part * rows
        n_keys = n_tp * rows
        kp = kv[h, 0].reshape(n_keys, HEAD_DIM)
        ks = jnp.concatenate([kv[h, 1].reshape(n_keys, HEAD_DIM), key_mask[...]], axis=1)
        ones = jnp.ones((n_keys, HEAD_DIM), jnp.bfloat16)
        vp = jnp.concatenate([kv[h, 2].reshape(n_keys, HEAD_DIM), ones], axis=1)
        vs = jnp.concatenate([kv[h, 3].reshape(n_keys, HEAD_DIM), ones], axis=1)
        position = lax.broadcasted_iota(jnp.int32, (n_rows, HEAD_DIM), 0) % rows + t * rows
        live = span_offset[0] + position < prompt_length[0]
        eyes = jnp.concatenate([eye[...]] * part, axis=0)

        def cols(i):
            start = h * (GROUP_SIZE * HEAD_DIM) + i * HEAD_DIM
            return pl.ds(pl.multiple_of(start, HEAD_DIM), HEAD_DIM)

        queries = [q_s[:, cols(i)] for i in range(GROUP_SIZE)]
        chains = GROUP_SIZE // part

        def scores_of(j):
            q = jnp.concatenate(queries[j * part : (j + 1) * part], axis=0)
            return dot_t(q, kp), dot_t(jnp.concatenate([q, eyes], axis=1), ks)

        ahead = scores_of(0)
        for j in range(chains):
            sp, ss = ahead
            if j + 1 < chains:
                ahead = scores_of(j + 1)
            mp = jnp.max(sp, axis=1, keepdims=True)
            m = jnp.max(ss, axis=1, keepdims=True)
            m = jnp.where(vis, jnp.maximum(m, mp), m)
            wp = jnp.exp2((sp - jnp.where(vis, m, -NEG)) * RATE)
            ws = jnp.exp2((ss - m) * RATE)
            o = dot_n(wp.astype(jnp.bfloat16), vp) + dot_n(ws.astype(jnp.bfloat16), vs)
            o = o[:, :HEAD_DIM] / o[:, HEAD_DIM:]
            o = jnp.where(live, o, 0.0).astype(jnp.bfloat16)
            for i in range(part):
                p_out[:, cols(j * part + i)] = o[i * rows : (i + 1) * rows]

    prefill_masks()
    decode()
    for h in range(3):
        stage_a(h)
    stage_b(0)
    arrivals_choose()
    stage_b(1)
    stage_c(0)
    stage_a(QUERY_ITEM)
    big[2].wait()

    def turn(s, c):
        @pl.when(s + 1 < KV_HEADS)
        def _():
            stage_c(s + 1)

        @pl.when(s + 2 < KV_HEADS)
        def _():
            stage_b(s + 2)

        @pl.when(s + 3 < KV_HEADS)
        def _():
            stage_a(s + 3)

        @pl.when(s + window < KV_HEADS)
        def _():
            start_item(s + window, 0)

        @pl.when(s == 0)
        def _():
            stage_b(QUERY_ITEM)

        @pl.when(s == 1)
        def _():
            stage_c(QUERY_ITEM)

        @pl.when(s == 2)
        def _():
            arrivals_partial()

        @pl.when(s == 5)
        def _():
            arrivals_join()

        stage_d(s)
        prefill_head(s)
        return c

    lax.fori_loop(0, KV_HEADS, turn, 0)

    all_rets().wait_recv()
    ao[g] = ret[g]
    a_out[...] = ao[...]

    def drain_tp(k, c):
        h = (t + k) & (n_tp - 1)
        po_copy(h, k).wait_send()
        ps_copy(h, k).wait_send()
        return c

    all_msgs().wait_send()
    all_rets().wait_send()
    lax.fori_loop(1, n_tp, drain_tp, 0)
    lax.fori_loop(0, ITEMS, drain_item, 0)


def to_rows(queries):
    b = queries.shape[0]
    return queries.reshape(b, STEPS, GROUP_SIZE, HEAD_DIM).transpose(0, 2, 1, 3)


def from_rows(rows, b):
    rows = rows.reshape(b, GROUP_SIZE, STEPS, HEAD_DIM).transpose(0, 2, 1, 3)
    return rows.reshape(b, STEPS, GROUP_SIZE * HEAD_DIM)


def local(
    prefill_queries,
    span_keys,
    span_values,
    prefix_keys,
    prefix_values,
    span_offsets,
    prompt_lengths,
    decode_queries,
    decode_new_keys,
    decode_new_values,
    cache_keys,
    cache_values,
    context_lengths,
    placement,
    finished_lengths,
    finished_keys,
    finished_values,
    arrival_queries,
    arrival_new_keys,
    arrival_new_values,
):
    n_groups = lax.axis_size("group")
    n_tp = lax.axis_size("tp")
    n_prompts, local_len, width = finished_keys.shape
    rows = prefill_queries.shape[0]
    dec = decode_queries.shape[0]
    slots = arrival_queries.shape[0]
    dq = to_rows(decode_queries).reshape(dec * ROWS16, HEAD_DIM)
    arrival_rows = to_rows(arrival_queries).reshape(n_groups, CAPACITY, ROWS16, HEAD_DIM)
    lanes = min(128, placement.shape[0])
    any_ = pl.BlockSpec(memory_space=pl.ANY)
    vmem = pl.BlockSpec(memory_space=pltpu.VMEM)
    smem = pl.BlockSpec(memory_space=pltpu.SMEM)
    bf, f32 = jnp.bfloat16, jnp.float32
    a_rows = n_prompts * ROWS16
    dma = pltpu.SemaphoreType.DMA
    p_out, d_out, a_out = pl.pallas_call(
        functools.partial(body, n_groups, n_tp),
        out_shape=(
            pltpu.VMEM(prefill_queries.shape, bf),
            pltpu.VMEM(dq.shape, bf),
            pltpu.VMEM((n_groups, CAPACITY, ROWS16, HEAD_DIM), bf),
        ),
        in_specs=[any_] * 5
        + [smem] * 2
        + [vmem] * 3
        + [any_] * 2
        + [vmem] * 3
        + [any_] * 2
        + [vmem] * 3,
        out_specs=[vmem, vmem, vmem],
        scratch_shapes=[
            pltpu.VMEM((ITEMS, 4, X_CHIPS, 2, rows, HEAD_DIM), bf),
            pltpu.VMEM(prefill_queries.shape, bf),
            pltpu.VMEM(cache_keys.shape, bf),
            pltpu.VMEM(cache_values.shape, bf),
            pltpu.VMEM((n_prompts * local_len, width), bf),
            pltpu.VMEM((n_prompts * local_len, width), bf),
            pltpu.VMEM((ITEMS, 2, 2, X_CHIPS, rows, HEAD_DIM), bf),
            pltpu.VMEM((n_groups, CAPACITY, 2 * ROWS16, HEAD_DIM), bf),
            pltpu.VMEM((n_groups, CAPACITY, 2 * ROWS16, HEAD_DIM), bf),
            pltpu.VMEM((n_tp, a_rows, HEAD_DIM), bf),
            pltpu.VMEM((n_tp, a_rows, HEAD_DIM), bf),
            pltpu.VMEM((n_tp, 4 * ROWS16, HEAD_DIM), f32),
            pltpu.VMEM((n_tp, 4 * ROWS16, HEAD_DIM), f32),
            pltpu.VMEM((a_rows, slots * ROWS16), bf),
            pltpu.VMEM((a_rows, HEAD_DIM), f32),
            pltpu.VMEM((n_tp * rows, rows), bf),
            pltpu.VMEM((rows, rows), bf),
            pltpu.VMEM((n_groups, CAPACITY, ROWS16, HEAD_DIM), bf),
            pltpu.VMEM((n_groups, CAPACITY, ROWS16, HEAD_DIM), bf),
            dma((KV_HEADS,)),
            dma((5,)),
            dma((ITEMS, 2)),
            dma((ITEMS, 5)),
            dma(()),
            dma(()),
            dma((n_tp,)),
            dma((n_tp,)),
            dma((n_tp,)),
            dma((n_tp,)),
            dma(()),
            dma(()),
        ],
        compiler_params=pltpu.CompilerParams(
            collective_id=0, has_side_effects=True, vmem_limit_bytes=56 * 1024 * 1024
        ),
    )(
        prefill_queries,
        span_keys,
        span_values,
        prefix_keys,
        prefix_values,
        span_offsets,
        prompt_lengths,
        dq,
        decode_new_keys,
        decode_new_values,
        cache_keys,
        cache_values,
        context_lengths[None, :],
        placement.reshape(-1, lanes),
        finished_lengths.reshape(-1, lanes),
        finished_keys.reshape(n_prompts * local_len, width),
        finished_values.reshape(n_prompts * local_len, width),
        arrival_rows,
        arrival_new_keys,
        arrival_new_values,
    )
    return (p_out, from_rows(d_out, dec), from_rows(a_out, slots))


def solution(mesh):
    both = P(("group", "tp"), None)
    heads = P("group", None, "tp")
    placed = (
        (both,) * 5
        + (P("group"),) * 2
        + (heads,) * 5
        + (P("group"), P(), P())
        + (P("group", "tp", None),) * 2
        + (heads,) * 3
    )
    return jax.shard_map(
        local,
        mesh=mesh,
        in_specs=placed,
        out_specs=(both, heads, heads),
        check_vma=False,
    )
```

```python
import functools
import math

import jax
import jax.numpy as jnp
from jax import lax
from jax.experimental import pallas as pl
from jax.experimental.pallas import tpu as pltpu
from jax.sharding import PartitionSpec as P

KV_HEADS = 8
GROUP_SIZE = 8
HEAD_DIM = 128
CAPACITY = 2
STEPS = 2
ROWS16 = GROUP_SIZE * STEPS
MESH = pl.DeviceIdType.MESH
NEG = -1e30
RATE = math.log2(math.e) / math.sqrt(HEAD_DIM)
X_CHIPS = 4
CORES = 2
STAT_LANES = 16
ITEMS = KV_HEADS + 1
QUERY_ITEM = KV_HEADS


def dot_t(a, b):
    return lax.dot_general(a, b, (((1,), (1,)), ((), ())), preferred_element_type=jnp.float32)


def dot_n(a, b):
    return lax.dot_general(a, b, (((1,), (0,)), ((), ())), preferred_element_type=jnp.float32)


def spread(row, count, reps, base):
    shape = (count * reps, row.shape[1])
    owner = lax.broadcasted_iota(jnp.int32, shape, 0) // reps + base
    lane = lax.broadcasted_iota(jnp.int32, shape, 1)
    return jnp.sum(jnp.where(owner == lane, row, 0.0), axis=1, keepdims=True)


def new_scores(q3, nk):
    shape = q3.shape[:2] + (1,)
    step = lax.broadcasted_iota(jnp.int32, shape, 1) % STEPS
    first = jnp.sum(q3 * nk[0], axis=2, keepdims=True)
    second = jnp.sum(q3 * nk[1], axis=2, keepdims=True)
    return first, jnp.where(step >= 1, second, NEG)


def body(
    n_groups,
    n_tp,
    pq,
    sk,
    sv,
    pk,
    pv,
    span_offset,
    prompt_length,
    dq,
    dnk,
    dnv,
    ck,
    cv,
    context,
    routes,
    lengths,
    fk,
    fv,
    arrival_q,
    ank,
    anv,
    p_out,
    d_out,
    a_out,
    kv,
    q_s,
    ck_s,
    cv_s,
    fk_s,
    fv_s,
    rel,
    msg,
    rm,
    po,
    ro,
    ps,
    rs,
    sel,
    bias,
    key_mask,
    eye,
    ret,
    ao,
    load_kv,
    load_big,
    x_send,
    x_recv,
    m_send,
    m_recv,
    o_send,
    o_recv,
    s_send,
    s_recv,
    b_send,
    b_recv,
):
    g = lax.axis_index("group")
    t = lax.axis_index("tp")
    x, yh = t >> 1, t & 1
    right = ((x + 1) & (X_CHIPS - 1)) * 2 + yh
    left = ((x + X_CHIPS - 1) & (X_CHIPS - 1)) * 2 + yh
    partner = x * 2 + (1 - yh)
    right_x = (x + 1) & (X_CHIPS - 1)
    left_x = (x + X_CHIPS - 1) & (X_CHIPS - 1)
    far_x = (x + 2) & (X_CHIPS - 1)
    yl = (g // CORES) & 1
    beside = g + CORES * (1 - 2 * yl)
    local_len = HEAD_DIM // 4
    n_prompts = fk_s.shape[0] // local_len
    a_rows = n_prompts * ROWS16
    quads = n_prompts // 4
    rows = pq.shape[0]

    arrays = (pk, sk, pv, sv)

    def kv_load(h, a):
        cols = pl.ds(pl.multiple_of(h * HEAD_DIM, HEAD_DIM), HEAD_DIM)
        return pltpu.make_async_copy(arrays[a].at[:, cols], kv.at[h, a, x, yh], load_kv.at[h])

    def start_loads(h, c):
        for a in range(4):
            kv_load(h, a).start()
        return c

    lax.fori_loop(0, KV_HEADS, start_loads, 0)
    big = [
        pltpu.make_async_copy(src, dst, load_big.at[i])
        for i, (src, dst) in enumerate(
            ((ck, ck_s), (cv, cv_s), (pq, q_s), (fk, fk_s), (fv, fv_s))
        )
    ]
    for copy in big:
        copy.start()

    barrier = pltpu.get_barrier_semaphore()

    def greet_group(k, c):
        pl.semaphore_signal(
            barrier, inc=1, device_id={"group": (g + k) & (n_groups - 1)}, device_id_type=MESH
        )
        return c

    def greet_tp(k, c):
        pl.semaphore_signal(barrier, inc=1, device_id={"tp": (t + k) & (n_tp - 1)}, device_id_type=MESH)
        return c

    lax.fori_loop(1, n_groups, greet_group, 0)
    lax.fori_loop(1, n_tp, greet_tp, 0)
    pl.semaphore_signal(
        barrier, inc=1, device_id={"group": beside, "tp": partner}, device_id_type=MESH
    )
    pl.semaphore_wait(barrier, n_groups - 1 + n_tp - 1 + 1)

    to_right, to_left = {"tp": right}, {"tp": left}
    to_same, to_cross = {"group": beside}, {"group": beside, "tp": partner}
    ny = 1 - yh

    def y_first(i):
        return i % 3 != 1

    def hop(src, dst, kind, i, device, sent=0):
        return pltpu.make_async_remote_copy(
            src_ref=src,
            dst_ref=dst,
            send_sem=x_send.at[i, sent],
            recv_sem=x_recv.at[i, kind],
            device_id=device,
            device_id_type=MESH,
        )

    def same(ref, kind, i, device):
        return hop(ref, ref, kind, i, device)

    keys, values = pl.ds(0, 2), pl.ds(2, 2)

    def own_right(i, xs):
        return same(kv.at[i, :, xs, yh], 0, i, to_right)

    def own_left(i, xs):
        return same(kv.at[i, :, xs, yh], 1, i, to_left)

    def one_y(i, part):
        rows_of = keys if part == 0 else values
        device = to_same if part == 0 else to_cross
        return hop(kv.at[i, rows_of, x, yh], rel.at[i, part, :, 0], 2 + part, i, device)

    def all_y(i, part):
        rows_of = keys if part == 0 else values
        device = to_same if part == 0 else to_cross
        return hop(kv.at[i, rows_of, :, yh], rel.at[i, part], 2 + part, i, device, 1)

    def one_relay(i, part):
        if part == 0:
            return hop(rel.at[i, 0, :, 0], kv.at[i, keys, x, yh], 4, i, to_cross)
        return hop(rel.at[i, 1, :, 0], kv.at[i, values, x, ny], 5, i, to_same)

    def all_relay(i, part):
        if part == 0:
            return hop(rel.at[i, 0], kv.at[i, keys, :, yh], 4, i, to_cross, 1)
        return hop(rel.at[i, 1], kv.at[i, values, :, ny], 5, i, to_same, 1)

    def one_landed(i, part):
        return same(kv.at[i, (keys, values)[part], x, ny], 4 + part, i, to_same)

    def all_landed(i, part):
        return same(kv.at[i, (keys, values)[part], :, ny], 4 + part, i, to_same)

    def partner_right(i, xs):
        return same(kv.at[i, :, xs, ny], 6, i, to_right)

    def partner_left(i, xs):
        return same(kv.at[i, :, xs, ny], 7, i, to_left)

    def pair_right(i, xs):
        return same(kv.at[i, keys, xs], 8, i, to_right)

    def pair_left(i, xs):
        return same(kv.at[i, values, xs], 9, i, to_left)

    def single_right(i, xs):
        return same(kv.at[i, keys, xs, yh], 8, i, to_right)

    def single_left(i, xs):
        return same(kv.at[i, values, xs, yh], 9, i, to_left)

    def by_kind(i, first, second):
        pl.when(y_first(i))(lambda: first(i))
        pl.when(jnp.logical_not(y_first(i)))(lambda: second(i))

    def stage1(i):
        @pl.when(y_first(i))
        def _():
            one_y(i, 0).start()
            one_y(i, 1).start()

        own_right(i, x).start()
        own_left(i, x).start()

    def first_a(i):
        for part in range(2):
            one_y(i, part).wait_recv()
            one_relay(i, part).start()

    def first_b(i):
        one_landed(i, 0).wait_recv()
        one_landed(i, 1).wait_recv()
        partner_right(i, x).start()
        partner_left(i, x).start()

    def first_c(i):
        own_right(i, left_x).wait_recv()
        partner_right(i, left_x).wait_recv()
        pair_right(i, left_x).start()
        own_left(i, right_x).wait_recv()
        partner_left(i, right_x).wait_recv()
        pair_left(i, right_x).start()

    def first_d(i):
        pair_right(i, far_x).wait_recv()
        pair_left(i, far_x).wait_recv()

    def second_a(i):
        own_right(i, left_x).wait_recv()
        single_right(i, left_x).start()
        own_left(i, right_x).wait_recv()
        single_left(i, right_x).start()

    def second_b(i):
        single_right(i, far_x).wait_recv()
        single_left(i, far_x).wait_recv()
        all_y(i, 0).start()
        all_y(i, 1).start()

    def second_c(i):
        for part in range(2):
            all_y(i, part).wait_recv()
            all_relay(i, part).start()

    def second_d(i):
        all_landed(i, 0).wait_recv()
        all_landed(i, 1).wait_recv()

    def stage_a(i):
        by_kind(i, first_a, second_a)

    def stage_b(i):
        by_kind(i, first_b, second_b)

    def stage_c(i):
        by_kind(i, first_c, second_c)

    def stage_d(i):
        by_kind(i, first_d, second_d)

    def sent_all(ref, which, i):
        hop(ref, ref, 0, i, to_right, which).wait_send()

    def first_drain(i):
        sent_all(kv.at[i], 0, i)

    def second_drain(i):
        sent_all(kv.at[i, :, pl.ds(0, 3), 0], 0, i)
        sent_all(kv.at[i], 1, i)

    def drain_item(i, c):
        by_kind(i, first_drain, second_drain)
        return c

    def start_item(i, c):
        block = kv.at[i, :, x, yh]
        pltpu.make_async_copy(block, block, load_kv.at[i]).wait()
        stage1(i)
        return c

    window = 4
    lax.fori_loop(0, window, start_item, 0)

    others = pl.ds(0, n_groups - 1)

    def group_copy(src, dst, send_sem, recv_sem, peer):
        return pltpu.make_async_remote_copy(
            src_ref=src,
            dst_ref=dst,
            send_sem=send_sem,
            recv_sem=recv_sem,
            device_id={"group": peer},
            device_id_type=MESH,
        )

    def all_msgs():
        return group_copy(msg.at[others], rm.at[others], m_send, m_recv, beside)

    def all_rets():
        return group_copy(ret.at[others], ao.at[others], b_send, b_recv, beside)

    def send_msg(k, c):
        peer = (g + k) & (n_groups - 1)
        group_copy(msg.at[peer], rm.at[g], m_send, m_recv, peer).start()
        return c

    def send_ret(k, c):
        peer = (g + k) & (n_groups - 1)
        group_copy(ret.at[peer], ao.at[g], b_send, b_recv, peer).start()
        return c

    pair = (n_groups, CAPACITY, ROWS16, HEAD_DIM)
    row_id = lax.broadcasted_iota(jnp.int32, (1, ROWS16, 1), 1)
    extra = jnp.zeros((n_groups * CAPACITY, ROWS16, HEAD_DIM), jnp.float32)
    for step in range(STEPS):
        nk = ank[...].astype(jnp.float32)[:, step : step + 1]
        nv = anv[...].astype(jnp.float32)[:, step : step + 1]
        extra = jnp.where(row_id == step, nk, jnp.where(row_id == STEPS + step, nv, extra))
    msg[:, :, 0:ROWS16, :] = arrival_q[...]
    msg[:, :, ROWS16 : 2 * ROWS16, :] = extra.astype(jnp.bfloat16).reshape(pair)
    lax.fori_loop(1, n_groups, send_msg, 0)
    rm[g] = msg[g]

    def decode():
        big[0].wait()
        big[1].wait()
        b = dnk.shape[0]
        q = dq[...].reshape(b, ROWS16, HEAD_DIM)
        s = lax.dot_general(
            q, ck_s[...], (((2,), (2,)), ((0,), (0,))), preferred_element_type=jnp.float32
        )
        limit = spread(context[...].astype(jnp.float32), b, ROWS16, 0).reshape(b, ROWS16, 1)
        slot = lax.broadcasted_iota(jnp.int32, s.shape, 2).astype(jnp.float32)
        s = jnp.where(slot < limit, s, NEG)
        nk = dnk[...].astype(jnp.float32)
        nv = dnv[...].astype(jnp.float32)
        n0, n1 = new_scores(q.astype(jnp.float32), (nk[:, 0:1], nk[:, 1:2]))
        m = jnp.maximum(jnp.max(s, axis=2, keepdims=True), jnp.maximum(n0, n1))
        w = jnp.exp2((s - m) * RATE)
        w0 = jnp.exp2((n0 - m) * RATE)
        w1 = jnp.exp2((n1 - m) * RATE)
        total = jnp.sum(w, axis=2, keepdims=True) + w0 + w1
        o = lax.dot_general(
            w.astype(jnp.bfloat16),
            cv_s[...],
            (((2,), (1,)), ((0,), (0,))),
            preferred_element_type=jnp.float32,
        )
        o = o + w0.astype(jnp.bfloat16).astype(jnp.float32) * nv[:, 0:1]
        o = o + w1.astype(jnp.bfloat16).astype(jnp.float32) * nv[:, 1:2]
        d_out[...] = (o / total).reshape(b * ROWS16, HEAD_DIM).astype(jnp.bfloat16)

    def quad_rows(i):
        half = i % 2 * (4 * ROWS16)
        return i // 2, slice(half, half + 4 * ROWS16)

    def queries_of(xs, ys):
        parts = []
        for i in range(quads):
            block, part = quad_rows(i)
            parts.append(kv[QUERY_ITEM, block, xs, ys, part, :])
        return jnp.concatenate(parts, axis=0)

    def arrivals_choose():
        all_msgs().wait_recv()
        lanes = routes.shape[1]
        per_row = lanes // n_prompts
        base = g % per_row * n_prompts
        own = routes[pl.ds(g // per_row, 1), :].astype(jnp.float32)
        dest = spread(own, n_prompts, ROWS16, base)
        owner = lax.broadcasted_iota(jnp.int32, (a_rows, lanes), 0) // ROWS16
        other = lax.broadcasted_iota(jnp.int32, (a_rows, lanes), 1) - base
        rank = jnp.sum(
            jnp.where((dest == own) & (other >= 0) & (other < owner), 1.0, 0.0),
            axis=1,
            keepdims=True,
        )
        within = lax.broadcasted_iota(jnp.int32, (a_rows, 1), 0) % ROWS16
        target = (dest * CAPACITY + rank) * ROWS16 + within.astype(jnp.float32)
        slot_rows = n_groups * CAPACITY * ROWS16
        column = lax.broadcasted_iota(jnp.int32, (a_rows, slot_rows), 1).astype(jnp.float32)
        sel[...] = jnp.where(column == target, 1.0, 0.0).astype(jnp.bfloat16)
        got = rm[:, :, 0:ROWS16, :].reshape(slot_rows, HEAD_DIM)
        chosen = dot_n(sel[...], got).astype(jnp.bfloat16)
        for i in range(quads):
            block, part = quad_rows(i)
            kv[QUERY_ITEM, block, x, yh, part, :] = chosen[i * 4 * ROWS16 : (i + 1) * 4 * ROWS16]
        stage1(QUERY_ITEM)
        own_len = lengths[pl.ds(g // per_row, 1), :].astype(jnp.float32)
        limit = spread(own_len, n_prompts, ROWS16, base) - (t * local_len).astype(jnp.float32)
        col = lax.broadcasted_iota(jnp.int32, (a_rows, HEAD_DIM), 1)
        quad_row = (lax.broadcasted_iota(jnp.int32, (a_rows, HEAD_DIM), 0) // ROWS16) % 4
        keep = (col // local_len == quad_row) & ((col % local_len).astype(jnp.float32) < limit)
        bias[...] = jnp.where(keep, 0.0, NEG)

    def po_copy(h, k):
        return pltpu.make_async_remote_copy(
            src_ref=po.at[h],
            dst_ref=ro.at[t],
            send_sem=o_send.at[k],
            recv_sem=o_recv.at[t],
            device_id={"tp": h},
            device_id_type=MESH,
        )

    def ps_copy(h, k):
        return pltpu.make_async_remote_copy(
            src_ref=ps.at[h],
            dst_ref=rs.at[t],
            send_sem=s_send.at[k],
            recv_sem=s_recv.at[t],
            device_id={"tp": h},
            device_id_type=MESH,
        )

    def po_wait(k):
        peer = (t + k) & (n_tp - 1)
        for send_sem, recv_sem, ref in ((o_send, o_recv, ro), (s_send, s_recv, rs)):
            pltpu.make_async_remote_copy(
                src_ref=ref.at[peer],
                dst_ref=ref.at[peer],
                send_sem=send_sem.at[k],
                recv_sem=recv_sem.at[peer],
                device_id={"tp": peer},
                device_id_type=MESH,
            ).wait_recv()

    def partial_head(h, o_ref, s_ref, at):
        cols = pl.ds(pl.multiple_of(h * HEAD_DIM, HEAD_DIM), HEAD_DIM)
        lane = lax.broadcasted_iota(jnp.int32, (4 * ROWS16, HEAD_DIM), 1)
        stats = jnp.zeros((4 * ROWS16, HEAD_DIM), jnp.float32)
        rows_of = [slice(i * 4 * ROWS16, (i + 1) * 4 * ROWS16) for i in range(quads)]
        keys_of = [slice(i * HEAD_DIM, (i + 1) * HEAD_DIM) for i in range(quads)]
        scores = []
        for i in range(quads):
            block, part = quad_rows(i)
            q = kv[QUERY_ITEM, block, h >> 1, h & 1, part, :]
            scores.append(dot_t(q, fk_s[keys_of[i], cols]))
        scores = [s + bias[r, :] for s, r in zip(scores, rows_of)]
        tops = [jnp.max(s, axis=1, keepdims=True) for s in scores]
        weights = [jnp.exp2((s - m) * RATE) for s, m in zip(scores, tops)]
        totals = [jnp.sum(w, axis=1, keepdims=True) for w in weights]
        outs = [
            dot_n(w.astype(jnp.bfloat16), fv_s[k, cols]) for w, k in zip(weights, keys_of)
        ]
        for i in range(quads):
            o_ref[at, rows_of[i], :] = outs[i].astype(jnp.bfloat16)
            stats = jnp.where(lane == i, tops[i], stats)
            stats = jnp.where(lane == STAT_LANES // 2 + i, totals[i], stats)
        s_ref[at] = stats

    def arrivals_partial():
        stage_d(QUERY_ITEM)
        big[3].wait()
        big[4].wait()

        def one(k, c):
            h = (t + k) & (n_tp - 1)
            partial_head(h, po, ps, h)
            po_copy(h, k).start()
            ps_copy(h, k).start()
            return c

        lax.fori_loop(1, n_tp, one, 0)
        partial_head(t, ro, rs, t)

    def arrivals_join():
        def wait(k, c):
            po_wait(k)
            return c

        lax.fori_loop(1, n_tp, wait, 0)
        slot_rows = n_groups * CAPACITY * ROWS16
        extra = rm[:, :, ROWS16 : 2 * ROWS16, :].reshape(slot_rows, HEAD_DIM)
        new = dot_n(sel[...], extra).reshape(n_prompts, ROWS16, HEAD_DIM)
        q3 = queries_of(x, yh).astype(jnp.float32).reshape(n_prompts, ROWS16, HEAD_DIM)
        n0, n1 = new_scores(q3, (new[:, 0:1], new[:, 1:2]))
        n0 = n0.reshape(a_rows, 1)
        n1 = n1.reshape(a_rows, 1)
        tile = (4 * ROWS16, HEAD_DIM)
        lane = lax.broadcasted_iota(jnp.int32, tile, 1)
        rows_of = [slice(i * 4 * ROWS16, (i + 1) * 4 * ROWS16) for i in range(quads)]
        t0 = jnp.full(tile, NEG, jnp.float32)
        t1 = jnp.full(tile, NEG, jnp.float32)
        for i in range(quads):
            t0 = jnp.where(lane == i, n0[rows_of[i]], t0)
            t1 = jnp.where(lane == i, n1[rows_of[i]], t1)
        live = lane < quads
        stats = [rs[p] for p in range(n_tp)]
        tops = [jnp.where(live, st, NEG) for st in stats]
        m = jnp.maximum(t0, t1)
        for top in tops:
            m = jnp.maximum(m, top)
        w0 = jnp.exp2((t0 - m) * RATE)
        w1 = jnp.exp2((t1 - m) * RATE)
        total = w0 + w1
        weights = [jnp.exp2((top - m) * RATE) for top in tops]
        for w, st in zip(weights, stats):
            total = total + w * pltpu.roll(st, HEAD_DIM - STAT_LANES // 2, 1)
        inverse = 1.0 / jnp.where(live, total, 1.0)
        weights = [w * inverse for w in weights]
        w0 = w0.astype(jnp.bfloat16).astype(jnp.float32) * inverse
        w1 = w1.astype(jnp.bfloat16).astype(jnp.float32) * inverse
        parts = []
        for i in range(quads):
            wide = (4, ROWS16, HEAD_DIM)
            v0 = jnp.broadcast_to(new[4 * i : 4 * i + 4, 2:3], wide).reshape(tile)
            v1 = jnp.broadcast_to(new[4 * i : 4 * i + 4, 3:4], wide).reshape(tile)
            o = w0[:, i : i + 1] * v0 + w1[:, i : i + 1] * v1
            for p in range(n_tp):
                o = o + weights[p][:, i : i + 1] * ro[p, rows_of[i], :].astype(jnp.float32)
            parts.append(o.astype(jnp.bfloat16))
        res = jnp.concatenate(parts, axis=0)
        back = lax.dot_general(
            sel[...], res, (((0,), (0,)), ((), ())), preferred_element_type=jnp.float32
        )
        ret[...] = back.astype(jnp.bfloat16).reshape(n_groups, CAPACITY, ROWS16, HEAD_DIM)

        lax.fori_loop(1, n_groups, send_ret, 0)

    def prefill_masks():
        shape = (n_tp * rows, rows)
        key = lax.broadcasted_iota(jnp.int32, shape, 0)
        row = lax.broadcasted_iota(jnp.int32, shape, 1) + t * rows
        key_mask[...] = jnp.where(key <= row, 0.0, NEG).astype(jnp.bfloat16)
        row = lax.broadcasted_iota(jnp.int32, (rows, rows), 0)
        column = lax.broadcasted_iota(jnp.int32, (rows, rows), 1)
        eye[...] = jnp.where(row == column, 1.0, 0.0).astype(jnp.bfloat16)

    def prefill_head(h):
        vis = span_offset[0] > 0
        part = 2
        n_rows = part * rows
        n_keys = n_tp * rows
        kp = kv[h, 0].reshape(n_keys, HEAD_DIM)
        ks = jnp.concatenate([kv[h, 1].reshape(n_keys, HEAD_DIM), key_mask[...]], axis=1)
        ones = jnp.ones((n_keys, HEAD_DIM), jnp.bfloat16)
        vp = jnp.concatenate([kv[h, 2].reshape(n_keys, HEAD_DIM), ones], axis=1)
        vs = jnp.concatenate([kv[h, 3].reshape(n_keys, HEAD_DIM), ones], axis=1)
        position = lax.broadcasted_iota(jnp.int32, (n_rows, HEAD_DIM), 0) % rows + t * rows
        live = span_offset[0] + position < prompt_length[0]
        eyes = jnp.concatenate([eye[...]] * part, axis=0)

        def cols(i):
            start = h * (GROUP_SIZE * HEAD_DIM) + i * HEAD_DIM
            return pl.ds(pl.multiple_of(start, HEAD_DIM), HEAD_DIM)

        queries = [q_s[:, cols(i)] for i in range(GROUP_SIZE)]
        chains = GROUP_SIZE // part

        def scores_of(j):
            q = jnp.concatenate(queries[j * part : (j + 1) * part], axis=0)
            return dot_t(q, kp), dot_t(jnp.concatenate([q, eyes], axis=1), ks)

        ahead = scores_of(0)
        for j in range(chains):
            sp, ss = ahead
            if j + 1 < chains:
                ahead = scores_of(j + 1)
            mp = jnp.max(sp, axis=1, keepdims=True)
            m = jnp.max(ss, axis=1, keepdims=True)
            m = jnp.where(vis, jnp.maximum(m, mp), m)
            wp = jnp.exp2((sp - jnp.where(vis, m, -NEG)) * RATE)
            ws = jnp.exp2((ss - m) * RATE)
            o = dot_n(wp.astype(jnp.bfloat16), vp) + dot_n(ws.astype(jnp.bfloat16), vs)
            o = o[:, :HEAD_DIM] / o[:, HEAD_DIM:]
            o = jnp.where(live, o, 0.0).astype(jnp.bfloat16)
            for i in range(part):
                p_out[:, cols(j * part + i)] = o[i * rows : (i + 1) * rows]

    prefill_masks()
    decode()
    for h in range(3):
        stage_a(h)
    stage_b(0)
    arrivals_choose()
    stage_b(1)
    stage_c(0)
    stage_a(QUERY_ITEM)
    big[2].wait()

    def turn(s, c):
        @pl.when(s + window < KV_HEADS)
        def _():
            start_item(s + window, 0)

        @pl.when(s + 3 < KV_HEADS)
        def _():
            stage_a(s + 3)

        @pl.when(s + 2 < KV_HEADS)
        def _():
            stage_b(s + 2)

        @pl.when(s + 1 < KV_HEADS)
        def _():
            stage_c(s + 1)

        @pl.when(s == 0)
        def _():
            stage_b(QUERY_ITEM)

        @pl.when(s == 1)
        def _():
            stage_c(QUERY_ITEM)

        @pl.when(s == 2)
        def _():
            arrivals_partial()

        @pl.when(s == 5)
        def _():
            arrivals_join()

        stage_d(s)
        prefill_head(s)
        return c

    lax.fori_loop(0, KV_HEADS, turn, 0)

    all_rets().wait_recv()
    ao[g] = ret[g]
    a_out[...] = ao[...]

    def drain_tp(k, c):
        h = (t + k) & (n_tp - 1)
        po_copy(h, k).wait_send()
        ps_copy(h, k).wait_send()
        return c

    all_msgs().wait_send()
    all_rets().wait_send()
    lax.fori_loop(1, n_tp, drain_tp, 0)
    lax.fori_loop(0, ITEMS, drain_item, 0)


def to_rows(queries):
    b = queries.shape[0]
    return queries.reshape(b, STEPS, GROUP_SIZE, HEAD_DIM).transpose(0, 2, 1, 3)


def from_rows(rows, b):
    rows = rows.reshape(b, GROUP_SIZE, STEPS, HEAD_DIM).transpose(0, 2, 1, 3)
    return rows.reshape(b, STEPS, GROUP_SIZE * HEAD_DIM)


def local(
    prefill_queries,
    span_keys,
    span_values,
    prefix_keys,
    prefix_values,
    span_offsets,
    prompt_lengths,
    decode_queries,
    decode_new_keys,
    decode_new_values,
    cache_keys,
    cache_values,
    context_lengths,
    placement,
    finished_lengths,
    finished_keys,
    finished_values,
    arrival_queries,
    arrival_new_keys,
    arrival_new_values,
):
    n_groups = lax.axis_size("group")
    n_tp = lax.axis_size("tp")
    n_prompts, local_len, width = finished_keys.shape
    rows = prefill_queries.shape[0]
    dec = decode_queries.shape[0]
    slots = arrival_queries.shape[0]
    dq = to_rows(decode_queries).reshape(dec * ROWS16, HEAD_DIM)
    arrival_rows = to_rows(arrival_queries).reshape(n_groups, CAPACITY, ROWS16, HEAD_DIM)
    lanes = min(128, placement.shape[0])
    any_ = pl.BlockSpec(memory_space=pl.ANY)
    vmem = pl.BlockSpec(memory_space=pltpu.VMEM)
    smem = pl.BlockSpec(memory_space=pltpu.SMEM)
    bf, f32 = jnp.bfloat16, jnp.float32
    a_rows = n_prompts * ROWS16
    dma = pltpu.SemaphoreType.DMA
    p_out, d_out, a_out = pl.pallas_call(
        functools.partial(body, n_groups, n_tp),
        out_shape=(
            pltpu.VMEM(prefill_queries.shape, bf),
            pltpu.VMEM(dq.shape, bf),
            pltpu.VMEM((n_groups, CAPACITY, ROWS16, HEAD_DIM), bf),
        ),
        in_specs=[any_] * 5
        + [smem] * 2
        + [vmem] * 3
        + [any_] * 2
        + [vmem] * 3
        + [any_] * 2
        + [vmem] * 3,
        out_specs=[vmem, vmem, vmem],
        scratch_shapes=[
            pltpu.VMEM((ITEMS, 4, X_CHIPS, 2, rows, HEAD_DIM), bf),
            pltpu.VMEM(prefill_queries.shape, bf),
            pltpu.VMEM(cache_keys.shape, bf),
            pltpu.VMEM(cache_values.shape, bf),
            pltpu.VMEM((n_prompts * local_len, width), bf),
            pltpu.VMEM((n_prompts * local_len, width), bf),
            pltpu.VMEM((ITEMS, 2, 2, X_CHIPS, rows, HEAD_DIM), bf),
            pltpu.VMEM((n_groups, CAPACITY, 2 * ROWS16, HEAD_DIM), bf),
            pltpu.VMEM((n_groups, CAPACITY, 2 * ROWS16, HEAD_DIM), bf),
            pltpu.VMEM((n_tp, a_rows, HEAD_DIM), bf),
            pltpu.VMEM((n_tp, a_rows, HEAD_DIM), bf),
            pltpu.VMEM((n_tp, 4 * ROWS16, HEAD_DIM), f32),
            pltpu.VMEM((n_tp, 4 * ROWS16, HEAD_DIM), f32),
            pltpu.VMEM((a_rows, slots * ROWS16), bf),
            pltpu.VMEM((a_rows, HEAD_DIM), f32),
            pltpu.VMEM((n_tp * rows, rows), bf),
            pltpu.VMEM((rows, rows), bf),
            pltpu.VMEM((n_groups, CAPACITY, ROWS16, HEAD_DIM), bf),
            pltpu.VMEM((n_groups, CAPACITY, ROWS16, HEAD_DIM), bf),
            dma((KV_HEADS,)),
            dma((5,)),
            dma((ITEMS, 2)),
            dma((ITEMS, 10)),
            dma(()),
            dma(()),
            dma((n_tp,)),
            dma((n_tp,)),
            dma((n_tp,)),
            dma((n_tp,)),
            dma(()),
            dma(()),
        ],
        compiler_params=pltpu.CompilerParams(
            collective_id=0, has_side_effects=True, vmem_limit_bytes=56 * 1024 * 1024
        ),
    )(
        prefill_queries,
        span_keys,
        span_values,
        prefix_keys,
        prefix_values,
        span_offsets,
        prompt_lengths,
        dq,
        decode_new_keys,
        decode_new_values,
        cache_keys,
        cache_values,
        context_lengths[None, :],
        placement.reshape(-1, lanes),
        finished_lengths.reshape(-1, lanes),
        finished_keys.reshape(n_prompts * local_len, width),
        finished_values.reshape(n_prompts * local_len, width),
        arrival_rows,
        arrival_new_keys,
        arrival_new_values,
    )
    return (p_out, from_rows(d_out, dec), from_rows(a_out, slots))


def solution(mesh):
    both = P(("group", "tp"), None)
    heads = P("group", None, "tp")
    placed = (
        (both,) * 5
        + (P("group"),) * 2
        + (heads,) * 5
        + (P("group"), P(), P())
        + (P("group", "tp", None),) * 2
        + (heads,) * 3
    )
    return jax.shard_map(
        local,
        mesh=mesh,
        in_specs=placed,
        out_specs=(both, heads, heads),
        check_vma=False,
    )
```

```python
import functools
import math

import jax
import jax.numpy as jnp
from jax import lax
from jax.experimental import pallas as pl
from jax.experimental.pallas import tpu as pltpu
from jax.sharding import PartitionSpec as P

KV_HEADS = 8
GROUP_SIZE = 8
HEAD_DIM = 128
CAPACITY = 2
STEPS = 2
ROWS16 = GROUP_SIZE * STEPS
MESH = pl.DeviceIdType.MESH
NEG = -1e30
RATE = math.log2(math.e) / math.sqrt(HEAD_DIM)
X_CHIPS = 4
CORES = 2
STAT_LANES = 16
ITEMS = KV_HEADS + 1
QUERY_ITEM = KV_HEADS


def dot_t(a, b):
    return lax.dot_general(a, b, (((1,), (1,)), ((), ())), preferred_element_type=jnp.float32)


def dot_n(a, b):
    return lax.dot_general(a, b, (((1,), (0,)), ((), ())), preferred_element_type=jnp.float32)


def spread(row, count, reps, base):
    shape = (count * reps, row.shape[1])
    owner = lax.broadcasted_iota(jnp.int32, shape, 0) // reps + base
    lane = lax.broadcasted_iota(jnp.int32, shape, 1)
    return jnp.sum(jnp.where(owner == lane, row, 0.0), axis=1, keepdims=True)


def new_scores(q3, nk):
    shape = q3.shape[:2] + (1,)
    step = lax.broadcasted_iota(jnp.int32, shape, 1) % STEPS
    first = jnp.sum(q3 * nk[0], axis=2, keepdims=True)
    second = jnp.sum(q3 * nk[1], axis=2, keepdims=True)
    return first, jnp.where(step >= 1, second, NEG)


def body(
    n_groups,
    n_tp,
    pq,
    sk,
    sv,
    pk,
    pv,
    span_offset,
    prompt_length,
    dq,
    dnk,
    dnv,
    ck,
    cv,
    context,
    routes,
    lengths,
    fk,
    fv,
    arrival_q,
    ank,
    anv,
    p_out,
    d_out,
    a_out,
    kv,
    q_s,
    ck_s,
    cv_s,
    fk_s,
    fv_s,
    rel,
    msg,
    rm,
    po,
    ro,
    ps,
    rs,
    sel,
    bias,
    key_mask,
    eye,
    ret,
    ao,
    load_kv,
    load_big,
    x_send,
    x_recv,
    m_send,
    m_recv,
    o_send,
    o_recv,
    s_send,
    s_recv,
    b_send,
    b_recv,
):
    g = lax.axis_index("group")
    t = lax.axis_index("tp")
    x, yh = t >> 1, t & 1
    right = ((x + 1) & (X_CHIPS - 1)) * 2 + yh
    left = ((x + X_CHIPS - 1) & (X_CHIPS - 1)) * 2 + yh
    partner = x * 2 + (1 - yh)
    right_x = (x + 1) & (X_CHIPS - 1)
    left_x = (x + X_CHIPS - 1) & (X_CHIPS - 1)
    far_x = (x + 2) & (X_CHIPS - 1)
    yl = (g // CORES) & 1
    beside = g + CORES * (1 - 2 * yl)
    local_len = HEAD_DIM // 4
    n_prompts = fk_s.shape[0] // local_len
    a_rows = n_prompts * ROWS16
    quads = n_prompts // 4
    rows = pq.shape[0]

    arrays = (pk, sk, pv, sv)

    def kv_load(h, a):
        cols = pl.ds(pl.multiple_of(h * HEAD_DIM, HEAD_DIM), HEAD_DIM)
        return pltpu.make_async_copy(arrays[a].at[:, cols], kv.at[h, a, x, yh], load_kv.at[h])

    def start_loads(h, c):
        for a in range(4):
            kv_load(h, a).start()
        return c

    lax.fori_loop(0, KV_HEADS, start_loads, 0)
    big = [
        pltpu.make_async_copy(src, dst, load_big.at[i])
        for i, (src, dst) in enumerate(
            ((ck, ck_s), (cv, cv_s), (pq, q_s), (fk, fk_s), (fv, fv_s))
        )
    ]
    for copy in big:
        copy.start()

    barrier = pltpu.get_barrier_semaphore()

    def greet_group(k, c):
        pl.semaphore_signal(
            barrier, inc=1, device_id={"group": (g + k) & (n_groups - 1)}, device_id_type=MESH
        )
        return c

    def greet_tp(k, c):
        pl.semaphore_signal(barrier, inc=1, device_id={"tp": (t + k) & (n_tp - 1)}, device_id_type=MESH)
        return c

    lax.fori_loop(1, n_groups, greet_group, 0)
    lax.fori_loop(1, n_tp, greet_tp, 0)
    pl.semaphore_signal(
        barrier, inc=1, device_id={"group": beside, "tp": partner}, device_id_type=MESH
    )
    pl.semaphore_wait(barrier, n_groups - 1 + n_tp - 1 + 1)

    to_right, to_left = {"tp": right}, {"tp": left}
    to_same, to_cross = {"group": beside}, {"group": beside, "tp": partner}
    ny = 1 - yh

    def y_first(i):
        return i % 3 != 1

    def hop(src, dst, kind, i, device, sent=0):
        return pltpu.make_async_remote_copy(
            src_ref=src,
            dst_ref=dst,
            send_sem=x_send.at[i, sent],
            recv_sem=x_recv.at[i, kind],
            device_id=device,
            device_id_type=MESH,
        )

    def same(ref, kind, i, device):
        return hop(ref, ref, kind, i, device)

    keys, values = pl.ds(0, 2), pl.ds(2, 2)

    def own_right(i, xs):
        return same(kv.at[i, :, xs, yh], 0, i, to_right)

    def own_left(i, xs):
        return same(kv.at[i, :, xs, yh], 1, i, to_left)

    def one_y(i, part):
        rows_of = keys if part == 0 else values
        device = to_same if part == 0 else to_cross
        return hop(kv.at[i, rows_of, x, yh], rel.at[i, part, :, 0], 2 + part, i, device)

    def all_y(i, part):
        rows_of = keys if part == 0 else values
        device = to_same if part == 0 else to_cross
        return hop(kv.at[i, rows_of, :, yh], rel.at[i, part], 2 + part, i, device, 1)

    def one_relay(i, part):
        if part == 0:
            return hop(rel.at[i, 0, :, 0], kv.at[i, keys, x, yh], 4, i, to_cross)
        return hop(rel.at[i, 1, :, 0], kv.at[i, values, x, ny], 5, i, to_same)

    def all_relay(i, part):
        if part == 0:
            return hop(rel.at[i, 0], kv.at[i, keys, :, yh], 4, i, to_cross, 1)
        return hop(rel.at[i, 1], kv.at[i, values, :, ny], 5, i, to_same, 1)

    def one_landed(i, part):
        return same(kv.at[i, (keys, values)[part], x, ny], 4 + part, i, to_same)

    def all_landed(i, part):
        return same(kv.at[i, (keys, values)[part], :, ny], 4 + part, i, to_same)

    def partner_right(i, xs):
        return same(kv.at[i, :, xs, ny], 6, i, to_right)

    def partner_left(i, xs):
        return same(kv.at[i, :, xs, ny], 7, i, to_left)

    def pair_right(i, xs):
        return same(kv.at[i, keys, xs], 8, i, to_right)

    def pair_left(i, xs):
        return same(kv.at[i, values, xs], 9, i, to_left)

    def single_right(i, xs):
        return same(kv.at[i, keys, xs, yh], 8, i, to_right)

    def single_left(i, xs):
        return same(kv.at[i, values, xs, yh], 9, i, to_left)

    def by_kind(i, first, second):
        pl.when(y_first(i))(lambda: first(i))
        pl.when(jnp.logical_not(y_first(i)))(lambda: second(i))

    def stage1(i):
        @pl.when(y_first(i))
        def _():
            one_y(i, 0).start()
            one_y(i, 1).start()

        own_right(i, x).start()
        own_left(i, x).start()

    def first_a(i):
        for part in range(2):
            one_y(i, part).wait_recv()
            one_relay(i, part).start()

    def first_b(i):
        one_landed(i, 0).wait_recv()
        one_landed(i, 1).wait_recv()
        partner_right(i, x).start()
        partner_left(i, x).start()

    def first_c(i):
        own_right(i, left_x).wait_recv()
        partner_right(i, left_x).wait_recv()
        pair_right(i, left_x).start()
        own_left(i, right_x).wait_recv()
        partner_left(i, right_x).wait_recv()
        pair_left(i, right_x).start()

    def first_d(i):
        pair_right(i, far_x).wait_recv()
        pair_left(i, far_x).wait_recv()

    def second_a(i):
        own_right(i, left_x).wait_recv()
        single_right(i, left_x).start()
        own_left(i, right_x).wait_recv()
        single_left(i, right_x).start()

    def second_b(i):
        single_right(i, far_x).wait_recv()
        single_left(i, far_x).wait_recv()
        all_y(i, 0).start()
        all_y(i, 1).start()

    def second_c(i):
        for part in range(2):
            all_y(i, part).wait_recv()
            all_relay(i, part).start()

    def second_d(i):
        all_landed(i, 0).wait_recv()
        all_landed(i, 1).wait_recv()

    def stage_a(i):
        by_kind(i, first_a, second_a)

    def stage_b(i):
        by_kind(i, first_b, second_b)

    def stage_c(i):
        by_kind(i, first_c, second_c)

    def stage_d(i):
        by_kind(i, first_d, second_d)

    def sent_all(ref, which, i):
        hop(ref, ref, 0, i, to_right, which).wait_send()

    def first_drain(i):
        sent_all(kv.at[i], 0, i)

    def second_drain(i):
        sent_all(kv.at[i, :, pl.ds(0, 3), 0], 0, i)
        sent_all(kv.at[i], 1, i)

    def drain_item(i, c):
        by_kind(i, first_drain, second_drain)
        return c

    def start_item(i, c):
        block = kv.at[i, :, x, yh]
        pltpu.make_async_copy(block, block, load_kv.at[i]).wait()
        stage1(i)
        return c

    window = 4
    lax.fori_loop(0, window, start_item, 0)

    others = pl.ds(0, n_groups - 1)

    def group_copy(src, dst, send_sem, recv_sem, peer):
        return pltpu.make_async_remote_copy(
            src_ref=src,
            dst_ref=dst,
            send_sem=send_sem,
            recv_sem=recv_sem,
            device_id={"group": peer},
            device_id_type=MESH,
        )

    def all_msgs():
        return group_copy(msg.at[others], rm.at[others], m_send, m_recv, beside)

    def all_rets():
        return group_copy(ret.at[others], ao.at[others], b_send, b_recv, beside)

    def send_msg(k, c):
        peer = (g + k) & (n_groups - 1)
        group_copy(msg.at[peer], rm.at[g], m_send, m_recv, peer).start()
        return c

    def send_ret(k, c):
        peer = (g + k) & (n_groups - 1)
        group_copy(ret.at[peer], ao.at[g], b_send, b_recv, peer).start()
        return c

    pair = (n_groups, CAPACITY, ROWS16, HEAD_DIM)
    row_id = lax.broadcasted_iota(jnp.int32, (1, ROWS16, 1), 1)
    extra = jnp.zeros((n_groups * CAPACITY, ROWS16, HEAD_DIM), jnp.float32)
    for step in range(STEPS):
        nk = ank[...].astype(jnp.float32)[:, step : step + 1]
        nv = anv[...].astype(jnp.float32)[:, step : step + 1]
        extra = jnp.where(row_id == step, nk, jnp.where(row_id == STEPS + step, nv, extra))
    msg[:, :, 0:ROWS16, :] = arrival_q[...]
    msg[:, :, ROWS16 : 2 * ROWS16, :] = extra.astype(jnp.bfloat16).reshape(pair)
    lax.fori_loop(1, n_groups, send_msg, 0)
    rm[g] = msg[g]

    def decode():
        big[0].wait()
        big[1].wait()
        b = dnk.shape[0]
        q = dq[...].reshape(b, ROWS16, HEAD_DIM)
        s = lax.dot_general(
            q, ck_s[...], (((2,), (2,)), ((0,), (0,))), preferred_element_type=jnp.float32
        )
        limit = spread(context[...].astype(jnp.float32), b, ROWS16, 0).reshape(b, ROWS16, 1)
        slot = lax.broadcasted_iota(jnp.int32, s.shape, 2).astype(jnp.float32)
        s = jnp.where(slot < limit, s, NEG)
        nk = dnk[...].astype(jnp.float32)
        nv = dnv[...].astype(jnp.float32)
        n0, n1 = new_scores(q.astype(jnp.float32), (nk[:, 0:1], nk[:, 1:2]))
        m = jnp.maximum(jnp.max(s, axis=2, keepdims=True), jnp.maximum(n0, n1))
        w = jnp.exp2((s - m) * RATE)
        w0 = jnp.exp2((n0 - m) * RATE)
        w1 = jnp.exp2((n1 - m) * RATE)
        total = jnp.sum(w, axis=2, keepdims=True) + w0 + w1
        o = lax.dot_general(
            w.astype(jnp.bfloat16),
            cv_s[...],
            (((2,), (1,)), ((0,), (0,))),
            preferred_element_type=jnp.float32,
        )
        o = o + w0.astype(jnp.bfloat16).astype(jnp.float32) * nv[:, 0:1]
        o = o + w1.astype(jnp.bfloat16).astype(jnp.float32) * nv[:, 1:2]
        d_out[...] = (o / total).reshape(b * ROWS16, HEAD_DIM).astype(jnp.bfloat16)

    def quad_rows(i):
        half = i % 2 * (4 * ROWS16)
        return i // 2, slice(half, half + 4 * ROWS16)

    def queries_of(xs, ys):
        parts = []
        for i in range(quads):
            block, part = quad_rows(i)
            parts.append(kv[QUERY_ITEM, block, xs, ys, part, :])
        return jnp.concatenate(parts, axis=0)

    def arrivals_choose():
        all_msgs().wait_recv()
        lanes = routes.shape[1]
        per_row = lanes // n_prompts
        base = g % per_row * n_prompts
        own = routes[pl.ds(g // per_row, 1), :].astype(jnp.float32)
        dest = spread(own, n_prompts, ROWS16, base)
        owner = lax.broadcasted_iota(jnp.int32, (a_rows, lanes), 0) // ROWS16
        other = lax.broadcasted_iota(jnp.int32, (a_rows, lanes), 1) - base
        rank = jnp.sum(
            jnp.where((dest == own) & (other >= 0) & (other < owner), 1.0, 0.0),
            axis=1,
            keepdims=True,
        )
        within = lax.broadcasted_iota(jnp.int32, (a_rows, 1), 0) % ROWS16
        target = (dest * CAPACITY + rank) * ROWS16 + within.astype(jnp.float32)
        slot_rows = n_groups * CAPACITY * ROWS16
        column = lax.broadcasted_iota(jnp.int32, (a_rows, slot_rows), 1).astype(jnp.float32)
        sel[...] = jnp.where(column == target, 1.0, 0.0).astype(jnp.bfloat16)
        got = rm[:, :, 0:ROWS16, :].reshape(slot_rows, HEAD_DIM)
        chosen = dot_n(sel[...], got).astype(jnp.bfloat16)
        for i in range(quads):
            block, part = quad_rows(i)
            kv[QUERY_ITEM, block, x, yh, part, :] = chosen[i * 4 * ROWS16 : (i + 1) * 4 * ROWS16]
        stage1(QUERY_ITEM)
        own_len = lengths[pl.ds(g // per_row, 1), :].astype(jnp.float32)
        limit = spread(own_len, n_prompts, ROWS16, base) - (t * local_len).astype(jnp.float32)
        col = lax.broadcasted_iota(jnp.int32, (a_rows, HEAD_DIM), 1)
        quad_row = (lax.broadcasted_iota(jnp.int32, (a_rows, HEAD_DIM), 0) // ROWS16) % 4
        keep = (col // local_len == quad_row) & ((col % local_len).astype(jnp.float32) < limit)
        bias[...] = jnp.where(keep, 0.0, NEG)

    def po_copy(h, k):
        return pltpu.make_async_remote_copy(
            src_ref=po.at[h],
            dst_ref=ro.at[t],
            send_sem=o_send.at[k],
            recv_sem=o_recv.at[t],
            device_id={"tp": h},
            device_id_type=MESH,
        )

    def ps_copy(h, k):
        return pltpu.make_async_remote_copy(
            src_ref=ps.at[h],
            dst_ref=rs.at[t],
            send_sem=s_send.at[k],
            recv_sem=s_recv.at[t],
            device_id={"tp": h},
            device_id_type=MESH,
        )

    def po_wait(k):
        peer = (t + k) & (n_tp - 1)
        for send_sem, recv_sem, ref in ((o_send, o_recv, ro), (s_send, s_recv, rs)):
            pltpu.make_async_remote_copy(
                src_ref=ref.at[peer],
                dst_ref=ref.at[peer],
                send_sem=send_sem.at[k],
                recv_sem=recv_sem.at[peer],
                device_id={"tp": peer},
                device_id_type=MESH,
            ).wait_recv()

    def partial_head(h, o_ref, s_ref, at):
        cols = pl.ds(pl.multiple_of(h * HEAD_DIM, HEAD_DIM), HEAD_DIM)
        lane = lax.broadcasted_iota(jnp.int32, (4 * ROWS16, HEAD_DIM), 1)
        stats = jnp.zeros((4 * ROWS16, HEAD_DIM), jnp.float32)
        rows_of = [slice(i * 4 * ROWS16, (i + 1) * 4 * ROWS16) for i in range(quads)]
        keys_of = [slice(i * HEAD_DIM, (i + 1) * HEAD_DIM) for i in range(quads)]
        scores = []
        for i in range(quads):
            block, part = quad_rows(i)
            q = kv[QUERY_ITEM, block, h >> 1, h & 1, part, :]
            scores.append(dot_t(q, fk_s[keys_of[i], cols]))
        scores = [s + bias[r, :] for s, r in zip(scores, rows_of)]
        tops = [jnp.max(s, axis=1, keepdims=True) for s in scores]
        weights = [jnp.exp2((s - m) * RATE) for s, m in zip(scores, tops)]
        totals = [jnp.sum(w, axis=1, keepdims=True) for w in weights]
        outs = [
            dot_n(w.astype(jnp.bfloat16), fv_s[k, cols]) for w, k in zip(weights, keys_of)
        ]
        for i in range(quads):
            o_ref[at, rows_of[i], :] = outs[i].astype(jnp.bfloat16)
            stats = jnp.where(lane == i, tops[i], stats)
            stats = jnp.where(lane == STAT_LANES // 2 + i, totals[i], stats)
        s_ref[at] = stats

    def arrivals_partial():
        stage_d(QUERY_ITEM)
        big[3].wait()
        big[4].wait()

        def one(k, c):
            h = (t + k) & (n_tp - 1)
            partial_head(h, po, ps, h)
            po_copy(h, k).start()
            ps_copy(h, k).start()
            return c

        lax.fori_loop(1, n_tp, one, 0)
        partial_head(t, ro, rs, t)

    def arrivals_join():
        def wait(k, c):
            po_wait(k)
            return c

        lax.fori_loop(1, n_tp, wait, 0)
        slot_rows = n_groups * CAPACITY * ROWS16
        extra = rm[:, :, ROWS16 : 2 * ROWS16, :].reshape(slot_rows, HEAD_DIM)
        new = dot_n(sel[...], extra).reshape(n_prompts, ROWS16, HEAD_DIM)
        q3 = queries_of(x, yh).astype(jnp.float32).reshape(n_prompts, ROWS16, HEAD_DIM)
        n0, n1 = new_scores(q3, (new[:, 0:1], new[:, 1:2]))
        n0 = n0.reshape(a_rows, 1)
        n1 = n1.reshape(a_rows, 1)
        tile = (4 * ROWS16, HEAD_DIM)
        lane = lax.broadcasted_iota(jnp.int32, tile, 1)
        rows_of = [slice(i * 4 * ROWS16, (i + 1) * 4 * ROWS16) for i in range(quads)]
        t0 = jnp.full(tile, NEG, jnp.float32)
        t1 = jnp.full(tile, NEG, jnp.float32)
        for i in range(quads):
            t0 = jnp.where(lane == i, n0[rows_of[i]], t0)
            t1 = jnp.where(lane == i, n1[rows_of[i]], t1)
        live = lane < quads
        stats = [rs[p] for p in range(n_tp)]
        tops = [jnp.where(live, st, NEG) for st in stats]
        m = jnp.maximum(t0, t1)
        for top in tops:
            m = jnp.maximum(m, top)
        w0 = jnp.exp2((t0 - m) * RATE)
        w1 = jnp.exp2((t1 - m) * RATE)
        total = w0 + w1
        weights = [jnp.exp2((top - m) * RATE) for top in tops]
        for w, st in zip(weights, stats):
            total = total + w * pltpu.roll(st, HEAD_DIM - STAT_LANES // 2, 1)
        inverse = 1.0 / jnp.where(live, total, 1.0)
        weights = [w * inverse for w in weights]
        w0 = w0.astype(jnp.bfloat16).astype(jnp.float32) * inverse
        w1 = w1.astype(jnp.bfloat16).astype(jnp.float32) * inverse
        parts = []
        for i in range(quads):
            wide = (4, ROWS16, HEAD_DIM)
            v0 = jnp.broadcast_to(new[4 * i : 4 * i + 4, 2:3], wide).reshape(tile)
            v1 = jnp.broadcast_to(new[4 * i : 4 * i + 4, 3:4], wide).reshape(tile)
            o = w0[:, i : i + 1] * v0 + w1[:, i : i + 1] * v1
            for p in range(n_tp):
                o = o + weights[p][:, i : i + 1] * ro[p, rows_of[i], :].astype(jnp.float32)
            parts.append(o.astype(jnp.bfloat16))
        res = jnp.concatenate(parts, axis=0)
        back = lax.dot_general(
            sel[...], res, (((0,), (0,)), ((), ())), preferred_element_type=jnp.float32
        )
        ret[...] = back.astype(jnp.bfloat16).reshape(n_groups, CAPACITY, ROWS16, HEAD_DIM)

        lax.fori_loop(1, n_groups, send_ret, 0)

    def prefill_masks():
        shape = (n_tp * rows, rows)
        key = lax.broadcasted_iota(jnp.int32, shape, 0)
        row = lax.broadcasted_iota(jnp.int32, shape, 1) + t * rows
        key_mask[...] = jnp.where(key <= row, 0.0, NEG).astype(jnp.bfloat16)
        row = lax.broadcasted_iota(jnp.int32, (rows, rows), 0)
        column = lax.broadcasted_iota(jnp.int32, (rows, rows), 1)
        eye[...] = jnp.where(row == column, 1.0, 0.0).astype(jnp.bfloat16)

    def prefill_head(h):
        vis = span_offset[0] > 0
        part = 2
        n_rows = part * rows
        n_keys = n_tp * rows
        kp = kv[h, 0].reshape(n_keys, HEAD_DIM)
        ks = jnp.concatenate([kv[h, 1].reshape(n_keys, HEAD_DIM), key_mask[...]], axis=1)
        ones = jnp.ones((n_keys, HEAD_DIM), jnp.bfloat16)
        vp = jnp.concatenate([kv[h, 2].reshape(n_keys, HEAD_DIM), ones], axis=1)
        vs = jnp.concatenate([kv[h, 3].reshape(n_keys, HEAD_DIM), ones], axis=1)
        position = lax.broadcasted_iota(jnp.int32, (n_rows, HEAD_DIM), 0) % rows + t * rows
        live = span_offset[0] + position < prompt_length[0]
        eyes = jnp.concatenate([eye[...]] * part, axis=0)

        def cols(i):
            start = h * (GROUP_SIZE * HEAD_DIM) + i * HEAD_DIM
            return pl.ds(pl.multiple_of(start, HEAD_DIM), HEAD_DIM)

        queries = [q_s[:, cols(i)] for i in range(GROUP_SIZE)]
        chains = GROUP_SIZE // part

        def scores_of(j):
            q = jnp.concatenate(queries[j * part : (j + 1) * part], axis=0)
            return dot_t(q, kp), dot_t(jnp.concatenate([q, eyes], axis=1), ks)

        ahead = scores_of(0)
        for j in range(chains):
            sp, ss = ahead
            if j + 1 < chains:
                ahead = scores_of(j + 1)
            mp = jnp.max(sp, axis=1, keepdims=True)
            m = jnp.max(ss, axis=1, keepdims=True)
            m = jnp.where(vis, jnp.maximum(m, mp), m)
            wp = jnp.exp2((sp - jnp.where(vis, m, -NEG)) * RATE)
            ws = jnp.exp2((ss - m) * RATE)
            o = dot_n(wp.astype(jnp.bfloat16), vp) + dot_n(ws.astype(jnp.bfloat16), vs)
            o = o[:, :HEAD_DIM] / o[:, HEAD_DIM:]
            o = jnp.where(live, o, 0.0).astype(jnp.bfloat16)
            for i in range(part):
                p_out[:, cols(j * part + i)] = o[i * rows : (i + 1) * rows]

    prefill_masks()
    stage_a(0)
    stage_a(2)
    decode()
    stage_b(0)
    stage_a(1)
    arrivals_choose()
    stage_b(1)
    stage_c(0)
    stage_a(QUERY_ITEM)
    big[2].wait()

    def turn(s, c):
        @pl.when(s + window < KV_HEADS)
        def _():
            start_item(s + window, 0)

        @pl.when(s + 3 < KV_HEADS)
        def _():
            stage_a(s + 3)

        @pl.when(s + 2 < KV_HEADS)
        def _():
            stage_b(s + 2)

        @pl.when(s + 1 < KV_HEADS)
        def _():
            stage_c(s + 1)

        @pl.when(s == 0)
        def _():
            stage_b(QUERY_ITEM)

        @pl.when(s == 1)
        def _():
            stage_c(QUERY_ITEM)

        @pl.when(s == 2)
        def _():
            arrivals_partial()

        @pl.when(s == 5)
        def _():
            arrivals_join()

        stage_d(s)
        prefill_head(s)
        return c

    lax.fori_loop(0, KV_HEADS, turn, 0)

    all_rets().wait_recv()
    ao[g] = ret[g]
    a_out[...] = ao[...]

    def drain_tp(k, c):
        h = (t + k) & (n_tp - 1)
        po_copy(h, k).wait_send()
        ps_copy(h, k).wait_send()
        return c

    all_msgs().wait_send()
    all_rets().wait_send()
    lax.fori_loop(1, n_tp, drain_tp, 0)
    lax.fori_loop(0, ITEMS, drain_item, 0)


def to_rows(queries):
    b = queries.shape[0]
    return queries.reshape(b, STEPS, GROUP_SIZE, HEAD_DIM).transpose(0, 2, 1, 3)


def from_rows(rows, b):
    rows = rows.reshape(b, GROUP_SIZE, STEPS, HEAD_DIM).transpose(0, 2, 1, 3)
    return rows.reshape(b, STEPS, GROUP_SIZE * HEAD_DIM)


def local(
    prefill_queries,
    span_keys,
    span_values,
    prefix_keys,
    prefix_values,
    span_offsets,
    prompt_lengths,
    decode_queries,
    decode_new_keys,
    decode_new_values,
    cache_keys,
    cache_values,
    context_lengths,
    placement,
    finished_lengths,
    finished_keys,
    finished_values,
    arrival_queries,
    arrival_new_keys,
    arrival_new_values,
):
    n_groups = lax.axis_size("group")
    n_tp = lax.axis_size("tp")
    n_prompts, local_len, width = finished_keys.shape
    rows = prefill_queries.shape[0]
    dec = decode_queries.shape[0]
    slots = arrival_queries.shape[0]
    dq = to_rows(decode_queries).reshape(dec * ROWS16, HEAD_DIM)
    arrival_rows = to_rows(arrival_queries).reshape(n_groups, CAPACITY, ROWS16, HEAD_DIM)
    lanes = min(128, placement.shape[0])
    any_ = pl.BlockSpec(memory_space=pl.ANY)
    vmem = pl.BlockSpec(memory_space=pltpu.VMEM)
    smem = pl.BlockSpec(memory_space=pltpu.SMEM)
    bf, f32 = jnp.bfloat16, jnp.float32
    a_rows = n_prompts * ROWS16
    dma = pltpu.SemaphoreType.DMA
    p_out, d_out, a_out = pl.pallas_call(
        functools.partial(body, n_groups, n_tp),
        out_shape=(
            pltpu.VMEM(prefill_queries.shape, bf),
            pltpu.VMEM(dq.shape, bf),
            pltpu.VMEM((n_groups, CAPACITY, ROWS16, HEAD_DIM), bf),
        ),
        in_specs=[any_] * 5
        + [smem] * 2
        + [vmem] * 3
        + [any_] * 2
        + [vmem] * 3
        + [any_] * 2
        + [vmem] * 3,
        out_specs=[vmem, vmem, vmem],
        scratch_shapes=[
            pltpu.VMEM((ITEMS, 4, X_CHIPS, 2, rows, HEAD_DIM), bf),
            pltpu.VMEM(prefill_queries.shape, bf),
            pltpu.VMEM(cache_keys.shape, bf),
            pltpu.VMEM(cache_values.shape, bf),
            pltpu.VMEM((n_prompts * local_len, width), bf),
            pltpu.VMEM((n_prompts * local_len, width), bf),
            pltpu.VMEM((ITEMS, 2, 2, X_CHIPS, rows, HEAD_DIM), bf),
            pltpu.VMEM((n_groups, CAPACITY, 2 * ROWS16, HEAD_DIM), bf),
            pltpu.VMEM((n_groups, CAPACITY, 2 * ROWS16, HEAD_DIM), bf),
            pltpu.VMEM((n_tp, a_rows, HEAD_DIM), bf),
            pltpu.VMEM((n_tp, a_rows, HEAD_DIM), bf),
            pltpu.VMEM((n_tp, 4 * ROWS16, HEAD_DIM), f32),
            pltpu.VMEM((n_tp, 4 * ROWS16, HEAD_DIM), f32),
            pltpu.VMEM((a_rows, slots * ROWS16), bf),
            pltpu.VMEM((a_rows, HEAD_DIM), f32),
            pltpu.VMEM((n_tp * rows, rows), bf),
            pltpu.VMEM((rows, rows), bf),
            pltpu.VMEM((n_groups, CAPACITY, ROWS16, HEAD_DIM), bf),
            pltpu.VMEM((n_groups, CAPACITY, ROWS16, HEAD_DIM), bf),
            dma((KV_HEADS,)),
            dma((5,)),
            dma((ITEMS, 2)),
            dma((ITEMS, 10)),
            dma(()),
            dma(()),
            dma((n_tp,)),
            dma((n_tp,)),
            dma((n_tp,)),
            dma((n_tp,)),
            dma(()),
            dma(()),
        ],
        compiler_params=pltpu.CompilerParams(
            collective_id=0, has_side_effects=True, vmem_limit_bytes=56 * 1024 * 1024
        ),
    )(
        prefill_queries,
        span_keys,
        span_values,
        prefix_keys,
        prefix_values,
        span_offsets,
        prompt_lengths,
        dq,
        decode_new_keys,
        decode_new_values,
        cache_keys,
        cache_values,
        context_lengths[None, :],
        placement.reshape(-1, lanes),
        finished_lengths.reshape(-1, lanes),
        finished_keys.reshape(n_prompts * local_len, width),
        finished_values.reshape(n_prompts * local_len, width),
        arrival_rows,
        arrival_new_keys,
        arrival_new_values,
    )
    return (p_out, from_rows(d_out, dec), from_rows(a_out, slots))


def solution(mesh):
    both = P(("group", "tp"), None)
    heads = P("group", None, "tp")
    placed = (
        (both,) * 5
        + (P("group"),) * 2
        + (heads,) * 5
        + (P("group"), P(), P())
        + (P("group", "tp", None),) * 2
        + (heads,) * 3
    )
    return jax.shard_map(
        local,
        mesh=mesh,
        in_specs=placed,
        out_specs=(both, heads, heads),
        check_vma=False,
    )
```
